32 devices in a mesh: row: 4 (over x, core), col: 8 (over z, y).
Axes of the slice: x: 2, y: 2, z: 4, core: 2. Of those that a mesh axis runs over, the one named last changes fastest.
Arguments:
- factor: float32 [6, 4, 8, 512, 512], P(None, 'row', 'col'), may hold values from -0.1875 to 0.1875
- rhs: float32 [6, 4, 8, 128, 128], P(None, 'row', 'col'), may hold values from -6 to 6
- inverses: float32 [4, 512, 512], replicated, may hold values from -0.5 to 2, as said below
Outputs:
- solved: float32 [4, 512, 128], P(None, 'col')
- remaining: float32 [6, 4, 8, 128, 128], P(None, 'row', 'col')
The draws below stay inside these ranges and needn't reach their ends.
Inputs may be any that keep to these rules, and one draw needn't show every extreme that they name: `inverses`: each block is lower triangular with its diagonal between 0.5 and 2 and entries below it of magnitude at most 4 / sqrt(512).
All inputs are finite; a program needn't handle non-finite values.
Results may differ from the reference program's by a relative error of at most 0.00011.
Values sent between devices are 32-bit elements; how exact they have to be, the bound alone decides.
No kernel may reach another device: no remote copies, remote signals or barrier semaphores. Data moves between devices by JAX's collectives and lax.ppermute only.
A program may use at most 64 MiB of HBM per device.

```python
import jax
import jax.numpy as jnp
from jax import lax

NB = 512
NRHS = 128
KSTEPS = 4
RB = 6
N_ROW = 4
N_COL = 8


def draw_inverses(key, part):
    first, second = jax.random.split(key)
    lower = jnp.clip(jax.random.normal(first, (KSTEPS, NB, NB), jnp.float32), -4.0, 4.0)
    diagonal = jax.random.uniform(second, (KSTEPS, NB), jnp.float32, 0.5, 2.0)
    row_pos = jnp.arange(NB)[:, None]
    col_pos = jnp.arange(NB)[None, :]
    below = (col_pos < row_pos).astype(jnp.float32)
    unit = (col_pos == row_pos).astype(jnp.float32)
    return lower * below * NB ** (-0.5) + unit * diagonal[:, :, None]


def block_levels(key, dims, cuts, least, largest):
    def one(dim, shards_of):
        draws = jax.random.uniform(jax.random.fold_in(jax.random.fold_in(key, 6), dim), (shards_of,), jnp.float32, least / len(cuts), largest / len(cuts))
        return jnp.repeat(jnp.exp(draws), dims[dim] // shards_of).reshape((-1,) + (1,) * (len(dims) - dim - 1))

    level = one(*cuts[0])
    for cut in cuts[1:]:
        level = level * one(*cut)
    return level


def centred(stream_key, extent, deviation, bound, shards=(), kind=jnp.bfloat16):
    result = deviation * jax.random.normal(stream_key, extent, jnp.float32)
    if shards:
        result = result * block_levels(stream_key, extent, shards, -0.22, 0.18)
    return jnp.clip(result, -bound, bound).astype(kind)


def setup_inputs(seed: int = 0) -> dict:
    streams_of = jax.random.split(jax.random.key(seed), 4)
    return {
        "factor": centred(streams_of[0], (RB, N_ROW, N_COL, NB, NB), (2 * NB) ** -0.5, 0.1875, ((1, 4), (2, 8)), jnp.float32),
        "rhs": centred(streams_of[1], (RB, N_ROW, N_COL, NB // KSTEPS, NRHS), 1.0, 6.0, ((1, 4), (2, 8)), jnp.float32),
        "inverses": draw_inverses(jax.random.fold_in(streams_of[3], 71), 0),
    }


def reference(factor, rhs, inverses):
    groups = N_COL // KSTEPS
    quarter = NB // KSTEPS
    block_ids = (jnp.arange(RB, dtype=jnp.int32)[:, None, None] * N_ROW + jnp.arange(N_ROW, dtype=jnp.int32)[None, :, None]) * groups + (jnp.arange(N_COL, dtype=jnp.int32) % groups)[None, None, :]
    current = rhs
    solved_list = []
    for k in range(KSTEPS):
        owner_row = k // groups
        owner_group = k % groups
        residual_block = current[0, owner_row, owner_group::groups].reshape(NB, NRHS)
        solved_block = jnp.dot(inverses[k], residual_block, precision=lax.Precision.HIGHEST)
        solved_list.append(solved_block)
        column_blocks = factor[:, :, k * groups:(k + 1) * groups]
        update = jnp.einsum("abgji,jh->abgih", column_blocks, solved_block, precision=lax.Precision.HIGHEST)
        update = update.reshape(RB, N_ROW, groups, KSTEPS, quarter, NRHS).transpose(0, 1, 3, 2, 4, 5).reshape(RB, N_ROW, N_COL, quarter, NRHS)
        keep = (block_ids > k).astype(jnp.float32)[:, :, :, None, None]
        current = current - update * keep
    return jnp.stack(solved_list), current
```

```python
import jax
import jax.numpy as jnp
from jax import lax
from jax.sharding import PartitionSpec as P

HIGH = lax.Precision.HIGH
AXES = ("row", "col")


def times(block, x):
    return lax.dot_general(block, x, (((0,), (0,)), ((), ())), precision=HIGH)


def on_device(factor, rhs, inverses):
    steps = inverses.shape[0]
    blocks = factor.shape[0]
    width = factor.shape[3]
    quarter = rhs.shape[3]
    nrhs = rhs.shape[4]
    row_count = lax.axis_size("row")
    col_count = lax.axis_size("col")
    groups = col_count // steps
    row_pos = lax.axis_index("row")
    col_pos = lax.axis_index("col")
    member = col_pos // groups
    group = col_pos % groups
    share = width // col_count

    def dev(row, mem, grp):
        return row * col_count + mem * groups + grp

    def line(g, mem):
        return dev(g // groups, mem, g % groups)

    def home(k):
        return line(k, k)

    def send(x, pairs):
        return lax.ppermute(x, AXES, pairs)

    def spread(x, planes):
        todo = {}
        have = {}
        for k in planes:
            row, grp = k // groups, k % groups
            twin = row ^ 1
            have[k] = [(row, grp)]
            rows = [r for r in range(row_count) if r % 2 == row % 2]
            todo[k] = [(r, g) for r in rows for g in range(groups) if (r, g) != (row, grp)]
        while any(todo.values()):
            rounds = [[] for _ in range(3)]
            for k in planes:
                fresh = []
                for src in have[k]:
                    for slot in range(3):
                        if todo[k]:
                            dst = todo[k].pop(0)
                            fresh.append(dst)
                            rounds[slot].append((dev(src[0], k, src[1]), dev(dst[0], k, dst[1])))
                have[k] += fresh
            got = x
            for pairs in rounds:
                if pairs:
                    me = row_pos * col_count + col_pos
                    here = jnp.zeros((), bool)
                    for _, d in pairs:
                        here = here | (me == d)
                    got = jnp.where(here, send(x, pairs), got)
            x = got
        pairs = [(dev(r, k, g), dev(r ^ 1, k, g)) for k in planes for r, g in have[k]]
        other = send(x, pairs)
        me = row_pos * col_count + col_pos
        here = jnp.zeros((), bool)
        for _, d in pairs:
            here = here | (me == d)
        return jnp.where(here, other, x)

    panel = factor[:, 0, 0]
    mine = rhs[0, 0, 0]
    low = member < 2

    lx = send(panel[0], [(line(2, 0), home(0)), (line(2, 1), home(1))])
    ly = send(panel[0], [(line(3, 0), home(0)), (line(3, 1), home(1))])
    la = send(panel[0], [(line(1, 0), home(1)), (line(3, 2), home(3))])

    whole = jnp.zeros((steps, quarter, nrhs), jnp.float32)
    whole = lax.dynamic_update_index_in_dim(whole, mine, member, 0)
    needs = {0: (0, 1), 1: (1,), 2: (2, 3), 3: (3,)}
    for offset in range(1, steps):
        pairs = [
            (line(g, (m - offset) % steps), line(g, m)) for g in needs for m in needs[g]
        ]
        piece = send(mine, pairs)
        whole = lax.dynamic_update_index_in_dim(whole, piece, (member - offset) % steps, 0)
    own = whole.reshape(width, nrhs)
    lent = send(own, [(line(0, 1), home(1)), (line(2, 3), home(3))])
    first = jnp.where(member % 2 == 1, lent, own)

    s_a = jnp.dot(inverses[0], first, precision=HIGH)
    s_b = jnp.dot(inverses[1], own - times(la, s_a), precision=HIGH)
    s_low = jnp.where(member == 0, s_a, s_b)
    w = jnp.stack([times(lx, s_low), times(ly, s_low)])
    w_a = send(w, [(home(0), home(3)), (home(1), home(2))])
    w_b = send(w, [(home(1), home(3)), (home(0), home(2))])

    w_sum = w_a + w_b
    s_c = jnp.dot(inverses[2], first - w_sum[0], precision=HIGH)
    s_d = jnp.dot(inverses[3], own - w_sum[1] - times(la, s_c), precision=HIGH)
    s_high = jnp.where(member == 2, s_c, s_d)

    block_ids = (jnp.arange(blocks, dtype=jnp.int32) * row_count + row_pos) * groups + group
    keep = (block_ids > member).astype(jnp.float32)[:, None, None]

    def update(s):
        full = jnp.einsum("rji,jh->rih", panel, s, precision=HIGH) * keep
        return full.reshape(blocks, steps, quarter, nrhs)

    def part_of(s, full, to):
        piece = lax.dynamic_index_in_dim(full, to, 1, keepdims=False)
        rows = lax.dynamic_slice_in_dim(s, (to * groups + group) * share, share, 0)
        return jnp.concatenate([piece.reshape(blocks * quarter, nrhs), rows])

    def exchange(s, full, sources):
        out = []
        for offset in range(1, steps):
            part = part_of(s, full, (member + offset) % steps)
            pairs = [
                (dev(r, m, g), dev(r, (m + offset) % steps, g))
                for m in sources for r in range(row_count) for g in range(groups)
            ]
            out.append(send(part, pairs))
        return out

    s_low = spread(s_low, (0, 1))
    full_low = update(s_low)
    got_low = exchange(s_low, full_low, (0, 1))
    s_high = spread(s_high, (2, 3))
    full_high = update(s_high)
    got_high = exchange(s_high, full_high, (2, 3))

    here = jnp.where(low, part_of(s_low, full_low, member), part_of(s_high, full_high, member))
    total = here[: blocks * quarter]
    solved = jnp.zeros((steps, share, nrhs), jnp.float32)
    solved = lax.dynamic_update_index_in_dim(solved, here[blocks * quarter:], member, 0)
    for offset in range(1, steps):
        source = (member - offset) % steps
        got = jnp.where(source < 2, got_low[offset - 1], got_high[offset - 1])
        total = total + got[: blocks * quarter]
        solved = lax.dynamic_update_index_in_dim(solved, got[blocks * quarter:], source, 0)
    remaining = rhs[:, 0, 0] - total.reshape(blocks, quarter, nrhs)
    return solved, remaining[:, None, None]


def solution(mesh):
    in_specs = (P(None, "row", "col", None, None), P(None, "row", "col", None, None), P())
    out_specs = (P(None, "col", None), P(None, "row", "col", None, None))
    return jax.shard_map(
        on_device, mesh=mesh, in_specs=in_specs, out_specs=out_specs, check_vma=False
    )
```

```python
import functools

import jax
import jax.numpy as jnp
from jax import lax
from jax.experimental import pallas as pl
from jax.experimental.pallas import tpu as pltpu
from jax.sharding import PartitionSpec as P

AXES = ("row", "col")
F32 = jnp.float32
VMEM = pltpu.VMEM
PARAMS = pltpu.CompilerParams(vmem_limit_bytes=40 * 2**20)
CHEAP = pl.CostEstimate(flops=1000, bytes_accessed=1000, transcendentals=0)


def split(x):
    high = x.astype(jnp.bfloat16)
    return high, (x - high.astype(F32)).astype(jnp.bfloat16)


def product(a, b, transposed=False):
    dims = (((1,), (1 if transposed else 0,)), ((), ()))
    a_high, a_low = split(a)
    b_high, b_low = split(b)
    n = a.shape[0]
    both = lax.dot_general(
        jnp.concatenate([a_high, a_low], 0), b_high, dims, preferred_element_type=F32
    )
    cross = lax.dot_general(a_high, b_low, dims, preferred_element_type=F32)
    return both[:n] + (both[n:] + cross)


def position(col_count):
    return lax.axis_index("row") * col_count + lax.axis_index("col")


def stacked(pieces, which):
    return jnp.concatenate([p[which].T for p in pieces], axis=1)


def low_kernel(homes, col_count, own, g1, g2, g3, near, la, lx, ly, inv, w, s_a, s_b):
    me = position(col_count)

    def work(block):
        pieces = (own, g1, g2, g3)
        first = product(stacked(pieces, 0), inv[0], True)
        s_a[...] = first
        second = product(stacked(pieces, 1) - product(first, block[...]), inv[1], True)
        s_b[...] = second
        w[...] = product(first, lx[...]) + product(second, ly[...])

    @pl.when(me == homes[0])
    def _():
        work(la)

    @pl.when(me == homes[1])
    def _():
        work(near)


def high_kernel(homes, col_count, own, g1, g2, g3, l_even, l_odd, w_1, w_2, inv, after, s_a, s_b):
    del after
    me = position(col_count)

    def work(block, w_even, w_odd):
        pieces = (g3, g2, g1, own)
        first = product(stacked(pieces, 0) - w_even[...], inv[0], True)
        s_a[...] = first
        s_b[...] = product(
            stacked(pieces, 1) - w_odd[...] - product(first, block[...]), inv[1], True
        )

    @pl.when(me == homes[0])
    def _():
        work(l_even, w_1, w_2)

    @pl.when(me == homes[1])
    def _():
        work(l_odd, w_2, w_1)


def update_kernel(cfg, s_twin, s_mine, panel, *rest):
    steps, groups, row_count, share, parity, members = cfg
    outs, full = rest[:steps], rest[steps]
    quarter = full.shape[1] // steps
    step = pl.program_id(0)
    row = lax.axis_index("row")
    col = lax.axis_index("col")
    member = col // groups
    group = col % groups
    block_id = (step * row_count + row) * groups + group
    keep = (block_id > member).astype(F32)

    def work(s):
        full[...] = product(s[...], panel[...]) * keep
        for offset in range(steps):
            to = lax.rem(member + offset, steps)
            columns = pl.ds(pl.multiple_of(to * quarter, quarter), quarter)
            rows = pl.ds(pl.multiple_of(step * quarter, quarter), quarter)
            outs[offset][rows, :] = full[:, columns]

        @pl.when(step == pl.num_programs(0) - 1)
        def _():
            for offset in range(steps):
                to = lax.rem(member + offset, steps)
                columns = pl.ds(pl.multiple_of(to * quarter, quarter), quarter)
                full[:, :quarter] = s[:, columns].T
                rows = pl.ds(pl.multiple_of(group * share, share), share)
                last = outs[offset].shape[0] - share
                outs[offset][last:, :] = full[rows, :quarter]

    here = functools.reduce(jnp.logical_or, [member == m for m in members])

    @pl.when(here & (lax.rem(row, 2) == parity))
    def _():
        work(s_mine)

    @pl.when(here & (lax.rem(row, 2) != parity))
    def _():
        work(s_twin)


def last_kernel(steps, groups, rhs, *refs):
    sources, (solved, out) = refs[: 2 * steps], refs[2 * steps:]
    lows, highs = sources[:steps], sources[steps:]
    blocks, quarter = rhs.shape[0], rhs.shape[1]
    member = lax.axis_index("col") // groups

    def finish(own):
        for r in range(blocks):
            rows = pl.ds(r * quarter, quarter)
            total = own[rows, :]
            for part in lows[1:] + highs[1:]:
                total = total + part[rows, :]
            out[r] = rhs[r] - total.T
        last = blocks * quarter
        solved[member] = own[last:, :]
        for offset in range(1, steps):
            solved[lax.rem(member + steps - offset, steps)] = (
                lows[offset][last:, :] + highs[offset][last:, :]
            )

    @pl.when(member < steps // 2)
    def _():
        finish(lows[0])

    @pl.when(member >= steps // 2)
    def _():
        finish(highs[0])


def on_device(factor, rhs, inverses):
    steps = inverses.shape[0]
    blocks = factor.shape[0]
    width = factor.shape[3]
    quarter = rhs.shape[3]
    nrhs = rhs.shape[4]
    row_count = lax.axis_size("row")
    col_count = lax.axis_size("col")
    groups = col_count // steps
    row_pos = lax.axis_index("row")
    col_pos = lax.axis_index("col")
    member = col_pos // groups
    group = col_pos % groups
    share = width // col_count
    top = steps - 1
    me = row_pos * col_count + col_pos

    def dev(row, mem, grp):
        return row * col_count + mem * groups + grp

    def line(g, mem):
        return dev(g // groups, mem, g % groups)

    low_homes = (line(0, 0), line(1, 0))
    high_homes = (line(2, top), line(3, top))

    def send(x, pairs):
        return lax.ppermute(x, AXES, pairs)

    def chosen(pairs, new, old):
        here = functools.reduce(jnp.logical_or, [me == d for _, d in pairs])
        return jnp.where(here, new, old)

    vmem = pl.BlockSpec(memory_space=VMEM)
    two_inverses = [pl.BlockSpec((2, width, width), lambda i, h=h: (h, 0, 0)) for h in (0, 1)]

    mine = rhs[0, 0, 0]
    other = send(mine, [(line(g ^ 1, m), line(g, m)) for g in range(4) for m in range(steps)])
    even = group % 2 == 0
    both = jnp.stack([jnp.where(even, mine, other), jnp.where(even, other, mine)])
    near = factor[0, 0, 0]
    ly = send(near, [(line(2, 1), low_homes[0]), (line(3, 1), low_homes[1]), (line(3, 2), high_homes[0])])
    la = send(near, [(line(1, 0), low_homes[0]), (line(3, 2), high_homes[1])])
    lx = send(near, [(line(2, 0), low_homes[0]), (line(3, 0), low_homes[1])])
    gathered = [
        send(both, [(line(g, j), line(g, 0)) for g in (0, 1)] + [(line(g, top - j), line(g, top)) for g in (2, 3)])
        for j in range(1, steps)
    ]

    vector = jax.ShapeDtypeStruct((nrhs, width), F32)
    full_piece = pl.BlockSpec((2, quarter, nrhs), lambda i: (0, 0, 0))
    square = pl.BlockSpec((width, width), lambda i: (0, 0))
    vec = pl.BlockSpec((nrhs, width), lambda i: (0, 0))
    w, s_0, s_1 = pl.pallas_call(
        functools.partial(low_kernel, low_homes, col_count),
        grid=(1,),
        in_specs=[full_piece] * 4 + [square] * 4 + [two_inverses[0]],
        out_specs=[vec] * 3,
        out_shape=[vector] * 3,
        compiler_params=PARAMS,
        cost_estimate=CHEAP,
        name="solve_low",
    )(both, *gathered, near, la, lx, ly, inverses)
    w_1 = send(w, [(low_homes[0], high_homes[0]), (low_homes[1], high_homes[1])])
    w_2 = send(w, [(low_homes[0], high_homes[1]), (low_homes[1], high_homes[0])])

    def spread(outer, inner, at, away, lines):
        moved = send(inner, [(line(g, at), line(g, away)) for g in lines])
        s = jnp.where(member == at, outer, moved)
        core = (lines[0] // groups) % 2
        have = [(g // groups, g % groups) for g in lines]
        todo = [
            (r, g) for r in range(row_count) for g in range(groups)
            if r % 2 == core and (r, g) not in have
        ]
        while todo:
            new, todo = todo[: len(have)], todo[len(have):]
            pairs = [
                (dev(a[0], m, a[1]), dev(b[0], m, b[1]))
                for m in (at, away) for a, b in zip(have, new)
            ]
            s = chosen(pairs, send(s, pairs), s)
            have = have + new
        pairs = [(dev(r, m, g), dev(r ^ 1, m, g)) for m in (at, away) for r, g in have]
        return send(s, pairs), s, core

    def update(twin, s, core, members):
        part = jax.ShapeDtypeStruct((blocks * quarter + share, nrhs), F32)
        cfg = (steps, groups, row_count, share, core, members)
        parts = pl.pallas_call(
            functools.partial(update_kernel, cfg),
            grid=(blocks,),
            in_specs=[vec, vec, pl.BlockSpec((None, None, None, width, width), lambda i: (i, 0, 0, 0, 0))],
            out_specs=[pl.BlockSpec(part.shape, lambda i: (0, 0))] * steps,
            out_shape=[part] * steps,
            scratch_shapes=[VMEM((nrhs, width), F32)],
            compiler_params=PARAMS,
            cost_estimate=CHEAP,
            name="update",
        )(twin, s, factor)
        got = [parts[0]]
        for offset in range(1, steps):
            pairs = [
                (dev(r, m, g), dev(r, (m + offset) % steps, g))
                for m in members for r in range(row_count) for g in range(groups)
            ]
            got.append(send(parts[offset], pairs))
        return got

    lows = update(*spread(s_0, s_1, 0, 1, (0, 1)), (0, 1))
    s_2, s_3 = pl.pallas_call(
        functools.partial(high_kernel, high_homes, col_count),
        grid=(1,),
        in_specs=[full_piece] * 4 + [square] * 2 + [vec] * 2 + [two_inverses[1], pl.BlockSpec(memory_space=pl.ANY)],
        out_specs=[vec] * 2,
        out_shape=[vector] * 2,
        compiler_params=PARAMS,
        cost_estimate=CHEAP,
        name="solve_high",
    )(both, *gathered, ly, la, w_1, w_2, inverses, lows[0])
    highs = update(*spread(s_3, s_2, top, top - 1, (2, 3)), (top - 1, top))

    solved, remaining = pl.pallas_call(
        functools.partial(last_kernel, steps, groups),
        in_specs=[vmem] * (1 + 2 * steps),
        out_specs=[vmem] * 2,
        out_shape=[
            jax.ShapeDtypeStruct((steps, share, nrhs), F32),
            jax.ShapeDtypeStruct((blocks, quarter, nrhs), F32),
        ],
        compiler_params=PARAMS,
        cost_estimate=CHEAP,
        name="add_up",
    )(rhs[:, 0, 0], *lows, *highs)
    return solved, remaining[:, None, None]


def solution(mesh):
    in_specs = (P(None, "row", "col", None, None), P(None, "row", "col", None, None), P())
    out_specs = (P(None, "col", None), P(None, "row", "col", None, None))
    return jax.shard_map(
        on_device, mesh=mesh, in_specs=in_specs, out_specs=out_specs, check_vma=False
    )
```

```python
import functools

import jax
import jax.numpy as jnp
from jax import lax
from jax.experimental import pallas as pl
from jax.experimental.pallas import tpu as pltpu
from jax.sharding import PartitionSpec as P

AXES = ("row", "col")
F32 = jnp.float32
VMEM = pltpu.VMEM
PARAMS = pltpu.CompilerParams(vmem_limit_bytes=40 * 2**20)
CHEAP = pl.CostEstimate(flops=1000, bytes_accessed=1000, transcendentals=0)


def split(x):
    high = x.astype(jnp.bfloat16)
    return high, (x - high.astype(F32)).astype(jnp.bfloat16)


def product(a, b, transposed=False):
    dims = (((1,), (1 if transposed else 0,)), ((), ()))
    a_high, a_low = split(a)
    b_high, b_low = split(b)
    n = a.shape[0]
    both = lax.dot_general(
        jnp.concatenate([a_high, a_low], 0), b_high, dims, preferred_element_type=F32
    )
    cross = lax.dot_general(a_high, b_low, dims, preferred_element_type=F32)
    return both[:n] + (both[n:] + cross)


def position(col_count):
    return lax.axis_index("row") * col_count + lax.axis_index("col")


def stacked(pieces, which):
    return jnp.concatenate([p[which].T for p in pieces], axis=1)


def low_kernel(homes, col_count, own, g1, g2, g3, near, la, lx, ly, inverses, w, s_a, s_b, inv, sem):
    me = position(col_count)

    def work(block):
        copies = [pltpu.make_async_copy(inverses.at[i], inv.at[i], sem.at[i]) for i in range(2)]
        for copy in copies:
            copy.start()
        pieces = (own, g1, g2, g3)
        right = stacked(pieces, 0)
        copies[0].wait()
        first = product(right, inv[0], True)
        s_a[...] = first
        right = stacked(pieces, 1) - product(first, block[...])
        copies[1].wait()
        second = product(right, inv[1], True)
        s_b[...] = second
        w[...] = product(first, lx[...]) + product(second, ly[...])

    @pl.when(me == homes[0])
    def _():
        work(la)

    @pl.when(me == homes[1])
    def _():
        work(near)


def high_kernel(homes, col_count, own, g1, g2, g3, l_even, l_odd, w_1, w_2, inverses, s_a, s_b, inv, sem):
    me = position(col_count)

    def work(block, w_even, w_odd):
        copies = [pltpu.make_async_copy(inverses.at[2 + i], inv.at[i], sem.at[i]) for i in range(2)]
        for copy in copies:
            copy.start()
        pieces = (g3, g2, g1, own)
        right = stacked(pieces, 0) - w_even[...]
        copies[0].wait()
        first = product(right, inv[0], True)
        s_a[...] = first
        right = stacked(pieces, 1) - w_odd[...] - product(first, block[...])
        copies[1].wait()
        s_b[...] = product(right, inv[1], True)

    @pl.when(me == homes[0])
    def _():
        work(l_even, w_1, w_2)

    @pl.when(me == homes[1])
    def _():
        work(l_odd, w_2, w_1)


def update_kernel(cfg, *refs):
    steps, groups, row_count, share, have, members, blocks = cfg
    ways, panel = refs[:8], refs[8]
    outs, (tiles, s, full, sems) = refs[9: 9 + steps], refs[9 + steps:]
    quarter = full.shape[2] // steps
    row = lax.axis_index("row")
    col = lax.axis_index("col")
    member = col // groups
    group = col % groups

    def among(spots):
        return functools.reduce(jnp.logical_or, [(row == r) & (group == g) for r, g in spots])

    core = have[0][0] % 2
    first, first_twin = among(have), among([(r ^ 1, g) for r, g in have])
    same = lax.rem(row, 2) == core
    roles = (
        first, same & jnp.logical_not(first), first_twin,
        jnp.logical_not(same) & jnp.logical_not(first_twin),
    )

    @pl.when(functools.reduce(jnp.logical_or, [member == m for m in members]))
    def _():
        copies = [
            pltpu.make_async_copy(panel.at[r, 0, 0], tiles.at[r], sems.at[r]) for r in range(blocks)
        ]
        for copy in copies:
            copy.start()
        for m, plane in enumerate(members):
            for way, role in enumerate(roles):
                @pl.when((member == plane) & role)
                def _(src=ways[4 * m + way]):
                    s[...] = src[...]

        for r in range(blocks):
            copies[r].wait()
            block_id = (r * row_count + row) * groups + group
            keep = (block_id > member).astype(F32)
            full[r] = product(s[...], tiles[r]) * keep
        for offset in range(steps):
            to = lax.rem(member + offset, steps)
            columns = pl.ds(pl.multiple_of(to * quarter, quarter), quarter)
            for r in range(blocks):
                outs[offset][pl.ds(r * quarter, quarter), :] = full[r, :, columns]
            full[blocks, :, :quarter] = s[:, columns].T
            rows = pl.ds(pl.multiple_of(group * share, share), share)
            outs[offset][blocks * quarter:, :] = full[blocks, rows, :quarter]


def last_kernel(steps, groups, rhs, *refs):
    sources, (solved, out) = refs[: 2 * steps], refs[2 * steps:]
    lows, highs = sources[:steps], sources[steps:]
    blocks, quarter = rhs.shape[0], rhs.shape[1]
    member = lax.axis_index("col") // groups

    def finish(own):
        for r in range(blocks):
            rows = pl.ds(r * quarter, quarter)
            total = own[rows, :]
            for part in lows[1:] + highs[1:]:
                total = total + part[rows, :]
            out[r] = rhs[r] - total.T
        last = blocks * quarter
        solved[member] = own[last:, :]
        for offset in range(1, steps):
            solved[lax.rem(member + steps - offset, steps)] = (
                lows[offset][last:, :] + highs[offset][last:, :]
            )

    @pl.when(member < steps // 2)
    def _():
        finish(lows[0])

    @pl.when(member >= steps // 2)
    def _():
        finish(highs[0])


def on_device(factor, rhs, inverses):
    steps = inverses.shape[0]
    blocks = factor.shape[0]
    width = factor.shape[3]
    quarter = rhs.shape[3]
    nrhs = rhs.shape[4]
    row_count = lax.axis_size("row")
    col_count = lax.axis_size("col")
    groups = col_count // steps
    row_pos = lax.axis_index("row")
    col_pos = lax.axis_index("col")
    member = col_pos // groups
    group = col_pos % groups
    share = width // col_count
    top = steps - 1
    me = row_pos * col_count + col_pos

    def dev(row, mem, grp):
        return row * col_count + mem * groups + grp

    def line(g, mem):
        return dev(g // groups, mem, g % groups)

    low_homes = (line(0, 0), line(1, 0))
    high_homes = (line(2, top), line(3, top))

    def send(x, pairs):
        return lax.ppermute(x, AXES, pairs)

    def chosen(pairs, new, old):
        here = functools.reduce(jnp.logical_or, [me == d for _, d in pairs])
        return jnp.where(here, new, old)

    vmem = pl.BlockSpec(memory_space=VMEM)
    hbm = pl.BlockSpec(memory_space=pltpu.HBM)

    held_factor = pltpu.with_memory_space_constraint(factor, pltpu.HBM)
    held_inverses = pltpu.with_memory_space_constraint(inverses, pltpu.HBM)

    mine = rhs[0, 0, 0]
    other = send(mine, [(line(g ^ 1, m), line(g, m)) for g in range(4) for m in range(steps)])
    even = group % 2 == 0
    both = jnp.stack([jnp.where(even, mine, other), jnp.where(even, other, mine)])
    near = factor[0, 0, 0]
    ly = send(near, [(line(2, 1), low_homes[0]), (line(3, 1), low_homes[1]), (line(3, 2), high_homes[0])])
    later = lax.optimization_barrier((near, other))[0]
    la = send(later, [(line(1, 0), low_homes[0]), (line(3, 2), high_homes[1])])
    lx = send(later, [(line(2, 0), low_homes[0]), (line(3, 0), low_homes[1])])
    gathered = [
        send(both, [(line(g, j), line(g, 0)) for g in (0, 1)] + [(line(g, top - j), line(g, top)) for g in (2, 3)])
        for j in range(1, steps)
    ]

    vector = jax.ShapeDtypeStruct((nrhs, width), F32)
    two = [VMEM((2, width, width), F32), pltpu.SemaphoreType.DMA((2,))]
    w, s_0, s_1 = pl.pallas_call(
        functools.partial(low_kernel, low_homes, col_count),
        in_specs=[vmem] * 8 + [hbm],
        out_specs=[vmem] * 3,
        out_shape=[vector] * 3,
        scratch_shapes=two,
        compiler_params=PARAMS,
        cost_estimate=CHEAP,
        name="solve_low",
    )(both, *gathered, near, la, lx, ly, held_inverses)
    w_1 = send(w, [(low_homes[0], high_homes[0]), (low_homes[1], high_homes[1])])
    w_2 = send(w, [(low_homes[0], high_homes[1]), (low_homes[1], high_homes[0])])
    s_2, s_3 = pl.pallas_call(
        functools.partial(high_kernel, high_homes, col_count),
        in_specs=[vmem] * 8 + [hbm],
        out_specs=[vmem] * 2,
        out_shape=[vector] * 2,
        scratch_shapes=two,
        compiler_params=PARAMS,
        cost_estimate=CHEAP,
        name="solve_high",
    )(both, *gathered, ly, la, w_1, w_2, held_inverses)

    def spread(s, plane, lines):
        have = [(g // groups, g % groups) for g in lines]
        todo = [
            (r, g) for r in range(row_count) for g in range(groups)
            if r % 2 == have[0][0] % 2 and (r, g) not in have
        ]
        spots, far = list(have), None
        while todo:
            new, todo = todo[: len(spots)], todo[len(spots):]
            pairs = [(dev(a[0], plane, a[1]), dev(b[0], plane, b[1])) for a, b in zip(spots, new)]
            if far is None:
                far = send(s, pairs)
            else:
                held = chosen([(0, dev(r, plane, g)) for r, g in have], s, far)
                far = chosen(pairs, send(held, pairs), far)
            spots = spots + new
        twins = [(dev(r, plane, g), dev(r ^ 1, plane, g)) for r, g in spots]
        return s, far, send(s, twins[: len(have)]), send(far, twins[len(have):])

    def update(ways, lines, members):
        part = jax.ShapeDtypeStruct((blocks * quarter + share, nrhs), F32)
        have = [(g // groups, g % groups) for g in lines]
        cfg = (steps, groups, row_count, share, have, members, blocks)
        parts = pl.pallas_call(
            functools.partial(update_kernel, cfg),
            in_specs=[vmem] * 8 + [hbm],
            out_specs=[vmem] * steps,
            out_shape=[part] * steps,
            scratch_shapes=[
                VMEM((blocks, width, width), F32),
                VMEM((nrhs, width), F32),
                VMEM((blocks + 1, nrhs, width), F32),
                pltpu.SemaphoreType.DMA((blocks,)),
            ],
            compiler_params=PARAMS,
            cost_estimate=CHEAP,
            name="update",
        )(*ways, held_factor)
        got = [parts[0]]
        for offset in range(1, steps):
            pairs = [
                (dev(r, m, g), dev(r, (m + offset) % steps, g))
                for m in members for r in range(row_count) for g in range(groups)
            ]
            got.append(send(parts[offset], pairs))
        return got

    def both_planes(outer, inner, at, away, lines):
        moved = send(inner, [(line(g, at), line(g, away)) for g in lines])
        return spread(outer, at, lines) + spread(moved, away, lines)

    lows = update(both_planes(s_0, s_1, 0, 1, (0, 1)), (0, 1), (0, 1))
    highs = update(both_planes(s_3, s_2, top, top - 1, (2, 3)), (2, 3), (top, top - 1))

    solved, remaining = pl.pallas_call(
        functools.partial(last_kernel, steps, groups),
        in_specs=[vmem] * (1 + 2 * steps),
        out_specs=[vmem] * 2,
        out_shape=[
            jax.ShapeDtypeStruct((steps, share, nrhs), F32),
            jax.ShapeDtypeStruct((blocks, quarter, nrhs), F32),
        ],
        compiler_params=PARAMS,
        cost_estimate=CHEAP,
        name="add_up",
    )(rhs[:, 0, 0], *lows, *highs)
    return solved, remaining[:, None, None]


def solution(mesh):
    in_specs = (P(None, "row", "col", None, None), P(None, "row", "col", None, None), P())
    out_specs = (P(None, "col", None), P(None, "row", "col", None, None))
    return jax.shard_map(
        on_device, mesh=mesh, in_specs=in_specs, out_specs=out_specs, check_vma=False
    )
```

```python
import functools

import jax
import jax.numpy as jnp
from jax import lax
from jax.experimental import pallas as pl
from jax.experimental.pallas import tpu as pltpu
from jax.sharding import PartitionSpec as P

AXES = ("row", "col")
F32 = jnp.float32
VMEM = pltpu.VMEM
PARAMS = pltpu.CompilerParams(vmem_limit_bytes=40 * 2**20)
CHEAP = pl.CostEstimate(flops=1000, bytes_accessed=1000, transcendentals=0)


def split(x):
    high = x.astype(jnp.bfloat16)
    return high, (x - high.astype(F32)).astype(jnp.bfloat16)


def product(a, b, transposed=False):
    dims = (((1,), (1 if transposed else 0,)), ((), ()))
    a_high, a_low = split(a)
    b_high, b_low = split(b)
    n = a.shape[0]
    both = lax.dot_general(
        jnp.concatenate([a_high, a_low], 0), b_high, dims, preferred_element_type=F32
    )
    cross = lax.dot_general(a_high, b_low, dims, preferred_element_type=F32)
    return both[:n] + (both[n:] + cross)


def position(col_count):
    return lax.axis_index("row") * col_count + lax.axis_index("col")


def stacked(pieces, which):
    return jnp.concatenate([p[which].T for p in pieces], axis=1)


def low_kernel(homes, col_count, own, g1, g2, g3, near, la, lx, ly, inverses, w, s_a, s_b, inv, sem):
    me = position(col_count)

    def work(block):
        copies = [pltpu.make_async_copy(inverses.at[i], inv.at[i], sem.at[i]) for i in range(2)]
        for copy in copies:
            copy.start()
        pieces = (own, g1, g2, g3)
        right = stacked(pieces, 0)
        copies[0].wait()
        first = product(right, inv[0], True)
        s_a[...] = first
        right = stacked(pieces, 1) - product(first, block[...])
        copies[1].wait()
        second = product(right, inv[1], True)
        s_b[...] = second
        w[...] = product(first, lx[...]) + product(second, ly[...])

    @pl.when(me == homes[0])
    def _():
        work(la)

    @pl.when(me == homes[1])
    def _():
        work(near)


def high_kernel(homes, col_count, own, g1, g2, g3, l_even, l_odd, w_1, w_2, inverses, s_a, s_b, inv, sem):
    me = position(col_count)

    def work(block, w_even, w_odd):
        copies = [pltpu.make_async_copy(inverses.at[2 + i], inv.at[i], sem.at[i]) for i in range(2)]
        for copy in copies:
            copy.start()
        pieces = (g3, g2, g1, own)
        right = stacked(pieces, 0) - w_even[...]
        copies[0].wait()
        first = product(right, inv[0], True)
        s_a[...] = first
        right = stacked(pieces, 1) - w_odd[...] - product(first, block[...])
        copies[1].wait()
        s_b[...] = product(right, inv[1], True)

    @pl.when(me == homes[0])
    def _():
        work(l_even, w_1, w_2)

    @pl.when(me == homes[1])
    def _():
        work(l_odd, w_2, w_1)


def update_kernel(cfg, *refs):
    steps, groups, row_count, share, have, members, blocks, slots = cfg
    ways, panel = refs[:8], refs[8]
    outs, (tiles, s, full, sems) = refs[9: 9 + steps], refs[9 + steps:]
    quarter = full.shape[2] // steps
    row = lax.axis_index("row")
    col = lax.axis_index("col")
    member = col // groups
    group = col % groups

    def among(spots):
        return functools.reduce(jnp.logical_or, [(row == r) & (group == g) for r, g in spots])

    core = have[0][0] % 2
    first, first_twin = among(have), among([(r ^ 1, g) for r, g in have])
    same = lax.rem(row, 2) == core
    roles = (
        first, same & jnp.logical_not(first), first_twin,
        jnp.logical_not(same) & jnp.logical_not(first_twin),
    )

    @pl.when(functools.reduce(jnp.logical_or, [member == m for m in members]))
    def _():
        copies = [
            pltpu.make_async_copy(panel.at[r, 0, 0], tiles.at[r], sems.at[r]) for r in range(blocks)
        ]
        for copy in copies:
            copy.start()
        for m, plane in enumerate(members):
            for way, role in enumerate(roles):
                @pl.when((member == plane) & role)
                def _(src=ways[4 * m + way]):
                    s[...] = src[...]

        for r in range(blocks):
            copies[r].wait()
            block_id = (r * row_count + row) * groups + group
            keep = (block_id > member).astype(F32)
            full[r] = product(s[...], tiles[r]) * keep
        for slot in range(steps):
            ends, nexts = slots
            to = jnp.where(member == members[0], ends[slot], nexts[slot])
            columns = pl.ds(pl.multiple_of(to * quarter, quarter), quarter)
            for r in range(blocks):
                outs[slot][pl.ds(r * quarter, quarter), :] = full[r, :, columns]
            full[blocks, :, :quarter] = s[:, columns].T
            rows = pl.ds(pl.multiple_of(group * share, share), share)
            outs[slot][blocks * quarter:, :] = full[blocks, rows, :quarter]


def join_kernel(cfg, mine, theirs, out):
    groups, share, at = cfg
    last = mine.shape[0] - share

    @pl.when(lax.axis_index("col") // groups == at)
    def _():
        out[:last, :] = mine[:last, :] + theirs[:last, :]
        out[pl.ds(last, share), :] = mine[last:, :]
        out[pl.ds(last + share, share), :] = theirs[last:, :]


def last_kernel(groups, rhs, *refs):
    lows, highs, (solved, out) = refs[:5], refs[5:10], refs[10:]
    blocks, quarter = rhs.shape[0], rhs.shape[1]
    last, share = blocks * quarter, solved.shape[1]
    member = lax.axis_index("col") // groups

    def finish(at, parts, joined, joined_members):
        @pl.when(member == at)
        def _():
            for r in range(blocks):
                rows = pl.ds(r * quarter, quarter)
                total = functools.reduce(jnp.add, [part[rows, :] for part, _ in parts])
                if joined is not None:
                    total = total + joined[rows, :]
                out[r] = rhs[r] - total.T
            for part, k in parts:
                solved[k] = part[last:, :]
            for i, k in enumerate(joined_members):
                solved[k] = joined[pl.ds(last + i * share, share), :]

    finish(0, [(lows[0], 0), (lows[2], 1)], highs[4], (2, 3))
    finish(1, [(lows[0], 1), (lows[3], 0), (highs[1], 2), (highs[2], 3)], None, ())
    finish(2, [(highs[0], 2), (highs[3], 3), (lows[1], 1), (lows[2], 0)], None, ())
    finish(3, [(highs[0], 3), (highs[2], 2)], lows[4], (1, 0))


def on_device(factor, rhs, inverses):
    steps = inverses.shape[0]
    blocks = factor.shape[0]
    width = factor.shape[3]
    quarter = rhs.shape[3]
    nrhs = rhs.shape[4]
    row_count = lax.axis_size("row")
    col_count = lax.axis_size("col")
    groups = col_count // steps
    row_pos = lax.axis_index("row")
    col_pos = lax.axis_index("col")
    member = col_pos // groups
    group = col_pos % groups
    share = width // col_count
    top = steps - 1
    me = row_pos * col_count + col_pos

    def dev(row, mem, grp):
        return row * col_count + mem * groups + grp

    def line(g, mem):
        return dev(g // groups, mem, g % groups)

    low_homes = (line(0, 0), line(1, 0))
    high_homes = (line(2, top), line(3, top))

    def send(x, pairs):
        return lax.ppermute(x, AXES, pairs)

    def chosen(pairs, new, old):
        here = functools.reduce(jnp.logical_or, [me == d for _, d in pairs])
        return jnp.where(here, new, old)

    vmem = pl.BlockSpec(memory_space=VMEM)
    hbm = pl.BlockSpec(memory_space=pltpu.HBM)

    held_factor = pltpu.with_memory_space_constraint(factor, pltpu.HBM)
    held_inverses = pltpu.with_memory_space_constraint(inverses, pltpu.HBM)

    mine = rhs[0, 0, 0]
    other = send(mine, [(line(g ^ 1, m), line(g, m)) for g in range(4) for m in range(steps)])
    even = group % 2 == 0
    both = jnp.stack([jnp.where(even, mine, other), jnp.where(even, other, mine)])
    near = factor[0, 0, 0]
    ly = send(near, [(line(2, 1), low_homes[0]), (line(3, 1), low_homes[1]), (line(3, 2), high_homes[0])])
    later = lax.optimization_barrier((near, other))[0]
    la = send(later, [(line(1, 0), low_homes[0]), (line(3, 2), high_homes[1])])
    gathered = [
        send(both, [(line(g, j), line(g, 0)) for g in (0, 1)] + [(line(g, top - j), line(g, top)) for g in (2, 3)])
        for j in range(1, steps)
    ]
    later = lax.optimization_barrier((near, *gathered))[0]
    lx = send(later, [(line(2, 0), low_homes[0]), (line(3, 0), low_homes[1])])

    vector = jax.ShapeDtypeStruct((nrhs, width), F32)
    two = [VMEM((2, width, width), F32), pltpu.SemaphoreType.DMA((2,))]
    w, s_0, s_1 = pl.pallas_call(
        functools.partial(low_kernel, low_homes, col_count),
        in_specs=[vmem] * 8 + [hbm],
        out_specs=[vmem] * 3,
        out_shape=[vector] * 3,
        scratch_shapes=two,
        compiler_params=PARAMS,
        cost_estimate=CHEAP,
        name="solve_low",
    )(both, *gathered, near, la, lx, ly, held_inverses)
    w_1 = send(w, [(low_homes[0], high_homes[0]), (low_homes[1], high_homes[1])])
    w_2 = send(w, [(low_homes[0], high_homes[1]), (low_homes[1], high_homes[0])])
    s_2, s_3 = pl.pallas_call(
        functools.partial(high_kernel, high_homes, col_count),
        in_specs=[vmem] * 8 + [hbm],
        out_specs=[vmem] * 2,
        out_shape=[vector] * 2,
        scratch_shapes=two,
        compiler_params=PARAMS,
        cost_estimate=CHEAP,
        name="solve_high",
    )(both, *gathered, ly, la, w_1, w_2, held_inverses)

    def spread(s, plane, lines):
        have = [(g // groups, g % groups) for g in lines]
        todo = [
            (r, g) for r in range(row_count) for g in range(groups)
            if r % 2 == have[0][0] % 2 and (r, g) not in have
        ]
        spots, far = list(have), None
        while todo:
            new, todo = todo[: len(spots)], todo[len(spots):]
            pairs = [(dev(a[0], plane, a[1]), dev(b[0], plane, b[1])) for a, b in zip(spots, new)]
            if far is None:
                far = send(s, pairs)
            else:
                held = chosen([(0, dev(r, plane, g)) for r, g in have], s, far)
                far = chosen(pairs, send(held, pairs), far)
            spots = spots + new
        twins = [(dev(r, plane, g), dev(r ^ 1, plane, g)) for r, g in spots]
        return s, far, send(s, twins[: len(have)]), send(far, twins[len(have):])

    def update(ways, lines, members):
        part = jax.ShapeDtypeStruct((blocks * quarter + share, nrhs), F32)
        have = [(g // groups, g % groups) for g in lines]
        if members[0] == 0:
            ends, nexts = (0, 3, 2, 1), (1, 2, 0, 3)
        else:
            ends, nexts = (3, 0, 1, 2), (2, 1, 3, 0)
        slots = (ends, nexts)
        cfg = (steps, groups, row_count, share, have, members, blocks, slots)
        parts = pl.pallas_call(
            functools.partial(update_kernel, cfg),
            in_specs=[vmem] * 8 + [hbm],
            out_specs=[vmem] * steps,
            out_shape=[part] * steps,
            scratch_shapes=[
                VMEM((blocks, width, width), F32),
                VMEM((nrhs, width), F32),
                VMEM((blocks + 1, nrhs, width), F32),
                pltpu.SemaphoreType.DMA((blocks,)),
            ],
            compiler_params=PARAMS,
            cost_estimate=CHEAP,
            name="update",
        )(*ways, held_factor)
        across = [(r, g) for r in range(row_count) for g in range(groups)]

        def route(hops):
            return [(dev(r, a, g), dev(r, b, g)) for a, b in hops for r, g in across]

        end, near_end = members
        part_a = send(parts[1], route([(end, near_end), (near_end, nexts[1])]))
        part_b = send(parts[2], route([(end, ends[2]), (near_end, nexts[2])]))
        part_c = send(parts[3], route([(end, near_end)]))
        joint = jax.ShapeDtypeStruct((blocks * quarter + 2 * share, nrhs), F32)
        joined = pl.pallas_call(
            functools.partial(join_kernel, (groups, share, near_end)),
            in_specs=[vmem] * 2,
            out_specs=vmem,
            out_shape=joint,
            compiler_params=PARAMS,
            cost_estimate=CHEAP,
            name="join",
        )(parts[3], part_a)
        return parts[0], part_a, part_b, part_c, send(joined, route([(near_end, ends[1])]))

    def both_planes(outer, inner, at, away, lines):
        moved = send(inner, [(line(g, at), line(g, away)) for g in lines])
        return spread(outer, at, lines) + spread(moved, away, lines)

    lows = update(both_planes(s_0, s_1, 0, 1, (0, 1)), (0, 1), (0, 1))
    highs = update(both_planes(s_3, s_2, top, top - 1, (2, 3)), (2, 3), (top, top - 1))

    solved, remaining = pl.pallas_call(
        functools.partial(last_kernel, groups),
        in_specs=[vmem] * 11,
        out_specs=[vmem] * 2,
        out_shape=[
            jax.ShapeDtypeStruct((steps, share, nrhs), F32),
            jax.ShapeDtypeStruct((blocks, quarter, nrhs), F32),
        ],
        compiler_params=PARAMS,
        cost_estimate=CHEAP,
        name="add_up",
    )(rhs[:, 0, 0], *lows, *highs)
    return solved, remaining[:, None, None]


def solution(mesh):
    in_specs = (P(None, "row", "col", None, None), P(None, "row", "col", None, None), P())
    out_specs = (P(None, "col", None), P(None, "row", "col", None, None))
    return jax.shard_map(
        on_device, mesh=mesh, in_specs=in_specs, out_specs=out_specs, check_vma=False
    )
```

```python
import functools

import jax
import jax.numpy as jnp
from jax import lax
from jax.experimental import pallas as pl
from jax.experimental.pallas import tpu as pltpu
from jax.sharding import PartitionSpec as P

AXES = ("row", "col")
F32 = jnp.float32
VMEM = pltpu.VMEM
PARAMS = pltpu.CompilerParams(vmem_limit_bytes=40 * 2**20)
CHEAP = pl.CostEstimate(flops=1000, bytes_accessed=1000, transcendentals=0)


def split(x):
    high = x.astype(jnp.bfloat16)
    return high, (x - high.astype(F32)).astype(jnp.bfloat16)


def product(a, b, transposed=False):
    dims = (((1,), (1 if transposed else 0,)), ((), ()))
    a_high, a_low = split(a)
    b_high, b_low = split(b)
    n = a.shape[0]
    both = lax.dot_general(
        jnp.concatenate([a_high, a_low], 0), b_high, dims, preferred_element_type=F32
    )
    cross = lax.dot_general(a_high, b_low, dims, preferred_element_type=F32)
    return both[:n] + (both[n:] + cross)


def position(col_count):
    return lax.axis_index("row") * col_count + lax.axis_index("col")


def stacked(pieces, which):
    return jnp.concatenate([p[which].T for p in pieces], axis=1)


def low_kernel(homes, col_count, own, g1, g2, g3, near, la, lx, ly, inverses, w, s_a, s_b, inv, sem):
    me = position(col_count)

    def work(block):
        copies = [pltpu.make_async_copy(inverses.at[i], inv.at[i], sem.at[i]) for i in range(2)]
        for copy in copies:
            copy.start()
        pieces = (own, g1, g2, g3)
        right = stacked(pieces, 0)
        copies[0].wait()
        first = product(right, inv[0], True)
        s_a[...] = first
        right = stacked(pieces, 1) - product(first, block[...])
        copies[1].wait()
        second = product(right, inv[1], True)
        s_b[...] = second
        w[...] = product(first, lx[...]) + product(second, ly[...])

    @pl.when(me == homes[0])
    def _():
        work(la)

    @pl.when(me == homes[1])
    def _():
        work(near)


def high_kernel(homes, col_count, own, g1, g2, g3, block, w_1, w_2, inverses, s, inv, sem):
    me = position(col_count)
    copies = [pltpu.make_async_copy(inverses.at[2 + i], inv.at[i], sem.at[i]) for i in range(2)]

    @pl.when(me == homes[0])
    def _():
        copies[0].start()
        right = stacked((g2, g1, own, g3), 0) - w_2[...]
        copies[0].wait()
        s[...] = product(right, inv[0], True)

    @pl.when(me == homes[1])
    def _():
        for copy in copies:
            copy.start()
        pieces = (g3, g2, g1, own)
        right = stacked(pieces, 0) - w_1[...]
        copies[0].wait()
        first = product(right, inv[0], True)
        right = stacked(pieces, 1) - w_2[...] - product(first, block[...])
        copies[1].wait()
        s[...] = product(right, inv[1], True)


def update_kernel(cfg, *refs):
    steps, groups, row_count, share, homes, members, blocks, slots = cfg
    ways, panel = refs[:4], refs[4]
    outs, (tiles, s, full, sems) = refs[5: 5 + steps], refs[5 + steps:]
    quarter = full.shape[2] // steps
    row = lax.axis_index("row")
    col = lax.axis_index("col")
    member = col // groups
    group = col % groups

    def among(flip):
        return functools.reduce(jnp.logical_or, [
            (member == m) & (row == (r ^ flip)) & (group == g) for m in members for r, g in homes[m]
        ])

    first, first_twin = among(0), among(1)
    same = lax.rem(row, 2) == homes[members[0]][0][0] % 2
    roles = (
        first, same & jnp.logical_not(first), first_twin,
        jnp.logical_not(same) & jnp.logical_not(first_twin),
    )

    @pl.when(functools.reduce(jnp.logical_or, [member == m for m in members]))
    def _():
        copies = [
            pltpu.make_async_copy(panel.at[r, 0, 0], tiles.at[r], sems.at[r]) for r in range(blocks)
        ]
        for copy in copies:
            copy.start()
        for way, role in zip(ways, roles):
            @pl.when(role)
            def _(src=way):
                s[...] = src[...]

        for r in range(blocks):
            copies[r].wait()
            block_id = (r * row_count + row) * groups + group
            keep = (block_id > member).astype(F32)
            full[r] = product(s[...], tiles[r]) * keep
        for slot in range(steps):
            ends, nexts = slots
            to = jnp.where(member == members[0], ends[slot], nexts[slot])
            columns = pl.ds(pl.multiple_of(to * quarter, quarter), quarter)
            for r in range(blocks):
                outs[slot][pl.ds(r * quarter, quarter), :] = full[r, :, columns]
            full[blocks, :, :quarter] = s[:, columns].T
            rows = pl.ds(pl.multiple_of(group * share, share), share)
            outs[slot][blocks * quarter:, :] = full[blocks, rows, :quarter]


def join_kernel(cfg, mine, theirs, out):
    groups, share, at = cfg
    last = mine.shape[0] - share

    @pl.when(lax.axis_index("col") // groups == at)
    def _():
        out[:last, :] = mine[:last, :] + theirs[:last, :]
        out[pl.ds(last, share), :] = mine[last:, :]
        out[pl.ds(last + share, share), :] = theirs[last:, :]


def last_kernel(groups, rhs, *refs):
    lows, highs, (solved, out) = refs[:5], refs[5:10], refs[10:]
    blocks, quarter = rhs.shape[0], rhs.shape[1]
    last, share = blocks * quarter, solved.shape[1]
    member = lax.axis_index("col") // groups

    def finish(at, parts, joined, joined_members):
        @pl.when(member == at)
        def _():
            for r in range(blocks):
                rows = pl.ds(r * quarter, quarter)
                total = functools.reduce(jnp.add, [part[rows, :] for part, _ in parts])
                if joined is not None:
                    total = total + joined[rows, :]
                out[r] = rhs[r] - total.T
            for part, k in parts:
                solved[k] = part[last:, :]
            for i, k in enumerate(joined_members):
                solved[k] = joined[pl.ds(last + i * share, share), :]

    finish(0, [(lows[0], 0), (lows[2], 1)], highs[4], (2, 3))
    finish(1, [(lows[0], 1), (lows[3], 0), (highs[1], 2), (highs[2], 3)], None, ())
    finish(2, [(highs[0], 2), (highs[3], 3), (lows[1], 1), (lows[2], 0)], None, ())
    finish(3, [(highs[0], 3), (highs[2], 2)], lows[4], (1, 0))


def on_device(factor, rhs, inverses):
    steps = inverses.shape[0]
    blocks = factor.shape[0]
    width = factor.shape[3]
    quarter = rhs.shape[3]
    nrhs = rhs.shape[4]
    row_count = lax.axis_size("row")
    col_count = lax.axis_size("col")
    groups = col_count // steps
    row_pos = lax.axis_index("row")
    col_pos = lax.axis_index("col")
    member = col_pos // groups
    group = col_pos % groups
    share = width // col_count
    top = steps - 1
    me = row_pos * col_count + col_pos

    def dev(row, mem, grp):
        return row * col_count + mem * groups + grp

    def line(g, mem):
        return dev(g // groups, mem, g % groups)

    low_homes = (line(0, 0), line(1, 0))
    high_homes = (line(2, top - 1), line(3, top))

    def send(x, pairs):
        return lax.ppermute(x, AXES, pairs)

    def chosen(pairs, new, old):
        here = functools.reduce(jnp.logical_or, [me == d for _, d in pairs])
        return jnp.where(here, new, old)

    vmem = pl.BlockSpec(memory_space=VMEM)
    hbm = pl.BlockSpec(memory_space=pltpu.HBM)

    held_factor = pltpu.with_memory_space_constraint(factor, pltpu.HBM)
    held_inverses = pltpu.with_memory_space_constraint(inverses, pltpu.HBM)

    mine = rhs[0, 0, 0]
    near = factor[0, 0, 0]
    lx = send(near, [(line(2, 0), low_homes[0]), (line(3, 0), low_homes[1])])
    ly = send(near, [(line(2, 1), low_homes[0]), (line(3, 1), low_homes[1])])
    other = send(mine, [(line(g ^ 1, m), line(g, m)) for g in (0, 1, 3) for m in range(steps)])
    even = group % 2 == 0
    both = jnp.stack([jnp.where(even, mine, other), jnp.where(even, other, mine)])
    both, lx = lax.optimization_barrier((both, lx))
    later = lax.optimization_barrier((near, other))[0]
    la = send(later, [(line(1, 0), low_homes[0]), (line(3, 2), high_homes[1])])
    gathered = [
        send(
            both,
            [(line(g, j), line(g, 0)) for g in (0, 1)]
            + [(line(2, (top - 1 - j) % steps), high_homes[0]), (line(3, top - j), high_homes[1])],
        )
        for j in range(1, steps)
    ]

    vector = jax.ShapeDtypeStruct((nrhs, width), F32)
    two = [VMEM((2, width, width), F32), pltpu.SemaphoreType.DMA((2,))]
    w, s_0, s_1 = pl.pallas_call(
        functools.partial(low_kernel, low_homes, col_count),
        in_specs=[vmem] * 8 + [hbm],
        out_specs=[vmem] * 3,
        out_shape=[vector] * 3,
        scratch_shapes=two,
        compiler_params=PARAMS,
        cost_estimate=CHEAP,
        name="solve_low",
    )(both, *gathered, near, la, lx, ly, held_inverses)
    w_1 = send(w, [(low_homes[0], high_homes[1])])
    w_2 = send(w, [(low_homes[1], high_homes[1]), (low_homes[0], high_homes[0])])
    s_high = pl.pallas_call(
        functools.partial(high_kernel, high_homes, col_count),
        in_specs=[vmem] * 7 + [hbm],
        out_specs=vmem,
        out_shape=vector,
        scratch_shapes=two,
        compiler_params=PARAMS,
        cost_estimate=CHEAP,
        name="solve_high",
    )(both, *gathered, la, w_1, w_2, held_inverses)

    def spread(s, homes):
        have = {k: list(homes[k]) for k in homes}
        todo = {
            k: [
                (r, g) for r in range(row_count) for g in range(groups)
                if r % 2 == homes[k][0][0] % 2 and (r, g) not in homes[k]
            ]
            for k in homes
        }
        fan = 1 if all(len(spots) > 1 for spots in homes.values()) else 3
        firsts = [(0, dev(r, k, g)) for k in homes for r, g in homes[k]]
        far = None
        while any(todo.values()):
            held = s if far is None else chosen(firsts, s, far)
            rounds = [[] for _ in range(fan)]
            for k in homes:
                spots = list(have[k])
                for pairs in rounds:
                    for a in spots:
                        if todo[k]:
                            b = todo[k].pop()
                            have[k].append(b)
                            pairs.append((dev(a[0], k, a[1]), dev(b[0], k, b[1])))
            for pairs in rounds:
                if pairs:
                    got = send(held, pairs)
                    far = got if far is None else chosen(pairs, got, far)
        twins = {
            k: [(dev(r, k, g), dev(r ^ 1, k, g)) for r, g in have[k]] for k in homes
        }
        near_twins = [pair for k in homes for pair in twins[k][: len(homes[k])]]
        far_twins = [pair for k in homes for pair in twins[k][len(homes[k]):]]
        return s, far, send(s, near_twins), send(far, far_twins)

    def update(s, homes, members):
        part = jax.ShapeDtypeStruct((blocks * quarter + share, nrhs), F32)
        ways = spread(s, homes)
        if members[0] == 0:
            ends, nexts = (0, 3, 2, 1), (1, 2, 0, 3)
        else:
            ends, nexts = (3, 0, 1, 2), (2, 1, 3, 0)
        slots = (ends, nexts)
        cfg = (steps, groups, row_count, share, homes, members, blocks, slots)
        parts = pl.pallas_call(
            functools.partial(update_kernel, cfg),
            in_specs=[vmem] * 4 + [hbm],
            out_specs=[vmem] * steps,
            out_shape=[part] * steps,
            scratch_shapes=[
                VMEM((blocks, width, width), F32),
                VMEM((nrhs, width), F32),
                VMEM((blocks + 1, nrhs, width), F32),
                pltpu.SemaphoreType.DMA((blocks,)),
            ],
            compiler_params=PARAMS,
            cost_estimate=CHEAP,
            name="update",
        )(*ways, held_factor)
        across = [(r, g) for r in range(row_count) for g in range(groups)]

        def route(hops):
            return [(dev(r, a, g), dev(r, b, g)) for a, b in hops for r, g in across]

        end, near_end = members
        part_a = send(parts[1], route([(end, near_end), (near_end, nexts[1])]))
        part_b = send(parts[2], route([(end, ends[2]), (near_end, nexts[2])]))
        part_c = send(parts[3], route([(end, near_end)]))
        joint = jax.ShapeDtypeStruct((blocks * quarter + 2 * share, nrhs), F32)
        joined = pl.pallas_call(
            functools.partial(join_kernel, (groups, share, near_end)),
            in_specs=[vmem] * 2,
            out_specs=vmem,
            out_shape=joint,
            compiler_params=PARAMS,
            cost_estimate=CHEAP,
            name="join",
        )(parts[3], part_a)
        return parts[0], part_a, part_b, part_c, send(joined, route([(near_end, ends[1])]))

    spots = [(g // groups, g % groups) for g in range(4)]
    moved = send(s_1, [(line(g, 0), line(g, 1)) for g in (0, 1)])
    s_low = jnp.where(member == 0, s_0, moved)
    lows = update(s_low, {0: spots[:2], 1: spots[:2]}, (0, 1))
    highs = update(s_high, {top: [spots[3]], top - 1: [spots[2]]}, (top, top - 1))

    solved, remaining = pl.pallas_call(
        functools.partial(last_kernel, groups),
        in_specs=[vmem] * 11,
        out_specs=[vmem] * 2,
        out_shape=[
            jax.ShapeDtypeStruct((steps, share, nrhs), F32),
            jax.ShapeDtypeStruct((blocks, quarter, nrhs), F32),
        ],
        compiler_params=PARAMS,
        cost_estimate=CHEAP,
        name="add_up",
    )(rhs[:, 0, 0], *lows, *highs)
    return solved, remaining[:, None, None]


def solution(mesh):
    in_specs = (P(None, "row", "col", None, None), P(None, "row", "col", None, None), P())
    out_specs = (P(None, "col", None), P(None, "row", "col", None, None))
    return jax.shard_map(
        on_device, mesh=mesh, in_specs=in_specs, out_specs=out_specs, check_vma=False
    )
```

```python
import functools

import jax
import jax.numpy as jnp
from jax import lax
from jax.experimental import pallas as pl
from jax.experimental.pallas import tpu as pltpu
from jax.sharding import PartitionSpec as P

AXES = ("row", "col")
F32 = jnp.float32
VMEM = pltpu.VMEM
PARAMS = pltpu.CompilerParams(vmem_limit_bytes=20 * 2**20)
CHEAP = pl.CostEstimate(flops=1000, bytes_accessed=1000, transcendentals=0)


def split(x):
    high = x.astype(jnp.bfloat16)
    return high, (x - high.astype(F32)).astype(jnp.bfloat16)


def product(a, b, transposed=False):
    dims = (((1,), (1 if transposed else 0,)), ((), ()))
    a_high, a_low = split(a)
    b_high, b_low = split(b)
    n = a.shape[0]
    both = lax.dot_general(
        jnp.concatenate([a_high, a_low], 0), b_high, dims, preferred_element_type=F32
    )
    cross = lax.dot_general(a_high, b_low, dims, preferred_element_type=F32)
    return both[:n] + (both[n:] + cross)


def position(col_count):
    return lax.axis_index("row") * col_count + lax.axis_index("col")


def stacked(pieces, which):
    return jnp.concatenate([p[which].T for p in pieces], axis=1)


def low_kernel(homes, col_count, own, g1, g2, g3, near, la, inverses, s_a, s_b, inv, sem):
    me = position(col_count)

    def work(block):
        copies = [pltpu.make_async_copy(inverses.at[i], inv.at[i], sem.at[i]) for i in range(2)]
        for copy in copies:
            copy.start()
        pieces = (own, g1, g2, g3)
        right = stacked(pieces, 0)
        copies[0].wait()
        first = product(right, inv[0], True)
        s_a[...] = first
        right = stacked(pieces, 1) - product(first, block[...])
        copies[1].wait()
        s_b[...] = product(right, inv[1], True)

    @pl.when(me == homes[0])
    def _():
        work(la)

    @pl.when(me == homes[1])
    def _():
        work(near)


def reduce_kernel(homes, col_count, s_a, s_b, lx, ly, w):
    me = position(col_count)

    @pl.when((me == homes[0]) | (me == homes[1]))
    def _():
        w[...] = product(s_a[...], lx[...]) + product(s_b[...], ly[...])


def high_kernel(homes, col_count, own, g1, g2, g3, block, w_1, w_2, inverses, s, inv, sem):
    me = position(col_count)
    copies = [pltpu.make_async_copy(inverses.at[2 + i], inv.at[i], sem.at[i]) for i in range(2)]

    @pl.when(me == homes[0])
    def _():
        copies[0].start()
        right = stacked((g2, g1, own, g3), 0) - w_2[...]
        copies[0].wait()
        s[...] = product(right, inv[0], True)

    @pl.when(me == homes[1])
    def _():
        for copy in copies:
            copy.start()
        pieces = (g3, g2, g1, own)
        right = stacked(pieces, 0) - w_1[...]
        copies[0].wait()
        first = product(right, inv[0], True)
        right = stacked(pieces, 1) - w_2[...] - product(first, block[...])
        copies[1].wait()
        s[...] = product(right, inv[1], True)


def update_kernel(cfg, *refs):
    groups, row_count, share, homes, slots, blocks = cfg
    steps = len(homes)
    ways, panel, refs = refs[:8], refs[8], refs[9:]
    outs, (tiles, s, turned, sems) = refs[:2], refs[2:]
    quarter = turned.shape[0]
    row = lax.axis_index("row")
    col = lax.axis_index("col")
    member = col // groups
    group = col % groups
    columns = []
    for table in slots:
        to = functools.reduce(jnp.add, [jnp.where(member == m, p, 0) for m, p in enumerate(table)])
        columns.append(pl.ds(pl.multiple_of(to * quarter, quarter), quarter))
    copies = [
        [
            pltpu.make_async_copy(
                panel.at[r, 0, 0, :, columns[i]],
                tiles.at[r, :, pl.ds(i * quarter, quarter)],
                sems.at[2 * r + i],
            )
            for i in range(2)
        ]
        for r in range(blocks)
    ]
    for pair in copies:
        for copy in pair:
            copy.start()

    for half in range(2):
        planes = [m for m in range(steps) if m // (steps // 2) == half]

        def among(flip):
            return functools.reduce(jnp.logical_or, [
                (member == m) & (row == (r ^ flip)) & (group == g)
                for m in planes for r, g in homes[m]
            ])

        first, first_twin = among(0), among(1)
        here = functools.reduce(jnp.logical_or, [member == m for m in planes])
        same = here & (lax.rem(row, 2) == homes[planes[0]][0][0] % 2)
        other = here & (lax.rem(row, 2) != homes[planes[0]][0][0] % 2)
        roles = (
            first, same & jnp.logical_not(first), first_twin, other & jnp.logical_not(first_twin)
        )
        for way, role in zip(ways[4 * half:], roles):
            @pl.when(role)
            def _(src=way):
                s[...] = src[...]

    for r in range(blocks):
        for copy in copies[r]:
            copy.wait()
        block_id = (r * row_count + row) * groups + group
        keep = (block_id > member).astype(F32)
        full = product(s[...], tiles[r]) * keep
        for i, out in enumerate(outs):
            out[pl.ds(r * quarter, quarter), :] = full[:, i * quarter: (i + 1) * quarter]
    for i, out in enumerate(outs):
        turned[...] = s[:, columns[i]].T
        rows = pl.ds(pl.multiple_of(group * share, share), share)
        out[blocks * quarter:, :] = turned[rows, :]


def join_kernel(cfg, mine, theirs, got_2, got_4, out):
    del got_2, got_4
    groups, share = cfg
    last = mine.shape[0] - share
    member = lax.axis_index("col") // groups

    @pl.when((member == 1) | (member == 2))
    def _():
        out[:last, :] = mine[:last, :] + theirs[:last, :]
        out[pl.ds(last, share), :] = mine[last:, :]
        out[pl.ds(last + share, share), :] = theirs[last:, :]


def last_kernel(groups, rhs, own, got_1, got_2, got_3, got_4, joined, solved, out):
    blocks, quarter = rhs.shape[0], rhs.shape[1]
    last, share = blocks * quarter, solved.shape[1]
    member = lax.axis_index("col") // groups

    def finish(at, parts, joined_members=()):
        @pl.when(member == at)
        def _():
            for r in range(blocks):
                rows = pl.ds(r * quarter, quarter)
                total = functools.reduce(jnp.add, [part[rows, :] for part, _ in parts])
                if joined_members:
                    total = total + joined[rows, :]
                out[r] = rhs[r] - total.T
            for part, k in parts:
                solved[k] = part[last:, :]
            for i, k in enumerate(joined_members):
                solved[k] = joined[pl.ds(last + i * share, share), :]

    finish(0, [(own, 0), (got_1, 1)], (2, 3))
    finish(1, [(own, 1), (got_2, 3), (got_3, 0), (got_4, 2)])
    finish(2, [(own, 2), (got_2, 0), (got_3, 3), (got_4, 1)])
    finish(3, [(own, 3), (got_1, 2)], (1, 0))


def on_device(factor, rhs, inverses):
    steps = inverses.shape[0]
    blocks = factor.shape[0]
    width = factor.shape[3]
    quarter = rhs.shape[3]
    nrhs = rhs.shape[4]
    row_count = lax.axis_size("row")
    col_count = lax.axis_size("col")
    groups = col_count // steps
    row_pos = lax.axis_index("row")
    col_pos = lax.axis_index("col")
    member = col_pos // groups
    group = col_pos % groups
    share = width // col_count
    top = steps - 1
    me = row_pos * col_count + col_pos

    def dev(row, mem, grp):
        return row * col_count + mem * groups + grp

    def line(g, mem):
        return dev(g // groups, mem, g % groups)

    low_homes = (line(0, 0), line(1, 0))
    high_homes = (line(2, top - 1), line(3, top))

    def send(x, pairs):
        return lax.ppermute(x, AXES, pairs)

    def chosen(pairs, new, old):
        here = functools.reduce(jnp.logical_or, [me == d for _, d in pairs])
        return jnp.where(here, new, old)

    vmem = pl.BlockSpec(memory_space=VMEM)
    hbm = pl.BlockSpec(memory_space=pltpu.HBM)

    held_factor = pltpu.with_memory_space_constraint(factor, pltpu.HBM)
    held_inverses = pltpu.with_memory_space_constraint(inverses, pltpu.HBM)

    mine = rhs[0, 0, 0]
    near = factor[0, 0, 0]
    lx = send(near, [(line(2, 0), low_homes[0]), (line(3, 0), low_homes[1])])
    ly = send(near, [(line(2, 1), low_homes[0]), (line(3, 1), low_homes[1])])
    other = send(mine, [(line(g ^ 1, m), line(g, m)) for g in (0, 1, 3) for m in range(steps)])
    even = group % 2 == 0
    both = jnp.stack([jnp.where(even, mine, other), jnp.where(even, other, mine)])
    both, lx = lax.optimization_barrier((both, lx))
    later = lax.optimization_barrier((near, other))[0]
    la = send(later, [(line(1, 0), low_homes[0]), (line(3, 2), high_homes[1])])
    gathered = [
        send(
            both,
            [(line(g, j), line(g, 0)) for g in (0, 1)]
            + [(line(2, (top - 1 - j) % steps), high_homes[0]), (line(3, top - j), high_homes[1])],
        )
        for j in range(1, steps)
    ]

    vector = jax.ShapeDtypeStruct((nrhs, width), F32)
    two = [VMEM((2, width, width), F32), pltpu.SemaphoreType.DMA((2,))]
    s_0, s_1 = pl.pallas_call(
        functools.partial(low_kernel, low_homes, col_count),
        in_specs=[vmem] * 6 + [hbm],
        out_specs=[vmem] * 2,
        out_shape=[vector] * 2,
        scratch_shapes=two,
        compiler_params=PARAMS,
        cost_estimate=CHEAP,
        name="solve_low",
    )(both, *gathered, near, la, held_inverses)
    w = pl.pallas_call(
        functools.partial(reduce_kernel, low_homes, col_count),
        in_specs=[vmem] * 4,
        out_specs=vmem,
        out_shape=vector,
        compiler_params=PARAMS,
        cost_estimate=CHEAP,
        name="reduce_low",
    )(s_0, s_1, lx, ly)
    w_1 = send(w, [(low_homes[0], high_homes[1])])
    w_2 = send(w, [(low_homes[1], high_homes[1]), (low_homes[0], high_homes[0])])
    s_high = pl.pallas_call(
        functools.partial(high_kernel, high_homes, col_count),
        in_specs=[vmem] * 7 + [hbm],
        out_specs=vmem,
        out_shape=vector,
        scratch_shapes=two,
        compiler_params=PARAMS,
        cost_estimate=CHEAP,
        name="solve_high",
    )(both, *gathered, la, w_1, w_2, held_inverses)

    def spread(s, homes):
        have = {k: list(homes[k]) for k in homes}
        todo = {
            k: sorted(
                [
                    (r, g) for r in range(row_count) for g in range(groups)
                    if r % 2 == homes[k][0][0] % 2 and (r, g) not in homes[k]
                ],
                key=lambda spot: -(spot[0] != homes[k][0][0]) - (spot[1] != homes[k][0][1]),
            )
            for k in homes
        }
        fan = 1 if all(len(spots) > 1 for spots in homes.values()) else 3
        firsts = [(0, dev(r, k, g)) for k in homes for r, g in homes[k]]
        far = None
        while any(todo.values()):
            held = s if far is None else chosen(firsts, s, far)
            rounds = [[] for _ in range(fan)]
            for k in homes:
                spots = list(have[k])
                for pairs in rounds:
                    for a in spots:
                        if todo[k]:
                            b = todo[k].pop()
                            have[k].append(b)
                            pairs.append((dev(a[0], k, a[1]), dev(b[0], k, b[1])))
            for pairs in rounds:
                if pairs:
                    got = send(held, pairs)
                    far = got if far is None else chosen(pairs, got, far)
        twins = {
            k: [(dev(r, k, g), dev(r ^ 1, k, g)) for r, g in have[k]] for k in homes
        }
        near_twins = [pair for k in homes for pair in twins[k][: len(homes[k])]]
        far_twins = [pair for k in homes for pair in twins[k][len(homes[k]):]]
        return s, far, send(s, near_twins), send(far, far_twins)

    spots = [(g // groups, g % groups) for g in range(4)]
    homes = (tuple(spots[:2]), tuple(spots[:2]), (spots[2],), (spots[3],))
    moved = send(s_1, [(line(g, 0), line(g, 1)) for g in (0, 1)])
    s_low = jnp.where(member == 0, s_0, moved)
    ways = spread(s_low, {0: homes[0], 1: homes[1]}) + spread(s_high, {2: homes[2], 3: homes[3]})

    part = jax.ShapeDtypeStruct((blocks * quarter + share, nrhs), F32)

    def update(name, *slots):
        return pl.pallas_call(
            functools.partial(update_kernel, (groups, row_count, share, homes, slots, blocks)),
            in_specs=[vmem] * 8 + [hbm],
            out_specs=[vmem] * 2,
            out_shape=[part] * 2,
            scratch_shapes=[
                VMEM((blocks, width, 2 * quarter), F32),
                VMEM((nrhs, width), F32),
                VMEM((quarter, nrhs), F32),
                pltpu.SemaphoreType.DMA((2 * blocks,)),
            ],
            compiler_params=PARAMS,
            cost_estimate=CHEAP,
            name=name,
        )(*ways, held_factor)

    part_a, part_b = update("update_first", (3, 0, 3, 0), (2, 2, 1, 1))
    own, part_c = update("update_second", (0, 1, 2, 3), (1, 3, 0, 2))
    across = [(r, g) for r in range(row_count) for g in range(groups)]

    def route(*hops):
        return [(dev(r, a, g), dev(r, b, g)) for a, b in hops for r, g in across]

    got_1 = send(part_a, route((3, 2), (0, 1), (1, 0), (2, 3)))
    got_4 = send(part_b, route((2, 1), (1, 2)))
    got_3 = send(part_c, route((3, 2), (0, 1)))
    got_2 = send(part_b, route((3, 1), (0, 2)))
    joint = jax.ShapeDtypeStruct((blocks * quarter + 2 * share, nrhs), F32)
    joined = pl.pallas_call(
        functools.partial(join_kernel, (groups, share)),
        in_specs=[vmem] * 2 + [pl.BlockSpec(memory_space=pl.ANY)] * 2,
        out_specs=vmem,
        out_shape=joint,
        compiler_params=PARAMS,
        cost_estimate=CHEAP,
        name="join",
    )(part_c, got_1, got_2, got_4)
    joined = send(joined, route((2, 0), (1, 3)))

    solved, remaining = pl.pallas_call(
        functools.partial(last_kernel, groups),
        in_specs=[vmem] * 7,
        out_specs=[vmem] * 2,
        out_shape=[
            jax.ShapeDtypeStruct((steps, share, nrhs), F32),
            jax.ShapeDtypeStruct((blocks, quarter, nrhs), F32),
        ],
        compiler_params=PARAMS,
        cost_estimate=CHEAP,
        name="add_up",
    )(rhs[:, 0, 0], own, got_1, got_2, got_3, got_4, joined)
    return solved, remaining[:, None, None]


def solution(mesh):
    in_specs = (P(None, "row", "col", None, None), P(None, "row", "col", None, None), P())
    out_specs = (P(None, "col", None), P(None, "row", "col", None, None))
    return jax.shard_map(
        on_device, mesh=mesh, in_specs=in_specs, out_specs=out_specs, check_vma=False
    )
```

```python
import functools

import jax
import jax.numpy as jnp
from jax import lax
from jax.experimental import pallas as pl
from jax.experimental.pallas import tpu as pltpu
from jax.sharding import PartitionSpec as P

AXES = ("row", "col")
F32 = jnp.float32
VMEM = pltpu.VMEM
PARAMS = pltpu.CompilerParams(vmem_limit_bytes=20 * 2**20)
CHEAP = pl.CostEstimate(flops=1000, bytes_accessed=1000, transcendentals=0)


def split(x):
    high = x.astype(jnp.bfloat16)
    return high, (x - high.astype(F32)).astype(jnp.bfloat16)


def product(a, b, transposed=False):
    dims = (((1,), (1 if transposed else 0,)), ((), ()))
    a_high, a_low = split(a)
    b_high, b_low = split(b)
    n = a.shape[0]
    both = lax.dot_general(
        jnp.concatenate([a_high, a_low], 0), b_high, dims, preferred_element_type=F32
    )
    cross = lax.dot_general(a_high, b_low, dims, preferred_element_type=F32)
    return both[:n] + (both[n:] + cross)


def position(col_count):
    return lax.axis_index("row") * col_count + lax.axis_index("col")


def turn_kernel(order, solver, col_count, own, g1, g2, g3, inverses, out, inv, sem):
    me = position(col_count)

    def joined(pieces):
        return jnp.concatenate([piece[...].T for piece in pieces], axis=1)

    @pl.when(me == solver)
    def _():
        copy = pltpu.make_async_copy(inverses.at[0], inv, sem)
        copy.start()
        right = joined((own, g1, g2, g3))
        copy.wait()
        out[...] = product(right, inv[...], True)

    for device, places in order:
        @pl.when(me == device)
        def _(places=places):
            refs = (own, g1, g2, g3)
            out[...] = joined([refs[i] for i in places])


def low_kernel(homes, col_count, out, swapped, near, la, inverses, s_a, s_b, inv, sem):
    me = position(col_count)

    def work(first, right, block):
        copy = pltpu.make_async_copy(inverses.at[1], inv, sem)
        copy.start()
        s_a[...] = first[...]
        left = right[...] - product(first[...], block[...])
        copy.wait()
        s_b[...] = product(left, inv[...], True)

    @pl.when(me == homes[0])
    def _():
        work(out, swapped, la)

    @pl.when(me == homes[1])
    def _():
        work(swapped, out, near)


def reduce_kernel(homes, col_count, s_a, s_b, lx, ly, w):
    me = position(col_count)

    @pl.when((me == homes[0]) | (me == homes[1]))
    def _():
        w[...] = product(s_a[...], lx[...]) + product(s_b[...], ly[...])


def high_kernel(homes, col_count, own, swapped, block, w_1, w_2, inverses, s, inv, sem):
    me = position(col_count)
    copies = [pltpu.make_async_copy(inverses.at[2 + i], inv.at[i], sem.at[i]) for i in range(2)]

    @pl.when(me == homes[0])
    def _():
        copies[0].start()
        right = own[...] - w_2[...]
        copies[0].wait()
        s[...] = product(right, inv[0], True)

    @pl.when(me == homes[1])
    def _():
        for copy in copies:
            copy.start()
        right = swapped[...] - w_1[...]
        copies[0].wait()
        first = product(right, inv[0], True)
        right = own[...] - w_2[...] - product(first, block[...])
        copies[1].wait()
        s[...] = product(right, inv[1], True)


def update_kernel(cfg, *refs):
    groups, row_count, share, homes, slots, blocks = cfg
    steps = len(homes)
    ways, panel, refs = refs[:8], refs[8], refs[9:]
    outs, (tiles, s, turned, sems) = refs[:2], refs[2:]
    quarter = turned.shape[0]
    row = lax.axis_index("row")
    col = lax.axis_index("col")
    member = col // groups
    group = col % groups
    columns = []
    for table in slots:
        to = functools.reduce(jnp.add, [jnp.where(member == m, p, 0) for m, p in enumerate(table)])
        columns.append(pl.ds(pl.multiple_of(to * quarter, quarter), quarter))
    copies = [
        [
            pltpu.make_async_copy(
                panel.at[r, 0, 0, :, columns[i]],
                tiles.at[r, :, pl.ds(i * quarter, quarter)],
                sems.at[2 * r + i],
            )
            for i in range(2)
        ]
        for r in range(blocks)
    ]
    for pair in copies:
        for copy in pair:
            copy.start()

    for half in range(2):
        planes = [m for m in range(steps) if m // (steps // 2) == half]

        def among(flip):
            return functools.reduce(jnp.logical_or, [
                (member == m) & (row == (r ^ flip)) & (group == g)
                for m in planes for r, g in homes[m]
            ])

        first, first_twin = among(0), among(1)
        here = functools.reduce(jnp.logical_or, [member == m for m in planes])
        same = here & (lax.rem(row, 2) == homes[planes[0]][0][0] % 2)
        other = here & (lax.rem(row, 2) != homes[planes[0]][0][0] % 2)
        roles = (
            first, same & jnp.logical_not(first), first_twin, other & jnp.logical_not(first_twin)
        )
        for way, role in zip(ways[4 * half:], roles):
            @pl.when(role)
            def _(src=way):
                s[...] = src[...]

    for r in range(blocks):
        for copy in copies[r]:
            copy.wait()
        block_id = (r * row_count + row) * groups + group
        keep = (block_id > member).astype(F32)
        full = product(s[...], tiles[r]) * keep
        for i, out in enumerate(outs):
            out[pl.ds(r * quarter, quarter), :] = full[:, i * quarter: (i + 1) * quarter]
    for i, out in enumerate(outs):
        turned[...] = s[:, columns[i]].T
        rows = pl.ds(pl.multiple_of(group * share, share), share)
        out[blocks * quarter:, :] = turned[rows, :]


def join_kernel(cfg, mine, theirs, got_2, got_4, out):
    del got_2, got_4
    groups, share = cfg
    last = mine.shape[0] - share
    member = lax.axis_index("col") // groups

    @pl.when((member == 1) | (member == 2))
    def _():
        out[:last, :] = mine[:last, :] + theirs[:last, :]
        out[pl.ds(last, share), :] = mine[last:, :]
        out[pl.ds(last + share, share), :] = theirs[last:, :]


def last_kernel(groups, rhs, own, got_1, got_2, got_3, got_4, joined, solved, out):
    blocks, quarter = rhs.shape[0], rhs.shape[1]
    last, share = blocks * quarter, solved.shape[1]
    member = lax.axis_index("col") // groups

    def finish(at, parts, joined_members=()):
        @pl.when(member == at)
        def _():
            for r in range(blocks):
                rows = pl.ds(r * quarter, quarter)
                total = functools.reduce(jnp.add, [part[rows, :] for part, _ in parts])
                if joined_members:
                    total = total + joined[rows, :]
                out[r] = rhs[r] - total.T
            for part, k in parts:
                solved[k] = part[last:, :]
            for i, k in enumerate(joined_members):
                solved[k] = joined[pl.ds(last + i * share, share), :]

    finish(0, [(own, 0), (got_1, 1)], (2, 3))
    finish(1, [(own, 1), (got_2, 3), (got_3, 0), (got_4, 2)])
    finish(2, [(own, 2), (got_2, 0), (got_3, 3), (got_4, 1)])
    finish(3, [(own, 3), (got_1, 2)], (1, 0))


def on_device(factor, rhs, inverses):
    steps = inverses.shape[0]
    blocks = factor.shape[0]
    width = factor.shape[3]
    quarter = rhs.shape[3]
    nrhs = rhs.shape[4]
    row_count = lax.axis_size("row")
    col_count = lax.axis_size("col")
    groups = col_count // steps
    row_pos = lax.axis_index("row")
    col_pos = lax.axis_index("col")
    member = col_pos // groups
    group = col_pos % groups
    share = width // col_count
    top = steps - 1
    me = row_pos * col_count + col_pos

    def dev(row, mem, grp):
        return row * col_count + mem * groups + grp

    def line(g, mem):
        return dev(g // groups, mem, g % groups)

    low_homes = (line(0, 0), line(1, 0))
    high_homes = (line(2, top - 1), line(3, top))

    def send(x, pairs):
        return lax.ppermute(x, AXES, pairs)

    def chosen(pairs, new, old):
        here = functools.reduce(jnp.logical_or, [me == d for _, d in pairs])
        return jnp.where(here, new, old)

    vmem = pl.BlockSpec(memory_space=VMEM)
    hbm = pl.BlockSpec(memory_space=pltpu.HBM)

    held_factor = pltpu.with_memory_space_constraint(factor, pltpu.HBM)
    held_inverses = pltpu.with_memory_space_constraint(inverses, pltpu.HBM)

    mine = rhs[0, 0, 0]
    gathered = [
        send(
            mine,
            [(line(g, j), line(g, 0)) for g in (0, 1)]
            + [(line(2, (top - 1 - j) % steps), high_homes[0]), (line(3, top - j), high_homes[1])],
        )
        for j in range(1, steps)
    ]
    near = factor[0, 0, 0]
    la = send(near, [(line(1, 0), low_homes[0]), (line(3, 2), high_homes[1])])
    ly = send(near, [(line(2, 1), low_homes[0]), (line(3, 1), low_homes[1])])

    vector = jax.ShapeDtypeStruct((nrhs, width), F32)
    one = [VMEM((width, width), F32), pltpu.SemaphoreType.DMA]
    two = [VMEM((2, width, width), F32), pltpu.SemaphoreType.DMA((2,))]
    order = ((low_homes[1], (0, 1, 2, 3)), (high_homes[0], (2, 1, 0, 3)), (high_homes[1], (3, 2, 1, 0)))
    turned = pl.pallas_call(
        functools.partial(turn_kernel, order, low_homes[0], col_count),
        in_specs=[vmem] * 4 + [hbm],
        out_specs=vmem,
        out_shape=vector,
        scratch_shapes=one,
        compiler_params=PARAMS,
        cost_estimate=CHEAP,
        name="turn",
    )(mine, *gathered, held_inverses)
    swapped = send(turned, [low_homes, low_homes[::-1], high_homes])
    later = lax.optimization_barrier((near, turned))[0]
    lx = send(later, [(line(2, 0), low_homes[0]), (line(3, 0), low_homes[1])])
    s_0, s_1 = pl.pallas_call(
        functools.partial(low_kernel, low_homes, col_count),
        in_specs=[vmem] * 4 + [hbm],
        out_specs=[vmem] * 2,
        out_shape=[vector] * 2,
        scratch_shapes=one,
        compiler_params=PARAMS,
        cost_estimate=CHEAP,
        name="solve_low",
    )(turned, swapped, near, la, held_inverses)
    w = pl.pallas_call(
        functools.partial(reduce_kernel, low_homes, col_count),
        in_specs=[vmem] * 4,
        out_specs=vmem,
        out_shape=vector,
        compiler_params=PARAMS,
        cost_estimate=CHEAP,
        name="reduce_low",
    )(s_0, s_1, lx, ly)
    w_1 = send(w, [(low_homes[0], high_homes[1])])
    w_2 = send(w, [(low_homes[1], high_homes[1]), (low_homes[0], high_homes[0])])
    s_high = pl.pallas_call(
        functools.partial(high_kernel, high_homes, col_count),
        in_specs=[vmem] * 5 + [hbm],
        out_specs=vmem,
        out_shape=vector,
        scratch_shapes=two,
        compiler_params=PARAMS,
        cost_estimate=CHEAP,
        name="solve_high",
    )(turned, swapped, la, w_1, w_2, held_inverses)

    def spread(s, homes):
        have = {k: list(homes[k]) for k in homes}
        todo = {
            k: sorted(
                [
                    (r, g) for r in range(row_count) for g in range(groups)
                    if r % 2 == homes[k][0][0] % 2 and (r, g) not in homes[k]
                ],
                key=lambda spot: -(spot[0] != homes[k][0][0]) - (spot[1] != homes[k][0][1]),
            )
            for k in homes
        }
        fan = 1 if all(len(spots) > 1 for spots in homes.values()) else 3
        firsts = [(0, dev(r, k, g)) for k in homes for r, g in homes[k]]
        far = None
        while any(todo.values()):
            held = s if far is None else chosen(firsts, s, far)
            rounds = [[] for _ in range(fan)]
            for k in homes:
                spots = list(have[k])
                for pairs in rounds:
                    for a in spots:
                        if todo[k]:
                            b = todo[k].pop()
                            have[k].append(b)
                            pairs.append((dev(a[0], k, a[1]), dev(b[0], k, b[1])))
            for pairs in rounds:
                if pairs:
                    got = send(held, pairs)
                    far = got if far is None else chosen(pairs, got, far)
        twins = {
            k: [(dev(r, k, g), dev(r ^ 1, k, g)) for r, g in have[k]] for k in homes
        }
        near_twins = [pair for k in homes for pair in twins[k][: len(homes[k])]]
        far_twins = [pair for k in homes for pair in twins[k][len(homes[k]):]]
        return s, far, send(s, near_twins), send(far, far_twins)

    spots = [(g // groups, g % groups) for g in range(4)]
    homes = (tuple(spots[:2]), tuple(spots[:2]), (spots[2],), (spots[3],))
    moved = send(s_1, [(line(g, 0), line(g, 1)) for g in (0, 1)])
    s_low = jnp.where(member == 0, s_0, moved)
    ways = spread(s_low, {0: homes[0], 1: homes[1]}) + spread(s_high, {2: homes[2], 3: homes[3]})

    part = jax.ShapeDtypeStruct((blocks * quarter + share, nrhs), F32)

    def update(name, *slots):
        return pl.pallas_call(
            functools.partial(update_kernel, (groups, row_count, share, homes, slots, blocks)),
            in_specs=[vmem] * 8 + [hbm],
            out_specs=[vmem] * 2,
            out_shape=[part] * 2,
            scratch_shapes=[
                VMEM((blocks, width, 2 * quarter), F32),
                VMEM((nrhs, width), F32),
                VMEM((quarter, nrhs), F32),
                pltpu.SemaphoreType.DMA((2 * blocks,)),
            ],
            compiler_params=PARAMS,
            cost_estimate=CHEAP,
            name=name,
        )(*ways, held_factor)

    part_a, part_b = update("update_first", (3, 0, 3, 0), (2, 2, 1, 1))
    own, part_c = update("update_second", (0, 1, 2, 3), (1, 3, 0, 2))
    across = [(r, g) for r in range(row_count) for g in range(groups)]

    def route(*hops):
        return [(dev(r, a, g), dev(r, b, g)) for a, b in hops for r, g in across]

    got_1 = send(part_a, route((3, 2), (0, 1), (1, 0), (2, 3)))
    got_4 = send(part_b, route((2, 1), (1, 2)))
    got_3 = send(part_c, route((3, 2), (0, 1)))
    got_2 = send(part_b, route((3, 1), (0, 2)))
    joint = jax.ShapeDtypeStruct((blocks * quarter + 2 * share, nrhs), F32)
    joined = pl.pallas_call(
        functools.partial(join_kernel, (groups, share)),
        in_specs=[vmem] * 2 + [pl.BlockSpec(memory_space=pl.ANY)] * 2,
        out_specs=vmem,
        out_shape=joint,
        compiler_params=PARAMS,
        cost_estimate=CHEAP,
        name="join",
    )(part_c, got_1, got_2, got_4)
    joined = send(joined, route((2, 0), (1, 3)))

    solved, remaining = pl.pallas_call(
        functools.partial(last_kernel, groups),
        in_specs=[vmem] * 7,
        out_specs=[vmem] * 2,
        out_shape=[
            jax.ShapeDtypeStruct((steps, share, nrhs), F32),
            jax.ShapeDtypeStruct((blocks, quarter, nrhs), F32),
        ],
        compiler_params=PARAMS,
        cost_estimate=CHEAP,
        name="add_up",
    )(rhs[:, 0, 0], own, got_1, got_2, got_3, got_4, joined)
    return solved, remaining[:, None, None]


def solution(mesh):
    in_specs = (P(None, "row", "col", None, None), P(None, "row", "col", None, None), P())
    out_specs = (P(None, "col", None), P(None, "row", "col", None, None))
    return jax.shard_map(
        on_device, mesh=mesh, in_specs=in_specs, out_specs=out_specs, check_vma=False
    )
```

```python
import functools

import jax
import jax.numpy as jnp
from jax import lax
from jax.experimental import pallas as pl
from jax.experimental.pallas import tpu as pltpu
from jax.sharding import PartitionSpec as P

AXES = ("row", "col")
F32 = jnp.float32
VMEM = pltpu.VMEM
PARAMS = pltpu.CompilerParams(vmem_limit_bytes=20 * 2**20)
CHEAP = pl.CostEstimate(flops=1000, bytes_accessed=1000, transcendentals=0)


def split(x):
    high = x.astype(jnp.bfloat16)
    return high, (x - high.astype(F32)).astype(jnp.bfloat16)


def product(a, b, transposed=False):
    dims = (((1,), (1 if transposed else 0,)), ((), ()))
    a_high, a_low = split(a)
    b_high, b_low = split(b)
    n = a.shape[0]
    both = lax.dot_general(
        jnp.concatenate([a_high, a_low], 0), b_high, dims, preferred_element_type=F32
    )
    cross = lax.dot_general(a_high, b_low, dims, preferred_element_type=F32)
    return both[:n] + (both[n:] + cross)


def position(col_count):
    return lax.axis_index("row") * col_count + lax.axis_index("col")


def turn_kernel(order, solver, col_count, own, g1, g2, g3, inverses, out, inv, sem):
    me = position(col_count)

    def joined(pieces):
        return jnp.concatenate([piece[...].T for piece in pieces], axis=1)

    @pl.when(me == solver)
    def _():
        copy = pltpu.make_async_copy(inverses.at[0], inv, sem)
        copy.start()
        right = joined((own, g1, g2, g3))
        copy.wait()
        out[...] = product(right, inv[...], True)

    for device, places in order:
        @pl.when(me == device)
        def _(places=places):
            refs = (own, g1, g2, g3)
            out[...] = joined([refs[i] for i in places])


def low_kernel(homes, col_count, out, swapped, near, la, inverses, s_a, s_b, inv, sem):
    me = position(col_count)

    def work(first, right, block):
        copy = pltpu.make_async_copy(inverses.at[1], inv, sem)
        copy.start()
        s_a[...] = first[...]
        left = right[...] - product(first[...], block[...])
        copy.wait()
        s_b[...] = product(left, inv[...], True)

    @pl.when(me == homes[0])
    def _():
        work(out, swapped, la)

    @pl.when(me == homes[1])
    def _():
        work(swapped, out, near)


def reduce_kernel(homes, col_count, s_a, s_b, lx, ly, w):
    me = position(col_count)

    @pl.when((me == homes[0]) | (me == homes[1]))
    def _():
        w[...] = product(s_a[...], lx[...]) + product(s_b[...], ly[...])


def high_kernel(homes, col_count, own, swapped, block, w_1, w_2, inverses, s, inv, sem):
    me = position(col_count)
    copies = [pltpu.make_async_copy(inverses.at[2 + i], inv.at[i], sem.at[i]) for i in range(2)]

    @pl.when(me == homes[0])
    def _():
        copies[0].start()
        right = own[...] - w_2[...]
        copies[0].wait()
        s[...] = product(right, inv[0], True)

    @pl.when(me == homes[1])
    def _():
        for copy in copies:
            copy.start()
        right = swapped[...] - w_1[...]
        copies[0].wait()
        first = product(right, inv[0], True)
        right = own[...] - w_2[...] - product(first, block[...])
        copies[1].wait()
        s[...] = product(right, inv[1], True)


def update_kernel(cfg, *refs):
    groups, row_count, share, homes, slots, blocks = cfg
    steps = len(homes)
    ways, panel, refs = refs[:8], refs[8], refs[9:]
    outs, (tiles, s, turned, sems) = refs[:2], refs[2:]
    quarter = turned.shape[0]
    row = lax.axis_index("row")
    col = lax.axis_index("col")
    member = col // groups
    group = col % groups
    columns = []
    for table in slots:
        to = functools.reduce(jnp.add, [jnp.where(member == m, p, 0) for m, p in enumerate(table)])
        columns.append(pl.ds(pl.multiple_of(to * quarter, quarter), quarter))
    copies = [
        [
            pltpu.make_async_copy(
                panel.at[r, 0, 0, :, columns[i]],
                tiles.at[r, :, pl.ds(i * quarter, quarter)],
                sems.at[2 * r + i],
            )
            for i in range(2)
        ]
        for r in range(blocks)
    ]
    for pair in copies:
        for copy in pair:
            copy.start()

    for half in range(2):
        planes = [m for m in range(steps) if m // (steps // 2) == half]

        def among(flip):
            return functools.reduce(jnp.logical_or, [
                (member == m) & (row == (r ^ flip)) & (group == g)
                for m in planes for r, g in homes[m]
            ])

        first, first_twin = among(0), among(1)
        here = functools.reduce(jnp.logical_or, [member == m for m in planes])
        same = here & (lax.rem(row, 2) == homes[planes[0]][0][0] % 2)
        other = here & (lax.rem(row, 2) != homes[planes[0]][0][0] % 2)
        roles = (
            first, same & jnp.logical_not(first), first_twin, other & jnp.logical_not(first_twin)
        )
        for way, role in zip(ways[4 * half:], roles):
            @pl.when(role)
            def _(src=way):
                s[...] = src[...]

    for r in range(blocks):
        for copy in copies[r]:
            copy.wait()
        block_id = (r * row_count + row) * groups + group
        keep = (block_id > member).astype(F32)
        full = product(s[...], tiles[r]) * keep
        for i, out in enumerate(outs):
            out[pl.ds(r * quarter, quarter), :] = full[:, i * quarter: (i + 1) * quarter]
    for i, out in enumerate(outs):
        turned[...] = s[:, columns[i]].T
        rows = pl.ds(pl.multiple_of(group * share, share), share)
        out[pl.ds(blocks * quarter, share), :] = turned[rows, :]


def join_kernel(cfg, mine, theirs, got_2, got_4, out):
    del got_2, got_4
    groups, share = cfg
    last = theirs.shape[0] - share
    member = lax.axis_index("col") // groups
    out[...] = mine[...]

    @pl.when((member == 1) | (member == 2))
    def _():
        out[:last, :] = mine[:last, :] + theirs[:last, :]
        out[pl.ds(last + share, share), :] = theirs[last:, :]


def last_kernel(groups, rhs, own, got_1, got_2, got_4, got_3, solved, out):
    blocks, quarter = rhs.shape[0], rhs.shape[1]
    last, share = blocks * quarter, solved.shape[1]
    member = lax.axis_index("col") // groups

    def finish(at, parts, joined_members=()):
        @pl.when(member == at)
        def _():
            for r in range(blocks):
                rows = pl.ds(r * quarter, quarter)
                total = functools.reduce(jnp.add, [part[rows, :] for part, _ in parts])
                if joined_members:
                    total = total + got_3[rows, :]
                out[r] = rhs[r] - total.T
            for part, k in parts:
                solved[k] = part[pl.ds(last, share), :]
            for i, k in enumerate(joined_members):
                solved[k] = got_3[pl.ds(last + i * share, share), :]

    finish(0, [(own, 0), (got_1, 1)], (2, 3))
    finish(1, [(own, 1), (got_2, 3), (got_3, 0), (got_4, 2)])
    finish(2, [(own, 2), (got_2, 0), (got_3, 3), (got_4, 1)])
    finish(3, [(own, 3), (got_1, 2)], (1, 0))


def on_device(factor, rhs, inverses):
    steps = inverses.shape[0]
    blocks = factor.shape[0]
    width = factor.shape[3]
    quarter = rhs.shape[3]
    nrhs = rhs.shape[4]
    row_count = lax.axis_size("row")
    col_count = lax.axis_size("col")
    groups = col_count // steps
    row_pos = lax.axis_index("row")
    col_pos = lax.axis_index("col")
    member = col_pos // groups
    group = col_pos % groups
    share = width // col_count
    top = steps - 1
    me = row_pos * col_count + col_pos

    def dev(row, mem, grp):
        return row * col_count + mem * groups + grp

    def line(g, mem):
        return dev(g // groups, mem, g % groups)

    low_homes = (line(0, 0), line(1, 0))
    high_homes = (line(2, top - 1), line(3, top))

    def send(x, pairs):
        onward = dict(pairs)
        for start in sorted(set(onward) - set(onward.values())):
            stop = onward[start]
            while stop in onward:
                stop = onward[stop]
            onward[stop] = start
        everyone = range(row_count * col_count)
        return lax.ppermute(x, AXES, [(i, onward.get(i, i)) for i in everyone])

    def chosen(pairs, new, old):
        here = functools.reduce(jnp.logical_or, [me == d for _, d in pairs])
        return jnp.where(here, new, old)

    vmem = pl.BlockSpec(memory_space=VMEM)
    hbm = pl.BlockSpec(memory_space=pltpu.HBM)

    held_factor = pltpu.with_memory_space_constraint(factor, pltpu.HBM)
    held_inverses = pltpu.with_memory_space_constraint(inverses, pltpu.HBM)

    mine = rhs[0, 0, 0]
    gathered = [
        send(
            mine,
            [(line(g, j), line(g, 0)) for g in (0, 1)]
            + [(line(2, (top - 1 - j) % steps), high_homes[0]), (line(3, top - j), high_homes[1])],
        )
        for j in range(1, steps)
    ]
    near = factor[0, 0, 0]
    la = send(near, [(line(1, 0), low_homes[0])])
    ly = send(near, [(line(2, 1), low_homes[0]), (line(3, 1), low_homes[1]), (line(3, 2), high_homes[1])])

    vector = jax.ShapeDtypeStruct((nrhs, width), F32)
    one = [VMEM((width, width), F32), pltpu.SemaphoreType.DMA]
    two = [VMEM((2, width, width), F32), pltpu.SemaphoreType.DMA((2,))]
    order = ((low_homes[1], (0, 1, 2, 3)), (high_homes[0], (2, 1, 0, 3)), (high_homes[1], (3, 2, 1, 0)))
    turned = pl.pallas_call(
        functools.partial(turn_kernel, order, low_homes[0], col_count),
        in_specs=[vmem] * 4 + [hbm],
        out_specs=vmem,
        out_shape=vector,
        scratch_shapes=one,
        compiler_params=PARAMS,
        cost_estimate=CHEAP,
        name="turn",
    )(mine, *gathered, held_inverses)
    swapped = send(turned, [low_homes, low_homes[::-1], high_homes])
    later = lax.optimization_barrier((near, turned))[0]
    lx = send(later, [(line(2, 0), low_homes[0]), (line(3, 0), low_homes[1])])
    s_0, s_1 = pl.pallas_call(
        functools.partial(low_kernel, low_homes, col_count),
        in_specs=[vmem] * 4 + [hbm],
        out_specs=[vmem] * 2,
        out_shape=[vector] * 2,
        scratch_shapes=one,
        compiler_params=PARAMS,
        cost_estimate=CHEAP,
        name="solve_low",
    )(turned, swapped, near, la, held_inverses)
    w = pl.pallas_call(
        functools.partial(reduce_kernel, low_homes, col_count),
        in_specs=[vmem] * 4,
        out_specs=vmem,
        out_shape=vector,
        compiler_params=PARAMS,
        cost_estimate=CHEAP,
        name="reduce_low",
    )(s_0, s_1, lx, ly)
    w_1 = send(w, [(low_homes[0], high_homes[1])])
    w_2 = send(w, [(low_homes[1], high_homes[1]), (low_homes[0], high_homes[0])])
    s_high = pl.pallas_call(
        functools.partial(high_kernel, high_homes, col_count),
        in_specs=[vmem] * 5 + [hbm],
        out_specs=vmem,
        out_shape=vector,
        scratch_shapes=two,
        compiler_params=PARAMS,
        cost_estimate=CHEAP,
        name="solve_high",
    )(turned, swapped, ly, w_1, w_2, held_inverses)

    def spread(s, homes):
        have = {k: list(homes[k]) for k in homes}
        todo = {
            k: sorted(
                [
                    (r, g) for r in range(row_count) for g in range(groups)
                    if r % 2 == homes[k][0][0] % 2 and (r, g) not in homes[k]
                ],
                key=lambda spot: -(spot[0] != homes[k][0][0]) - (spot[1] != homes[k][0][1]),
            )
            for k in homes
        }
        fan = 1 if all(len(spots) > 1 for spots in homes.values()) else 3
        firsts = [(0, dev(r, k, g)) for k in homes for r, g in homes[k]]
        far = None
        while any(todo.values()):
            held = s if far is None else chosen(firsts, s, far)
            rounds = [[] for _ in range(fan)]
            for k in homes:
                spots = list(have[k])
                for pairs in rounds:
                    for a in spots:
                        if todo[k]:
                            b = todo[k].pop()
                            have[k].append(b)
                            pairs.append((dev(a[0], k, a[1]), dev(b[0], k, b[1])))
            for pairs in rounds:
                if pairs:
                    got = send(held, pairs)
                    far = got if far is None else chosen(pairs, got, far)
        twins = {
            k: [(dev(r, k, g), dev(r ^ 1, k, g)) for r, g in have[k]] for k in homes
        }
        near_twins = [pair for k in homes for pair in twins[k][: len(homes[k])]]
        far_twins = [pair for k in homes for pair in twins[k][len(homes[k]):]]
        return s, far, send(s, near_twins), send(far, far_twins)

    spots = [(g // groups, g % groups) for g in range(4)]
    homes = (tuple(spots[:2]), tuple(spots[:2]), (spots[2],), (spots[3],))
    moved = send(s_1, [(line(g, 0), line(g, 1)) for g in (0, 1)])
    s_low = jnp.where(member == 0, s_0, moved)
    ways = spread(s_low, {0: homes[0], 1: homes[1]}) + spread(s_high, {2: homes[2], 3: homes[3]})

    part, joint = [
        jax.ShapeDtypeStruct((blocks * quarter + n * share, nrhs), F32) for n in (1, 2)
    ]

    def update(name, shapes, *slots):
        return pl.pallas_call(
            functools.partial(update_kernel, (groups, row_count, share, homes, slots, blocks)),
            in_specs=[vmem] * 8 + [hbm],
            out_specs=[vmem] * 2,
            out_shape=shapes,
            scratch_shapes=[
                VMEM((blocks, width, 2 * quarter), F32),
                VMEM((nrhs, width), F32),
                VMEM((quarter, nrhs), F32),
                pltpu.SemaphoreType.DMA((2 * blocks,)),
            ],
            compiler_params=PARAMS,
            cost_estimate=CHEAP,
            name=name,
        )(*ways, held_factor)

    part_a, part_b = update("update_first", [part, part], (3, 0, 3, 0), (2, 2, 1, 1))
    own, part_c = update("update_second", [part, joint], (0, 1, 2, 3), (1, 3, 0, 2))
    across = [(r, g) for r in range(row_count) for g in range(groups)]

    def route(*hops):
        return [(dev(r, a, g), dev(r, b, g)) for a, b in hops for r, g in across]

    got_1 = send(part_a, route((3, 2), (0, 1), (1, 0), (2, 3)))
    got_4 = send(part_b, route((2, 1), (1, 2)))
    got_2 = send(part_b, route((3, 1), (1, 0), (0, 2), (2, 3)))
    joined = pl.pallas_call(
        functools.partial(join_kernel, (groups, share)),
        in_specs=[vmem] * 2 + [pl.BlockSpec(memory_space=pl.ANY)] * 2,
        out_specs=vmem,
        out_shape=joint,
        compiler_params=PARAMS,
        cost_estimate=CHEAP,
        name="join",
    )(part_c, got_1, got_2, got_4)
    got_3 = send(joined, route((3, 2), (0, 1), (2, 0), (1, 3)))

    solved, remaining = pl.pallas_call(
        functools.partial(last_kernel, groups),
        in_specs=[vmem] * 6,
        out_specs=[vmem] * 2,
        out_shape=[
            jax.ShapeDtypeStruct((steps, share, nrhs), F32),
            jax.ShapeDtypeStruct((blocks, quarter, nrhs), F32),
        ],
        compiler_params=PARAMS,
        cost_estimate=CHEAP,
        name="add_up",
    )(rhs[:, 0, 0], own, got_1, got_2, got_4, got_3)
    return solved, remaining[:, None, None]


def solution(mesh):
    in_specs = (P(None, "row", "col", None, None), P(None, "row", "col", None, None), P())
    out_specs = (P(None, "col", None), P(None, "row", "col", None, None))
    return jax.shard_map(
        on_device, mesh=mesh, in_specs=in_specs, out_specs=out_specs, check_vma=False
    )
```

```python
import functools

import jax
import jax.numpy as jnp
from jax import lax
from jax.experimental import pallas as pl
from jax.experimental.pallas import tpu as pltpu
from jax.sharding import PartitionSpec as P

AXES = ("row", "col")
F32 = jnp.float32
VMEM = pltpu.VMEM
PARAMS = pltpu.CompilerParams(vmem_limit_bytes=20 * 2**20)
CHEAP = pl.CostEstimate(flops=1000, bytes_accessed=1000, transcendentals=0)


def split(x):
    high = x.astype(jnp.bfloat16)
    return high, (x - high.astype(F32)).astype(jnp.bfloat16)


def product(a, b, transposed=False):
    dims = (((1,), (1 if transposed else 0,)), ((), ()))
    a_high, a_low = split(a)
    b_high, b_low = split(b)
    n = a.shape[0]
    both = lax.dot_general(
        jnp.concatenate([a_high, a_low], 0), b_high, dims, preferred_element_type=F32
    )
    cross = lax.dot_general(a_high, b_low, dims, preferred_element_type=F32)
    return both[:n] + (both[n:] + cross)


def position(col_count):
    return lax.axis_index("row") * col_count + lax.axis_index("col")


def turn_kernel(order, solver, col_count, own, g1, g2, g3, inverses, out, inv, sem):
    me = position(col_count)

    def joined(pieces):
        return jnp.concatenate([piece[...].T for piece in pieces], axis=1)

    @pl.when(me == solver)
    def _():
        copy = pltpu.make_async_copy(inverses.at[0], inv, sem)
        copy.start()
        right = joined((own, g1, g2, g3))
        copy.wait()
        out[...] = product(right, inv[...], True)

    for device, places in order:
        @pl.when(me == device)
        def _(places=places):
            refs = (own, g1, g2, g3)
            out[...] = joined([refs[i] for i in places])


def low_kernel(homes, col_count, out, swapped, near, la, inverses, s_a, s_b, inv, sem):
    me = position(col_count)

    def work(first, right, block):
        copy = pltpu.make_async_copy(inverses.at[1], inv, sem)
        copy.start()
        s_a[...] = first[...]
        left = right[...] - product(first[...], block[...])
        copy.wait()
        s_b[...] = product(left, inv[...], True)

    @pl.when(me == homes[0])
    def _():
        work(out, swapped, la)

    @pl.when(me == homes[1])
    def _():
        work(swapped, out, near)


def reduce_kernel(homes, col_count, s_a, s_b, lx, ly, w):
    me = position(col_count)

    @pl.when((me == homes[0]) | (me == homes[1]))
    def _():
        w[...] = product(s_a[...], lx[...]) + product(s_b[...], ly[...])


def high_kernel(homes, col_count, own, swapped, block, w_1, w_2, inverses, s, inv, sem):
    me = position(col_count)
    copies = [pltpu.make_async_copy(inverses.at[2 + i], inv.at[i], sem.at[i]) for i in range(2)]

    @pl.when(me == homes[0])
    def _():
        copies[0].start()
        right = own[...] - w_2[...]
        copies[0].wait()
        s[...] = product(right, inv[0], True)

    @pl.when(me == homes[1])
    def _():
        for copy in copies:
            copy.start()
        right = swapped[...] - w_1[...]
        copies[0].wait()
        first = product(right, inv[0], True)
        right = own[...] - w_2[...] - product(first, block[...])
        copies[1].wait()
        s[...] = product(right, inv[1], True)


def update_kernel(cfg, *refs):
    groups, row_count, share, homes, slots, blocks = cfg
    steps = len(homes)
    ways, panel, refs = refs[:8], refs[8], refs[9:]
    outs, (tiles, s, turned, sems) = refs[:2], refs[2:]
    quarter = turned.shape[0]
    row = lax.axis_index("row")
    col = lax.axis_index("col")
    member = col // groups
    group = col % groups
    columns = []
    for table in slots:
        to = functools.reduce(jnp.add, [jnp.where(member == m, p, 0) for m, p in enumerate(table)])
        columns.append(pl.ds(pl.multiple_of(to * quarter, quarter), quarter))
    copies = [
        [
            pltpu.make_async_copy(
                panel.at[r, 0, 0, :, columns[i]],
                tiles.at[r, :, pl.ds(i * quarter, quarter)],
                sems.at[2 * r + i],
            )
            for i in range(2)
        ]
        for r in range(blocks)
    ]
    for pair in copies:
        for copy in pair:
            copy.start()

    for half in range(2):
        planes = [m for m in range(steps) if m // (steps // 2) == half]

        def among(flip):
            return functools.reduce(jnp.logical_or, [
                (member == m) & (row == (r ^ flip)) & (group == g)
                for m in planes for r, g in homes[m]
            ])

        first, first_twin = among(0), among(1)
        here = functools.reduce(jnp.logical_or, [member == m for m in planes])
        same = here & (lax.rem(row, 2) == homes[planes[0]][0][0] % 2)
        other = here & (lax.rem(row, 2) != homes[planes[0]][0][0] % 2)
        roles = (
            first, same & jnp.logical_not(first), first_twin, other & jnp.logical_not(first_twin)
        )
        for way, role in zip(ways[4 * half:], roles):
            @pl.when(role)
            def _(src=way):
                s[...] = src[...]

    for r in range(blocks):
        for copy in copies[r]:
            copy.wait()
        block_id = (r * row_count + row) * groups + group
        keep = (block_id > member).astype(F32)
        full = product(s[...], tiles[r]) * keep
        for i, out in enumerate(outs):
            out[pl.ds(r * quarter, quarter), :] = full[:, i * quarter: (i + 1) * quarter]
    for i, out in enumerate(outs):
        turned[...] = s[:, columns[i]].T
        rows = pl.ds(pl.multiple_of(group * share, share), share)
        out[pl.ds(blocks * quarter, share), :] = turned[rows, :]


def join_kernel(cfg, mine, theirs, got_2, got_4, out):
    del got_2, got_4
    groups, share = cfg
    last = theirs.shape[0] - share
    member = lax.axis_index("col") // groups
    out[...] = mine[...]

    @pl.when((member == 1) | (member == 2))
    def _():
        out[:last, :] = mine[:last, :] + theirs[:last, :]
        out[pl.ds(last + share, share), :] = theirs[last:, :]


def last_kernel(groups, rhs, own, got_1, got_2, got_4, got_3, solved, out):
    blocks, quarter = rhs.shape[0], rhs.shape[1]
    last, share = blocks * quarter, solved.shape[1]
    member = lax.axis_index("col") // groups

    def finish(at, parts, joined_members=()):
        @pl.when(member == at)
        def _():
            for r in range(blocks):
                rows = pl.ds(r * quarter, quarter)
                total = functools.reduce(jnp.add, [part[rows, :] for part, _ in parts])
                if joined_members:
                    total = total + got_3[rows, :]
                out[r] = rhs[r] - total.T
            for part, k in parts:
                solved[k] = part[pl.ds(last, share), :]
            for i, k in enumerate(joined_members):
                solved[k] = got_3[pl.ds(last + i * share, share), :]

    finish(0, [(own, 0), (got_1, 1)], (2, 3))
    finish(1, [(own, 1), (got_2, 3), (got_3, 0), (got_4, 2)])
    finish(2, [(own, 2), (got_2, 0), (got_3, 3), (got_4, 1)])
    finish(3, [(own, 3), (got_1, 2)], (1, 0))


def on_device(factor, rhs, inverses):
    steps = inverses.shape[0]
    blocks = factor.shape[0]
    width = factor.shape[3]
    quarter = rhs.shape[3]
    nrhs = rhs.shape[4]
    row_count = lax.axis_size("row")
    col_count = lax.axis_size("col")
    groups = col_count // steps
    row_pos = lax.axis_index("row")
    col_pos = lax.axis_index("col")
    member = col_pos // groups
    group = col_pos % groups
    share = width // col_count
    top = steps - 1
    me = row_pos * col_count + col_pos

    def dev(row, mem, grp):
        return row * col_count + mem * groups + grp

    def line(g, mem):
        return dev(g // groups, mem, g % groups)

    low_homes = (line(0, 0), line(1, 0))
    high_homes = (line(2, top - 1), line(3, top))

    def send(x, pairs):
        onward = dict(pairs)
        for start in sorted(set(onward) - set(onward.values())):
            stop = onward[start]
            while stop in onward:
                stop = onward[stop]
            onward[stop] = start
        idle = [i for i in range(row_count * col_count) if i not in onward]
        rest = []
        for i in idle:
            twin = i + col_count if (i // col_count) % 2 == 0 else i - col_count
            if twin in idle:
                onward[i] = twin
            else:
                rest.append(i)
        rest.sort(key=lambda i: i % col_count)
        while rest:
            ring, rest = (rest, []) if len(rest) == 3 else (rest[:2], rest[2:])
            for i, j in zip(ring, ring[1:] + ring[:1]):
                onward[i] = j
        return lax.ppermute(x, AXES, sorted(onward.items()))

    def send_some(x, pairs):
        return lax.ppermute(x, AXES, pairs)

    def chosen(pairs, new, old):
        here = functools.reduce(jnp.logical_or, [me == d for _, d in pairs])
        return jnp.where(here, new, old)

    vmem = pl.BlockSpec(memory_space=VMEM)
    hbm = pl.BlockSpec(memory_space=pltpu.HBM)

    held_factor = pltpu.with_memory_space_constraint(factor, pltpu.HBM)
    held_inverses = pltpu.with_memory_space_constraint(inverses, pltpu.HBM)

    mine = rhs[0, 0, 0]
    gathered = [
        send(
            mine,
            [(line(g, j), line(g, 0)) for g in (0, 1)]
            + [(line(2, (top - 1 - j) % steps), high_homes[0]), (line(3, top - j), high_homes[1])],
        )
        for j in range(1, steps)
    ]
    near = factor[0, 0, 0]
    la = send_some(near, [(line(1, 0), low_homes[0])])
    ly = send_some(near, [(line(2, 1), low_homes[0]), (line(3, 1), low_homes[1]), (line(3, 2), high_homes[1])])

    vector = jax.ShapeDtypeStruct((nrhs, width), F32)
    one = [VMEM((width, width), F32), pltpu.SemaphoreType.DMA]
    two = [VMEM((2, width, width), F32), pltpu.SemaphoreType.DMA((2,))]
    order = ((low_homes[1], (0, 1, 2, 3)), (high_homes[0], (2, 1, 0, 3)), (high_homes[1], (3, 2, 1, 0)))
    turned = pl.pallas_call(
        functools.partial(turn_kernel, order, low_homes[0], col_count),
        in_specs=[vmem] * 4 + [hbm],
        out_specs=vmem,
        out_shape=vector,
        scratch_shapes=one,
        compiler_params=PARAMS,
        cost_estimate=CHEAP,
        name="turn",
    )(mine, *gathered, held_inverses)
    swapped = send(turned, [low_homes, low_homes[::-1], high_homes])
    later = lax.optimization_barrier((near, turned))[0]
    lx = send_some(later, [(line(2, 0), low_homes[0]), (line(3, 0), low_homes[1])])
    s_0, s_1 = pl.pallas_call(
        functools.partial(low_kernel, low_homes, col_count),
        in_specs=[vmem] * 4 + [hbm],
        out_specs=[vmem] * 2,
        out_shape=[vector] * 2,
        scratch_shapes=one,
        compiler_params=PARAMS,
        cost_estimate=CHEAP,
        name="solve_low",
    )(turned, swapped, near, la, held_inverses)
    w = pl.pallas_call(
        functools.partial(reduce_kernel, low_homes, col_count),
        in_specs=[vmem] * 4,
        out_specs=vmem,
        out_shape=vector,
        compiler_params=PARAMS,
        cost_estimate=CHEAP,
        name="reduce_low",
    )(s_0, s_1, lx, ly)
    w_1 = send(w, [(low_homes[0], high_homes[1])])
    w_2 = send(w, [(low_homes[1], high_homes[1]), (low_homes[0], high_homes[0])])
    s_high = pl.pallas_call(
        functools.partial(high_kernel, high_homes, col_count),
        in_specs=[vmem] * 5 + [hbm],
        out_specs=vmem,
        out_shape=vector,
        scratch_shapes=two,
        compiler_params=PARAMS,
        cost_estimate=CHEAP,
        name="solve_high",
    )(turned, swapped, ly, w_1, w_2, held_inverses)

    def spread(s, homes):
        have = {k: list(homes[k]) for k in homes}
        todo = {
            k: sorted(
                [
                    (r, g) for r in range(row_count) for g in range(groups)
                    if r % 2 == homes[k][0][0] % 2 and (r, g) not in homes[k]
                ],
                key=lambda spot: -(spot[0] != homes[k][0][0]) - (spot[1] != homes[k][0][1]),
            )
            for k in homes
        }
        fan = 1 if all(len(spots) > 1 for spots in homes.values()) else 3
        firsts = [(0, dev(r, k, g)) for k in homes for r, g in homes[k]]
        far = None
        while any(todo.values()):
            held = s if far is None else chosen(firsts, s, far)
            rounds = [[] for _ in range(fan)]
            for k in homes:
                spots = list(have[k])
                for pairs in rounds:
                    for a in spots:
                        if todo[k]:
                            b = todo[k].pop()
                            have[k].append(b)
                            pairs.append((dev(a[0], k, a[1]), dev(b[0], k, b[1])))
            for pairs in rounds:
                if pairs:
                    got = send(held, pairs)
                    far = got if far is None else chosen(pairs, got, far)
        twins = {
            k: [(dev(r, k, g), dev(r ^ 1, k, g)) for r, g in have[k]] for k in homes
        }
        near_twins = [pair for k in homes for pair in twins[k][: len(homes[k])]]
        far_twins = [pair for k in homes for pair in twins[k][len(homes[k]):]]
        return s, far, send(s, near_twins), send(far, far_twins)

    spots = [(g // groups, g % groups) for g in range(4)]
    homes = (tuple(spots[:2]), tuple(spots[:2]), (spots[2],), (spots[3],))
    moved = send(s_1, [(line(g, 0), line(g, 1)) for g in (0, 1)])
    s_low = jnp.where(member == 0, s_0, moved)
    ways = spread(s_low, {0: homes[0], 1: homes[1]}) + spread(s_high, {2: homes[2], 3: homes[3]})

    part, joint = [
        jax.ShapeDtypeStruct((blocks * quarter + n * share, nrhs), F32) for n in (1, 2)
    ]

    def update(name, shapes, *slots):
        return pl.pallas_call(
            functools.partial(update_kernel, (groups, row_count, share, homes, slots, blocks)),
            in_specs=[vmem] * 8 + [hbm],
            out_specs=[vmem] * 2,
            out_shape=shapes,
            scratch_shapes=[
                VMEM((blocks, width, 2 * quarter), F32),
                VMEM((nrhs, width), F32),
                VMEM((quarter, nrhs), F32),
                pltpu.SemaphoreType.DMA((2 * blocks,)),
            ],
            compiler_params=PARAMS,
            cost_estimate=CHEAP,
            name=name,
        )(*ways, held_factor)

    part_a, part_b = update("update_first", [part, part], (3, 0, 3, 0), (2, 2, 1, 1))
    own, part_c = update("update_second", [part, joint], (0, 1, 2, 3), (1, 3, 0, 2))
    across = [(r, g) for r in range(row_count) for g in range(groups)]

    def route(*hops):
        return [(dev(r, a, g), dev(r, b, g)) for a, b in hops for r, g in across]

    got_1 = send(part_a, route((3, 2), (0, 1), (1, 0), (2, 3)))
    got_4 = send(part_b, route((2, 1), (1, 2)))
    got_2 = send(part_b, route((3, 1), (1, 0), (0, 2), (2, 3)))
    joined = pl.pallas_call(
        functools.partial(join_kernel, (groups, share)),
        in_specs=[vmem] * 2 + [pl.BlockSpec(memory_space=pl.ANY)] * 2,
        out_specs=vmem,
        out_shape=joint,
        compiler_params=PARAMS,
        cost_estimate=CHEAP,
        name="join",
    )(part_c, got_1, got_2, got_4)
    got_3 = send(joined, route((3, 2), (0, 1), (2, 0), (1, 3)))

    solved, remaining = pl.pallas_call(
        functools.partial(last_kernel, groups),
        in_specs=[vmem] * 6,
        out_specs=[vmem] * 2,
        out_shape=[
            jax.ShapeDtypeStruct((steps, share, nrhs), F32),
            jax.ShapeDtypeStruct((blocks, quarter, nrhs), F32),
        ],
        compiler_params=PARAMS,
        cost_estimate=CHEAP,
        name="add_up",
    )(rhs[:, 0, 0], own, got_1, got_2, got_4, got_3)
    return solved, remaining[:, None, None]


def solution(mesh):
    in_specs = (P(None, "row", "col", None, None), P(None, "row", "col", None, None), P())
    out_specs = (P(None, "col", None), P(None, "row", "col", None, None))
    return jax.shard_map(
        on_device, mesh=mesh, in_specs=in_specs, out_specs=out_specs, check_vma=False
    )
```

```python
import functools

import jax
import jax.numpy as jnp
from jax import lax
from jax.experimental import pallas as pl
from jax.experimental.pallas import tpu as pltpu
from jax.sharding import PartitionSpec as P

AXES = ("row", "col")
F32 = jnp.float32
VMEM = pltpu.VMEM
PARAMS = pltpu.CompilerParams(vmem_limit_bytes=20 * 2**20)
CHEAP = pl.CostEstimate(flops=1000, bytes_accessed=1000, transcendentals=0)


def split(x):
    high = x.astype(jnp.bfloat16)
    return high, (x - high.astype(F32)).astype(jnp.bfloat16)


def product(a, b, transposed=False):
    dims = (((1,), (1 if transposed else 0,)), ((), ()))
    a_high, a_low = split(a)
    b_high, b_low = split(b)
    n = a.shape[0]
    both = lax.dot_general(
        jnp.concatenate([a_high, a_low], 0), b_high, dims, preferred_element_type=F32
    )
    cross = lax.dot_general(a_high, b_low, dims, preferred_element_type=F32)
    return both[:n] + (both[n:] + cross)


def position(col_count):
    return lax.axis_index("row") * col_count + lax.axis_index("col")


def turn_kernel(order, solver, col_count, own, g1, g2, g3, inverses, out, inv, sem):
    me = position(col_count)

    def joined(pieces):
        return jnp.concatenate([piece[...].T for piece in pieces], axis=1)

    @pl.when(me == solver)
    def _():
        copy = pltpu.make_async_copy(inverses.at[0], inv, sem)
        copy.start()
        right = joined((own, g1, g2, g3))
        copy.wait()
        out[...] = product(right, inv[...], True)

    for device, places in order:
        @pl.when(me == device)
        def _(places=places):
            refs = (own, g1, g2, g3)
            out[...] = joined([refs[i] for i in places])


def low_kernel(homes, col_count, out, swapped, near, la, inverses, s_a, s_b, inv, sem):
    me = position(col_count)

    def work(first, right, block):
        copy = pltpu.make_async_copy(inverses.at[1], inv, sem)
        copy.start()
        s_a[...] = first[...]
        left = right[...] - product(first[...], block[...])
        copy.wait()
        s_b[...] = product(left, inv[...], True)

    @pl.when(me == homes[0])
    def _():
        work(out, swapped, la)

    @pl.when(me == homes[1])
    def _():
        work(swapped, out, near)


def reduce_kernel(homes, col_count, s_a, s_b, lx, ly, w):
    me = position(col_count)

    @pl.when((me == homes[0]) | (me == homes[1]))
    def _():
        w[...] = product(s_a[...], lx[...]) + product(s_b[...], ly[...])


def high_kernel(homes, col_count, own, swapped, block, w_1, w_2, inverses, s, inv, sem):
    me = position(col_count)
    copies = [pltpu.make_async_copy(inverses.at[2 + i], inv.at[i], sem.at[i]) for i in range(2)]

    @pl.when(me == homes[0])
    def _():
        copies[0].start()
        right = own[...] - w_2[...]
        copies[0].wait()
        s[...] = product(right, inv[0], True)

    @pl.when(me == homes[1])
    def _():
        for copy in copies:
            copy.start()
        right = swapped[...] - w_1[...]
        copies[0].wait()
        first = product(right, inv[0], True)
        right = own[...] - w_2[...] - product(first, block[...])
        copies[1].wait()
        s[...] = product(right, inv[1], True)


def update_kernel(cfg, *refs):
    groups, row_count, share, homes, slots, blocks = cfg
    steps = len(homes)
    ways, panel, refs = refs[:8], refs[8], refs[9:]
    outs, shares, (tiles, s, turned, sems) = refs[:2], refs[2:-4], refs[-4:]
    quarter = turned.shape[0]
    row = lax.axis_index("row")
    col = lax.axis_index("col")
    member = col // groups
    group = col % groups
    columns = []
    for table in slots:
        to = functools.reduce(jnp.add, [jnp.where(member == m, p, 0) for m, p in enumerate(table)])
        columns.append(pl.ds(pl.multiple_of(to * quarter, quarter), quarter))
    copies = [
        [
            pltpu.make_async_copy(
                panel.at[r, 0, 0, :, columns[i]],
                tiles.at[r, :, pl.ds(i * quarter, quarter)],
                sems.at[2 * r + i],
            )
            for i in range(len(outs))
        ]
        for r in range(blocks)
    ]
    for pair in copies:
        for copy in pair:
            copy.start()

    for half in range(2):
        planes = [m for m in range(steps) if m // (steps // 2) == half]

        def among(flip):
            return functools.reduce(jnp.logical_or, [
                (member == m) & (row == (r ^ flip)) & (group == g)
                for m in planes for r, g in homes[m]
            ])

        first, first_twin = among(0), among(1)
        here = functools.reduce(jnp.logical_or, [member == m for m in planes])
        same = here & (lax.rem(row, 2) == homes[planes[0]][0][0] % 2)
        other = here & (lax.rem(row, 2) != homes[planes[0]][0][0] % 2)
        roles = (
            first, same & jnp.logical_not(first), first_twin, other & jnp.logical_not(first_twin)
        )
        for way, role in zip(ways[4 * half:], roles):
            @pl.when(role)
            def _(src=way):
                s[...] = src[...]

    for r in range(blocks):
        for copy in copies[r]:
            copy.wait()
        block_id = (r * row_count + row) * groups + group
        keep = (block_id > member).astype(F32)
        full = product(s[...], tiles[r]) * keep
        for i, out in enumerate(outs):
            out[pl.ds(r * quarter, quarter), :] = full[:, i * quarter: (i + 1) * quarter]
    for place, out in zip(columns, outs + shares):
        turned[...] = s[:, place].T
        rows = pl.ds(pl.multiple_of(group * share, share), share)
        first = blocks * quarter if out.shape[0] > share else 0
        out[pl.ds(first, share), :] = turned[rows, :]


def join_kernel(cfg, mine, theirs, out):
    groups, share = cfg
    last = out.shape[0] - share
    member = lax.axis_index("col") // groups

    @pl.when((member == 1) | (member == 2))
    def _():
        out[:last, :] = mine[:last, :] + theirs[:last, :]
        out[last:, :] = mine[pl.ds(last, share), :]


def last_kernel(groups, rhs, own, got_1, got_2, got_3, got_4, joined, far, solved, out):
    blocks, quarter = rhs.shape[0], rhs.shape[1]
    last, share = blocks * quarter, solved.shape[1]
    member = lax.axis_index("col") // groups

    def finish(at, *parts):
        @pl.when(member == at)
        def _():
            for r in range(blocks):
                rows = pl.ds(r * quarter, quarter)
                total = functools.reduce(jnp.add, [part[rows, :] for part, _ in parts])
                out[r] = rhs[r] - total.T
            for part, k in parts:
                solved[k] = part[pl.ds(last, share), :]
            if at in (0, 3):
                solved[3 - at] = far[...]

    finish(0, (own, 0), (got_1, 1), (joined, 2))
    finish(1, (own, 1), (got_2, 3), (got_3, 0), (got_4, 2))
    finish(2, (own, 2), (got_2, 0), (got_3, 3), (got_4, 1))
    finish(3, (own, 3), (got_1, 2), (joined, 1))


def on_device(factor, rhs, inverses):
    steps = inverses.shape[0]
    blocks = factor.shape[0]
    width = factor.shape[3]
    quarter = rhs.shape[3]
    nrhs = rhs.shape[4]
    row_count = lax.axis_size("row")
    col_count = lax.axis_size("col")
    groups = col_count // steps
    row_pos = lax.axis_index("row")
    col_pos = lax.axis_index("col")
    member = col_pos // groups
    group = col_pos % groups
    share = width // col_count
    top = steps - 1
    me = row_pos * col_count + col_pos

    def dev(row, mem, grp):
        return row * col_count + mem * groups + grp

    def line(g, mem):
        return dev(g // groups, mem, g % groups)

    low_homes = (line(0, 0), line(1, 0))
    high_homes = (line(2, top - 1), line(3, top))

    def send(x, pairs):
        def twin(i):
            return i + col_count if (i // col_count) % 2 == 0 else i - col_count

        onward = dict(pairs)
        taken = set(onward) | set(onward.values())
        for start in sorted(set(onward) - set(onward.values())):
            stop = onward[start]
            while stop in onward:
                stop = onward[stop]
            back = [twin(stop), twin(start)]
            if twin(start) == stop or taken & set(back):
                onward[stop] = start
            else:
                onward[stop], onward[back[0]], onward[back[1]] = back[0], back[1], start
                taken |= set(back)
        left = []
        for i in range(row_count * col_count):
            if i not in onward:
                if twin(i) in taken:
                    left.append(i)
                else:
                    onward[i] = twin(i)
        paired = [i for i in sorted(onward) if onward[i] == twin(i) and i not in taken]
        for i in left:
            j = min(paired, key=lambda j: (j % col_count != i % col_count, abs(j - i)))
            onward[i], onward[j] = onward[j], i
            paired.remove(j)
        return lax.ppermute(x, AXES, sorted(onward.items()))

    def send_some(x, pairs):
        return lax.ppermute(x, AXES, pairs)

    def chosen(pairs, new, old):
        here = functools.reduce(jnp.logical_or, [me == d for _, d in pairs])
        return jnp.where(here, new, old)

    vmem = pl.BlockSpec(memory_space=VMEM)
    hbm = pl.BlockSpec(memory_space=pltpu.HBM)

    held_factor = pltpu.with_memory_space_constraint(factor, pltpu.HBM)
    held_inverses = pltpu.with_memory_space_constraint(inverses, pltpu.HBM)

    mine = rhs[0, 0, 0]
    gathered = [
        send(
            mine,
            [(line(g, j), line(g, 0)) for g in (0, 1)]
            + [(line(2, (top - 1 - j) % steps), high_homes[0]), (line(3, top - j), high_homes[1])],
        )
        for j in range(1, steps)
    ]
    near = factor[0, 0, 0]
    la = send(near, [(line(1, 0), low_homes[0])])
    ly = send(near, [(line(2, 1), low_homes[0]), (line(3, 1), low_homes[1]), (line(3, 2), high_homes[1])])

    vector = jax.ShapeDtypeStruct((nrhs, width), F32)
    one = [VMEM((width, width), F32), pltpu.SemaphoreType.DMA]
    two = [VMEM((2, width, width), F32), pltpu.SemaphoreType.DMA((2,))]
    order = ((low_homes[1], (0, 1, 2, 3)), (high_homes[0], (2, 1, 0, 3)), (high_homes[1], (3, 2, 1, 0)))
    turned = pl.pallas_call(
        functools.partial(turn_kernel, order, low_homes[0], col_count),
        in_specs=[vmem] * 4 + [hbm],
        out_specs=vmem,
        out_shape=vector,
        scratch_shapes=one,
        compiler_params=PARAMS,
        cost_estimate=CHEAP,
        name="turn",
    )(mine, *gathered, held_inverses)
    swapped = send(turned, [low_homes, low_homes[::-1], high_homes])
    later = lax.optimization_barrier((near, turned))[0]
    lx = send(later, [(line(2, 0), low_homes[0]), (line(3, 0), low_homes[1])])
    s_0, s_1 = pl.pallas_call(
        functools.partial(low_kernel, low_homes, col_count),
        in_specs=[vmem] * 4 + [hbm],
        out_specs=[vmem] * 2,
        out_shape=[vector] * 2,
        scratch_shapes=one,
        compiler_params=PARAMS,
        cost_estimate=CHEAP,
        name="solve_low",
    )(turned, swapped, near, la, held_inverses)
    w = pl.pallas_call(
        functools.partial(reduce_kernel, low_homes, col_count),
        in_specs=[vmem] * 4,
        out_specs=vmem,
        out_shape=vector,
        compiler_params=PARAMS,
        cost_estimate=CHEAP,
        name="reduce_low",
    )(s_0, s_1, lx, ly)
    w_1 = send(w, [(low_homes[0], high_homes[1])])
    w_2 = send(w, [(low_homes[1], high_homes[1]), (low_homes[0], high_homes[0])])
    s_high = pl.pallas_call(
        functools.partial(high_kernel, high_homes, col_count),
        in_specs=[vmem] * 5 + [hbm],
        out_specs=vmem,
        out_shape=vector,
        scratch_shapes=two,
        compiler_params=PARAMS,
        cost_estimate=CHEAP,
        name="solve_high",
    )(turned, swapped, ly, w_1, w_2, held_inverses)

    def spread(s, homes):
        have = {k: list(homes[k]) for k in homes}
        todo = {
            k: sorted(
                [
                    (r, g) for r in range(row_count) for g in range(groups)
                    if r % 2 == homes[k][0][0] % 2 and (r, g) not in homes[k]
                ],
                key=lambda spot: -(spot[0] != homes[k][0][0]) - (spot[1] != homes[k][0][1]),
            )
            for k in homes
        }
        fan = 1 if all(len(spots) > 1 for spots in homes.values()) else 3
        firsts = [(0, dev(r, k, g)) for k in homes for r, g in homes[k]]
        far = None
        while any(todo.values()):
            held = s if far is None else chosen(firsts, s, far)
            rounds = [[] for _ in range(fan)]
            for k in homes:
                spots = list(have[k])
                for pairs in rounds:
                    for a in spots:
                        if todo[k]:
                            b = todo[k].pop()
                            have[k].append(b)
                            pairs.append((dev(a[0], k, a[1]), dev(b[0], k, b[1])))
            for pairs in rounds:
                if pairs:
                    got = send(held, pairs)
                    far = got if far is None else chosen(pairs, got, far)
        twins = {
            k: [(dev(r, k, g), dev(r ^ 1, k, g)) for r, g in have[k]] for k in homes
        }
        near_twins = [pair for k in homes for pair in twins[k][: len(homes[k])]]
        far_twins = [pair for k in homes for pair in twins[k][len(homes[k]):]]
        return s, far, send(s, near_twins), send(far, far_twins)

    spots = [(g // groups, g % groups) for g in range(4)]
    homes = (tuple(spots[:2]), tuple(spots[:2]), (spots[2],), (spots[3],))
    moved = send(s_1, [(line(g, 0), line(g, 1)) for g in (0, 1)])
    s_low = jnp.where(member == 0, s_0, moved)
    ways = spread(s_low, {0: homes[0], 1: homes[1]}) + spread(s_high, {2: homes[2], 3: homes[3]})

    far_share, part, longer = [
        jax.ShapeDtypeStruct((n, nrhs), F32)
        for n in (share, blocks * quarter + share, blocks * quarter + share + 8)
    ]

    def update(name, shapes, *slots):
        return pl.pallas_call(
            functools.partial(update_kernel, (groups, row_count, share, homes, slots, blocks)),
            in_specs=[vmem] * 8 + [hbm],
            out_specs=[vmem] * len(shapes),
            out_shape=shapes,
            scratch_shapes=[
                VMEM((blocks, width, 2 * quarter), F32),
                VMEM((nrhs, width), F32),
                VMEM((quarter, nrhs), F32),
                pltpu.SemaphoreType.DMA((2 * blocks,)),
            ],
            compiler_params=PARAMS,
            cost_estimate=CHEAP,
            name=name,
        )(*ways, held_factor)

    part_a, part_b, far = update(
        "update_first", [part, longer, far_share], (3, 0, 3, 0), (2, 2, 1, 1), (3, 0, 0, 0)
    )
    own, part_c = update("update_second", [part, longer], (0, 1, 2, 3), (1, 3, 0, 2))
    across = [(r, g) for r in range(row_count) for g in range(groups)]

    def route(*hops):
        return [(dev(r, a, g), dev(r, b, g)) for a, b in hops for r, g in across]

    got_1 = send(part_a, route((3, 2), (0, 1), (1, 0), (2, 3)))
    got_4 = send(part_b, route((2, 1), (1, 2)))
    got_2 = send(part_b, route((3, 1), (1, 0), (0, 2), (2, 3)))
    got_3 = send_some(part_c, route((3, 2), (0, 1)))
    joined = pl.pallas_call(
        functools.partial(join_kernel, (groups, share)),
        in_specs=[vmem] * 2,
        out_specs=vmem,
        out_shape=part,
        compiler_params=PARAMS,
        cost_estimate=CHEAP,
        name="join",
    )(part_c, got_1)
    joined = send_some(joined, route((2, 0), (1, 3)))
    far = send(far, route((3, 0), (0, 3), (1, 2), (2, 1)))

    solved, remaining = pl.pallas_call(
        functools.partial(last_kernel, groups),
        in_specs=[vmem] * 8,
        out_specs=[vmem] * 2,
        out_shape=[
            jax.ShapeDtypeStruct((steps, share, nrhs), F32),
            jax.ShapeDtypeStruct((blocks, quarter, nrhs), F32),
        ],
        compiler_params=PARAMS,
        cost_estimate=CHEAP,
        name="add_up",
    )(rhs[:, 0, 0], own, got_1, got_2, got_3, got_4, joined, far)
    return solved, remaining[:, None, None]


def solution(mesh):
    in_specs = (P(None, "row", "col", None, None), P(None, "row", "col", None, None), P())
    out_specs = (P(None, "col", None), P(None, "row", "col", None, None))
    return jax.shard_map(
        on_device, mesh=mesh, in_specs=in_specs, out_specs=out_specs, check_vma=False
    )
```

```python
import functools

import jax
import jax.numpy as jnp
from jax import lax
from jax.experimental import pallas as pl
from jax.experimental.pallas import tpu as pltpu
from jax.sharding import PartitionSpec as P

AXES = ("row", "col")
F32 = jnp.float32
VMEM = pltpu.VMEM
PARAMS = pltpu.CompilerParams(vmem_limit_bytes=20 * 2**20)
CHEAP = pl.CostEstimate(flops=1000, bytes_accessed=1000, transcendentals=0)


def split(x):
    high = x.astype(jnp.bfloat16)
    return high, (x - high.astype(F32)).astype(jnp.bfloat16)


def product(a, b, transposed=False):
    b_high, b_low = b if isinstance(b, tuple) else split(b)
    dims = (((1,), (1 if transposed else 0,)), ((), ()))
    a_high, a_low = split(a)
    n = a.shape[0]
    both = lax.dot_general(
        jnp.concatenate([a_high, a_low], 0), b_high, dims, preferred_element_type=F32
    )
    cross = lax.dot_general(a_high, b_low, dims, preferred_element_type=F32)
    return both[:n] + (both[n:] + cross)


def position(col_count):
    return lax.axis_index("row") * col_count + lax.axis_index("col")


def fetch_kernel(factor, rhs, near, mine, sem):
    copies = [
        pltpu.make_async_copy(rhs.at[0, 0, 0], mine, sem.at[0]),
        pltpu.make_async_copy(factor.at[0, 0, 0], near, sem.at[1]),
    ]
    for copy in copies:
        copy.start()
    for copy in copies:
        copy.wait()


def ready_kernel(solvers, col_count, inverses, high, low, inv, sem):
    me = position(col_count)
    for devices, first in zip(solvers, (0, 2)):
        @pl.when((me == devices[0]) | (me == devices[1]))
        def _(first=first):
            copies = [
                pltpu.make_async_copy(inverses.at[first + i], inv.at[i], sem.at[i]) for i in range(2)
            ]
            for copy in copies:
                copy.start()
            for i, copy in enumerate(copies):
                copy.wait()
                high[i], low[i] = split(inv[i])


def ahead_kernel(groups, table_pair, panel, high, low, tiles, sems):
    blocks, quarter = tiles.shape[0], tiles.shape[2] // 2
    copies = column_copies(groups, table_pair, panel, tiles, sems)
    for pair in copies:
        for copy in pair:
            copy.start()
    for r in range(blocks):
        for copy in copies[r]:
            copy.wait()
        high[r], low[r] = split(tiles[r])


def piece_columns(groups, table, quarter):
    member = lax.axis_index("col") // groups
    to = functools.reduce(jnp.add, [jnp.where(member == m, p, 0) for m, p in enumerate(table)])
    return pl.ds(pl.multiple_of(to * quarter, quarter), quarter)


def column_copies(groups, table_pair, panel, tiles, sems):
    quarter = tiles.shape[2] // 2
    return [
        [
            pltpu.make_async_copy(
                panel.at[r, 0, 0, :, piece_columns(groups, table, quarter)],
                tiles.at[r, :, pl.ds(i * quarter, quarter)],
                sems.at[2 * r + i],
            )
            for i, table in enumerate(table_pair)
        ]
        for r in range(tiles.shape[0])
    ]


def turn_kernel(order, solver, col_count, own, g1, g2, g3, high, low, out):
    me = position(col_count)

    def joined(pieces):
        return jnp.concatenate([piece[...].T for piece in pieces], axis=1)

    @pl.when(me == solver)
    def _():
        out[...] = product(joined((own, g1, g2, g3)), (high[0], low[0]), True)

    for device, places in order:
        @pl.when(me == device)
        def _(places=places):
            refs = (own, g1, g2, g3)
            out[...] = joined([refs[i] for i in places])


def low_kernel(homes, col_count, out, swapped, near, la, high, low, s_a, s_b):
    me = position(col_count)

    def work(first, right, block):
        s_a[...] = first[...]
        left = right[...] - product(first[...], block[...])
        s_b[...] = product(left, (high[1], low[1]), True)

    @pl.when(me == homes[0])
    def _():
        work(out, swapped, la)

    @pl.when(me == homes[1])
    def _():
        work(swapped, out, near)


def reduce_kernel(homes, col_count, s_a, s_b, lx, ly, w):
    me = position(col_count)

    @pl.when((me == homes[0]) | (me == homes[1]))
    def _():
        w[...] = product(s_a[...], lx[...]) + product(s_b[...], ly[...])


def high_kernel(homes, col_count, own, swapped, block, w_1, w_2, high, low, early_high, early_low, s):
    del early_high, early_low
    me = position(col_count)

    @pl.when(me == homes[0])
    def _():
        s[...] = product(own[...] - w_2[...], (high[0], low[0]), True)

    @pl.when(me == homes[1])
    def _():
        first = product(swapped[...] - w_1[...], (high[0], low[0]), True)
        left = own[...] - w_2[...] - product(first, block[...])
        s[...] = product(left, (high[1], low[1]), True)


def update_kernel(cfg, *refs):
    groups, row_count, share, homes, slots, blocks, early = cfg
    steps = len(homes)
    ways, refs = refs[:8], refs[8:]
    if early:
        (high, low), refs = refs[:2], refs[2:]
        s, turned = refs[-2:]
        outs, shares = refs[:2], refs[2:-2]
    else:
        panel, outs, shares, (s, turned, tiles, sems) = refs[0], refs[1:3], refs[3:-4], refs[-4:]
        copies = column_copies(groups, slots, panel, tiles, sems)
        for pair in copies:
            for copy in pair:
                copy.start()
    quarter = turned.shape[0]
    row = lax.axis_index("row")
    col = lax.axis_index("col")
    member = col // groups
    group = col % groups
    columns = [piece_columns(groups, table, quarter) for table in slots]

    for half in range(2):
        planes = [m for m in range(steps) if m // (steps // 2) == half]

        def among(flip):
            return functools.reduce(jnp.logical_or, [
                (member == m) & (row == (r ^ flip)) & (group == g)
                for m in planes for r, g in homes[m]
            ])

        first, first_twin = among(0), among(1)
        here = functools.reduce(jnp.logical_or, [member == m for m in planes])
        same = here & (lax.rem(row, 2) == homes[planes[0]][0][0] % 2)
        other = here & (lax.rem(row, 2) != homes[planes[0]][0][0] % 2)
        roles = (
            first, same & jnp.logical_not(first), first_twin, other & jnp.logical_not(first_twin)
        )
        for way, role in zip(ways[4 * half:], roles):
            @pl.when(role)
            def _(src=way):
                s[...] = src[...]

    for r in range(blocks):
        if early:
            block = (high[r], low[r])
        else:
            for copy in copies[r]:
                copy.wait()
            block = tiles[r]
        block_id = (r * row_count + row) * groups + group
        keep = (block_id > member).astype(F32)
        full = product(s[...], block) * keep
        for i, out in enumerate(outs):
            out[pl.ds(r * quarter, quarter), :] = full[:, i * quarter: (i + 1) * quarter]
    for place, out in zip(columns, outs + shares):
        turned[...] = s[:, place].T
        rows = pl.ds(pl.multiple_of(group * share, share), share)
        first = blocks * quarter if out.shape[0] > share else 0
        out[pl.ds(first, share), :] = turned[rows, :]


def join_kernel(cfg, mine, theirs, out):
    groups, share = cfg
    last = out.shape[0] - share
    member = lax.axis_index("col") // groups

    @pl.when((member == 1) | (member == 2))
    def _():
        out[:last, :] = mine[:last, :] + theirs[:last, :]
        out[last:, :] = mine[pl.ds(last, share), :]


def last_kernel(groups, rhs, own, got_1, got_2, got_3, got_4, joined, far, solved, out):
    blocks, quarter = rhs.shape[0], rhs.shape[1]
    last, share = blocks * quarter, solved.shape[1]
    member = lax.axis_index("col") // groups

    def finish(at, *parts):
        @pl.when(member == at)
        def _():
            for r in range(blocks):
                rows = pl.ds(r * quarter, quarter)
                total = functools.reduce(jnp.add, [part[rows, :] for part, _ in parts])
                out[r] = rhs[r] - total.T
            for part, k in parts:
                solved[k] = part[pl.ds(last, share), :]
            if at in (0, 3):
                solved[3 - at] = far[...]

    finish(0, (own, 0), (got_1, 1), (joined, 2))
    finish(1, (own, 1), (got_2, 3), (got_3, 0), (got_4, 2))
    finish(2, (own, 2), (got_2, 0), (got_3, 3), (got_4, 1))
    finish(3, (own, 3), (got_1, 2), (joined, 1))


def on_device(factor, rhs, inverses):
    steps = inverses.shape[0]
    blocks = factor.shape[0]
    width = factor.shape[3]
    quarter = rhs.shape[3]
    nrhs = rhs.shape[4]
    row_count = lax.axis_size("row")
    col_count = lax.axis_size("col")
    groups = col_count // steps
    row_pos = lax.axis_index("row")
    col_pos = lax.axis_index("col")
    member = col_pos // groups
    group = col_pos % groups
    share = width // col_count
    top = steps - 1
    me = row_pos * col_count + col_pos

    def dev(row, mem, grp):
        return row * col_count + mem * groups + grp

    def line(g, mem):
        return dev(g // groups, mem, g % groups)

    low_homes = (line(0, 0), line(1, 0))
    high_homes = (line(2, top - 1), line(3, top))

    def send(x, pairs):
        def twin(i):
            return i + col_count if (i // col_count) % 2 == 0 else i - col_count

        onward = dict(pairs)
        taken = set(onward) | set(onward.values())
        for start in sorted(set(onward) - set(onward.values())):
            stop = onward[start]
            while stop in onward:
                stop = onward[stop]
            back = [twin(stop), twin(start)]
            if twin(start) == stop or taken & set(back):
                onward[stop] = start
            else:
                onward[stop], onward[back[0]], onward[back[1]] = back[0], back[1], start
                taken |= set(back)
        left = []
        for i in range(row_count * col_count):
            if i not in onward:
                if twin(i) in taken:
                    left.append(i)
                else:
                    onward[i] = twin(i)
        paired = [i for i in sorted(onward) if onward[i] == twin(i) and i not in taken]
        for i in left:
            j = min(paired, key=lambda j: (j % col_count != i % col_count, abs(j - i)))
            onward[i], onward[j] = onward[j], i
            paired.remove(j)
        return lax.ppermute(x, AXES, sorted(onward.items()))

    def send_some(x, pairs):
        return lax.ppermute(x, AXES, pairs)

    def chosen(pairs, new, old):
        here = functools.reduce(jnp.logical_or, [me == d for _, d in pairs])
        return jnp.where(here, new, old)

    vmem = pl.BlockSpec(memory_space=VMEM)
    hbm = pl.BlockSpec(memory_space=pltpu.HBM)

    held_factor = pltpu.with_memory_space_constraint(factor, pltpu.HBM)
    held_inverses = pltpu.with_memory_space_constraint(inverses, pltpu.HBM)

    half = jax.ShapeDtypeStruct((2, width, width), jnp.bfloat16)
    near, mine = pl.pallas_call(
        fetch_kernel,
        in_specs=[hbm] * 2,
        out_specs=[vmem] * 2,
        out_shape=[
            jax.ShapeDtypeStruct((width, width), F32), jax.ShapeDtypeStruct((quarter, nrhs), F32)
        ],
        scratch_shapes=[pltpu.SemaphoreType.DMA((2,))],
        compiler_params=PARAMS,
        cost_estimate=CHEAP,
        name="fetch",
    )(held_factor, pltpu.with_memory_space_constraint(rhs, pltpu.HBM))
    ready = pl.pallas_call(
        functools.partial(ready_kernel, (low_homes, high_homes), col_count),
        in_specs=[hbm],
        out_specs=[vmem] * 2,
        out_shape=[half] * 2,
        scratch_shapes=[VMEM((2, width, width), F32), pltpu.SemaphoreType.DMA((2,))],
        compiler_params=PARAMS,
        cost_estimate=CHEAP,
        name="ready",
    )(held_inverses)
    gathered = [
        send(
            mine,
            [(line(g, j), line(g, 0)) for g in (0, 1)]
            + [(line(2, (top - 1 - j) % steps), high_homes[0]), (line(3, top - j), high_homes[1])],
        )
        for j in range(1, steps)
    ]
    la = send(near, [(line(1, 0), low_homes[0])])
    ly = send_some(near, [(line(2, 1), low_homes[0]), (line(3, 1), low_homes[1]), (line(3, 2), high_homes[1])])

    vector = jax.ShapeDtypeStruct((nrhs, width), F32)
    order = ((low_homes[1], (0, 1, 2, 3)), (high_homes[0], (2, 1, 0, 3)), (high_homes[1], (3, 2, 1, 0)))
    turned = pl.pallas_call(
        functools.partial(turn_kernel, order, low_homes[0], col_count),
        in_specs=[vmem] * 6,
        out_specs=vmem,
        out_shape=vector,
        compiler_params=PARAMS,
        cost_estimate=CHEAP,
        name="turn",
    )(mine, *gathered, *ready)
    swapped = send(turned, [low_homes, low_homes[::-1], high_homes])
    later = lax.optimization_barrier((near, turned))[0]
    lx = send(later, [(line(2, 0), low_homes[0]), (line(3, 0), low_homes[1])])
    s_0, s_1 = pl.pallas_call(
        functools.partial(low_kernel, low_homes, col_count),
        in_specs=[vmem] * 6,
        out_specs=[vmem] * 2,
        out_shape=[vector] * 2,
        compiler_params=PARAMS,
        cost_estimate=CHEAP,
        name="solve_low",
    )(turned, swapped, near, la, *ready)
    w = pl.pallas_call(
        functools.partial(reduce_kernel, low_homes, col_count),
        in_specs=[vmem] * 4,
        out_specs=vmem,
        out_shape=vector,
        compiler_params=PARAMS,
        cost_estimate=CHEAP,
        name="reduce_low",
    )(s_0, s_1, lx, ly)
    w_1 = send(w, [(low_homes[0], high_homes[1])])
    w_2 = send(w, [(low_homes[1], high_homes[1]), (low_homes[0], high_homes[0])])
    first_slots, second_slots = ((3, 0, 3, 0), (2, 2, 1, 1)), ((0, 1, 2, 3), (1, 3, 0, 2))
    loads = [VMEM((blocks, width, 2 * quarter), F32), pltpu.SemaphoreType.DMA((2 * blocks,))]
    early = pl.pallas_call(
        functools.partial(ahead_kernel, groups, first_slots),
        in_specs=[hbm],
        out_specs=[vmem] * 2,
        out_shape=[jax.ShapeDtypeStruct((blocks, width, 2 * quarter), jnp.bfloat16)] * 2,
        scratch_shapes=loads,
        compiler_params=PARAMS,
        cost_estimate=CHEAP,
        name="ahead",
    )(lax.optimization_barrier((held_factor, w))[0])
    s_high = pl.pallas_call(
        functools.partial(high_kernel, high_homes, col_count),
        in_specs=[vmem] * 7 + [pl.BlockSpec(memory_space=pl.ANY)] * 2,
        out_specs=vmem,
        out_shape=vector,
        compiler_params=PARAMS,
        cost_estimate=CHEAP,
        name="solve_high",
    )(turned, swapped, ly, w_1, w_2, *ready, *early)

    def spread(s, homes):
        have = {k: list(homes[k]) for k in homes}
        todo = {
            k: sorted(
                [
                    (r, g) for r in range(row_count) for g in range(groups)
                    if r % 2 == homes[k][0][0] % 2 and (r, g) not in homes[k]
                ],
                key=lambda spot: -(spot[0] != homes[k][0][0]) - (spot[1] != homes[k][0][1]),
            )
            for k in homes
        }
        fan = 1 if all(len(spots) > 1 for spots in homes.values()) else 3
        firsts = [(0, dev(r, k, g)) for k in homes for r, g in homes[k]]
        far = None
        while any(todo.values()):
            held = s if far is None else chosen(firsts, s, far)
            rounds = [[] for _ in range(fan)]
            for k in homes:
                spots = list(have[k])
                for pairs in rounds:
                    for a in spots:
                        if todo[k]:
                            b = todo[k].pop()
                            have[k].append(b)
                            pairs.append((dev(a[0], k, a[1]), dev(b[0], k, b[1])))
            for pairs in rounds:
                if pairs:
                    got = send(held, pairs)
                    far = got if far is None else chosen(pairs, got, far)
        twins = {
            k: [(dev(r, k, g), dev(r ^ 1, k, g)) for r, g in have[k]] for k in homes
        }
        near_twins = [pair for k in homes for pair in twins[k][: len(homes[k])]]
        far_twins = [pair for k in homes for pair in twins[k][len(homes[k]):]]
        return s, far, send(s, near_twins), send(far, far_twins)

    spots = [(g // groups, g % groups) for g in range(4)]
    homes = (tuple(spots[:2]), tuple(spots[:2]), (spots[2],), (spots[3],))
    moved = send(s_1, [(line(g, 0), line(g, 1)) for g in (0, 1)])
    s_low = jnp.where(member == 0, s_0, moved)
    ways = spread(s_low, {0: homes[0], 1: homes[1]}) + spread(s_high, {2: homes[2], 3: homes[3]})

    far_share, part, longer = [
        jax.ShapeDtypeStruct((n, nrhs), F32)
        for n in (share, blocks * quarter + share, blocks * quarter + share + 8)
    ]

    def update(name, shapes, slots, *block):
        cfg = (groups, row_count, share, homes, slots, blocks, len(block) == 2)
        return pl.pallas_call(
            functools.partial(update_kernel, cfg),
            in_specs=[vmem] * 8 + ([vmem] * 2 if len(block) == 2 else [hbm]),
            out_specs=[vmem] * len(shapes),
            out_shape=shapes,
            scratch_shapes=[VMEM((nrhs, width), F32), VMEM((quarter, nrhs), F32)]
            + (loads if len(block) == 1 else []),
            compiler_params=PARAMS,
            cost_estimate=CHEAP,
            name=name,
        )(*ways, *block)

    part_a, part_b, far = update(
        "update_first", [part, longer, far_share], first_slots + ((3, 0, 0, 0),), *early
    )
    own, part_c = update("update_second", [part, longer], second_slots, held_factor)
    across = [(r, g) for r in range(row_count) for g in range(groups)]

    def route(*hops):
        return [(dev(r, a, g), dev(r, b, g)) for a, b in hops for r, g in across]

    got_1 = send(part_a, route((3, 2), (0, 1), (1, 0), (2, 3)))
    got_4 = send(part_b, route((2, 1), (1, 2)))
    got_2 = send(part_b, route((3, 1), (1, 0), (0, 2), (2, 3)))
    got_3 = send_some(part_c, route((3, 2), (0, 1)))
    joined = pl.pallas_call(
        functools.partial(join_kernel, (groups, share)),
        in_specs=[vmem] * 2,
        out_specs=vmem,
        out_shape=part,
        compiler_params=PARAMS,
        cost_estimate=CHEAP,
        name="join",
    )(part_c, got_1)
    joined = send_some(joined, route((2, 0), (1, 3)))
    far = send(far, route((3, 0), (0, 3), (1, 2), (2, 1)))

    solved, remaining = pl.pallas_call(
        functools.partial(last_kernel, groups),
        in_specs=[vmem] * 8,
        out_specs=[vmem] * 2,
        out_shape=[
            jax.ShapeDtypeStruct((steps, share, nrhs), F32),
            jax.ShapeDtypeStruct((blocks, quarter, nrhs), F32),
        ],
        compiler_params=PARAMS,
        cost_estimate=CHEAP,
        name="add_up",
    )(rhs[:, 0, 0], own, got_1, got_2, got_3, got_4, joined, far)
    return solved, remaining[:, None, None]


def solution(mesh):
    in_specs = (P(None, "row", "col", None, None), P(None, "row", "col", None, None), P())
    out_specs = (P(None, "col", None), P(None, "row", "col", None, None))
    return jax.shard_map(
        on_device, mesh=mesh, in_specs=in_specs, out_specs=out_specs, check_vma=False
    )
```

```python
import functools

import jax
import jax.numpy as jnp
from jax import lax
from jax.experimental import pallas as pl
from jax.experimental.pallas import tpu as pltpu
from jax.sharding import PartitionSpec as P

AXES = ("row", "col")
F32 = jnp.float32
VMEM = pltpu.VMEM
PARAMS = pltpu.CompilerParams(vmem_limit_bytes=20 * 2**20)
CHEAP = pl.CostEstimate(flops=1000, bytes_accessed=1000, transcendentals=0)


def split(x):
    high = x.astype(jnp.bfloat16)
    return high, (x - high.astype(F32)).astype(jnp.bfloat16)


def product(a, b, transposed=False):
    b_high, b_low = b if isinstance(b, tuple) else split(b)
    dims = (((1,), (1 if transposed else 0,)), ((), ()))
    a_high, a_low = a if isinstance(a, tuple) else split(a)
    n = a_high.shape[0]
    both = lax.dot_general(
        jnp.concatenate([a_high, a_low], 0), b_high, dims, preferred_element_type=F32
    )
    cross = lax.dot_general(a_high, b_low, dims, preferred_element_type=F32)
    return both[:n] + (both[n:] + cross)


def position(col_count):
    return lax.axis_index("row") * col_count + lax.axis_index("col")


def fetch_kernel(factor, rhs, near, mine, sem):
    copies = [
        pltpu.make_async_copy(rhs.at[0, 0, 0], mine, sem.at[0]),
        pltpu.make_async_copy(factor.at[0, 0, 0], near, sem.at[1]),
    ]
    for copy in copies:
        copy.start()
    for copy in copies:
        copy.wait()


def ready_kernel(solvers, col_count, inverses, high, low, inv, sem):
    me = position(col_count)

    @pl.when((me == solvers[0]) | (me == solvers[1]))
    def _():
        copies = [pltpu.make_async_copy(inverses.at[i], inv.at[i], sem.at[i]) for i in range(2)]
        for copy in copies:
            copy.start()
        for i, copy in enumerate(copies):
            copy.wait()
            high[i], low[i] = split(inv[i])


def piece_columns(groups, table, quarter):
    member = lax.axis_index("col") // groups
    to = functools.reduce(jnp.add, [jnp.where(member == m, p, 0) for m, p in enumerate(table)])
    return pl.ds(pl.multiple_of(to * quarter, quarter), quarter)


def column_copies(groups, table_pair, panel, tiles, sems):
    quarter = tiles.shape[2] // 2
    return [
        [
            pltpu.make_async_copy(
                panel.at[r, 0, 0, :, piece_columns(groups, table, quarter)],
                tiles.at[r, :, pl.ds(i * quarter, quarter)],
                sems.at[2 * r + i],
            )
            for i, table in enumerate(table_pair)
        ]
        for r in range(tiles.shape[0])
    ]


def turn_kernel(order, solver, col_count, own, g1, g2, g3, high, low, out):
    me = position(col_count)

    def joined(pieces):
        return jnp.concatenate([piece[...].T for piece in pieces], axis=1)

    @pl.when(me == solver)
    def _():
        out[...] = product(joined((own, g1, g2, g3)), (high[0], low[0]), True)

    for device, places in order:
        @pl.when(me == device)
        def _(places=places):
            refs = (own, g1, g2, g3)
            out[...] = joined([refs[i] for i in places])


def low_kernel(homes, col_count, out, swapped, near, la, high, low, ly, s_a, s_b):
    del ly
    me = position(col_count)

    def work(first, right, block):
        s_a[...] = first[...]
        left = right[...] - product(first[...], block[...])
        s_b[...] = product(left, (high[1], low[1]), True)

    @pl.when(me == homes[0])
    def _():
        work(out, swapped, la)

    @pl.when(me == homes[1])
    def _():
        work(swapped, out, near)


def reduce_kernel(homes, col_count, s_a, s_b, lx, ly, w):
    me = position(col_count)

    @pl.when((me == homes[0]) | (me == homes[1]))
    def _():
        w[...] = product(s_a[...], lx[...]) + product(s_b[...], ly[...])


def high_kernel(homes, col_count, own, swapped, block, w_1, w_2, inverses, s, inv, sem):
    me = position(col_count)
    copies = [pltpu.make_async_copy(inverses.at[2 + i], inv.at[i], sem.at[i]) for i in range(2)]

    @pl.when(me == homes[0])
    def _():
        copies[0].start()
        right = own[...] - w_2[...]
        copies[0].wait()
        s[...] = product(right, inv[0], True)

    @pl.when(me == homes[1])
    def _():
        for copy in copies:
            copy.start()
        right = swapped[...] - w_1[...]
        copies[0].wait()
        first = product(right, inv[0], True)
        right = own[...] - w_2[...] - product(first, block[...])
        copies[1].wait()
        s[...] = product(right, inv[1], True)


def update_kernel(cfg, *refs):
    groups, row_count, share, homes, slots, blocks = cfg
    steps = len(homes)
    ways, panel, refs = refs[:8], refs[8], refs[9:]
    outs, shares, (s, turned, tiles, sems) = refs[:2], refs[2:-4], refs[-4:]
    copies = column_copies(groups, slots[:2], panel, tiles, sems)
    for pair in copies:
        for copy in pair:
            copy.start()
    quarter = turned.shape[0]
    row = lax.axis_index("row")
    col = lax.axis_index("col")
    member = col // groups
    group = col % groups
    columns = [piece_columns(groups, table, quarter) for table in slots]

    for half in range(2):
        planes = [m for m in range(steps) if m // (steps // 2) == half]

        def among(flip):
            return functools.reduce(jnp.logical_or, [
                (member == m) & (row == (r ^ flip)) & (group == g)
                for m in planes for r, g in homes[m]
            ])

        first, first_twin = among(0), among(1)
        here = functools.reduce(jnp.logical_or, [member == m for m in planes])
        same = here & (lax.rem(row, 2) == homes[planes[0]][0][0] % 2)
        other = here & (lax.rem(row, 2) != homes[planes[0]][0][0] % 2)
        roles = (
            first, same & jnp.logical_not(first), first_twin, other & jnp.logical_not(first_twin)
        )
        for way, role in zip(ways[4 * half:], roles):
            @pl.when(role)
            def _(src=way):
                s[...] = src[...]

    parts = split(s[...])
    for r in range(blocks):
        for copy in copies[r]:
            copy.wait()
        block_id = (r * row_count + row) * groups + group
        keep = (block_id > member).astype(F32)
        full = product(parts, tiles[r]) * keep
        for i, out in enumerate(outs):
            out[pl.ds(r * quarter, quarter), :] = full[:, i * quarter: (i + 1) * quarter]
    for place, out in zip(columns, outs + shares):
        turned[...] = s[:, place].T
        rows = pl.ds(pl.multiple_of(group * share, share), share)
        first = blocks * quarter if out.shape[0] > share else 0
        out[pl.ds(first, share), :] = turned[rows, :]


def join_kernel(cfg, mine, theirs, out):
    groups, share = cfg
    last = out.shape[0] - share
    member = lax.axis_index("col") // groups

    @pl.when((member == 1) | (member == 2))
    def _():
        out[:last, :] = mine[:last, :] + theirs[:last, :]
        out[last:, :] = mine[pl.ds(last, share), :]


def last_kernel(groups, rhs, own, got_1, got_2, got_3, got_4, joined, far, solved, out):
    blocks, quarter = rhs.shape[0], rhs.shape[1]
    last, share = blocks * quarter, solved.shape[1]
    member = lax.axis_index("col") // groups

    def finish(at, *parts):
        @pl.when(member == at)
        def _():
            for r in range(blocks):
                rows = pl.ds(r * quarter, quarter)
                total = functools.reduce(jnp.add, [part[rows, :] for part, _ in parts])
                out[r] = rhs[r] - total.T
            for part, k in parts:
                solved[k] = part[pl.ds(last, share), :]
            if at in (0, 3):
                solved[3 - at] = far[...]

    finish(0, (own, 0), (got_1, 1), (joined, 2))
    finish(1, (own, 1), (got_2, 3), (got_3, 0), (got_4, 2))
    finish(2, (own, 2), (got_2, 0), (got_3, 3), (got_4, 1))
    finish(3, (own, 3), (got_1, 2), (joined, 1))


def on_device(factor, rhs, inverses):
    steps = inverses.shape[0]
    blocks = factor.shape[0]
    width = factor.shape[3]
    quarter = rhs.shape[3]
    nrhs = rhs.shape[4]
    row_count = lax.axis_size("row")
    col_count = lax.axis_size("col")
    groups = col_count // steps
    row_pos = lax.axis_index("row")
    col_pos = lax.axis_index("col")
    member = col_pos // groups
    group = col_pos % groups
    share = width // col_count
    top = steps - 1
    me = row_pos * col_count + col_pos

    def dev(row, mem, grp):
        return row * col_count + mem * groups + grp

    def line(g, mem):
        return dev(g // groups, mem, g % groups)

    low_homes = (line(0, 0), line(1, 0))
    high_homes = (line(2, top - 1), line(3, top))

    def send(x, pairs):
        def twin(i):
            return i + col_count if (i // col_count) % 2 == 0 else i - col_count

        onward = dict(pairs)
        taken = set(onward) | set(onward.values())
        for start in sorted(set(onward) - set(onward.values())):
            stop = onward[start]
            while stop in onward:
                stop = onward[stop]
            back = [twin(stop), twin(start)]
            if twin(start) == stop or taken & set(back):
                onward[stop] = start
            else:
                onward[stop], onward[back[0]], onward[back[1]] = back[0], back[1], start
                taken |= set(back)
        left = []
        for i in range(row_count * col_count):
            if i not in onward:
                if twin(i) in taken:
                    left.append(i)
                else:
                    onward[i] = twin(i)
        paired = [i for i in sorted(onward) if onward[i] == twin(i) and i not in taken]
        for i in left:
            j = min(paired, key=lambda j: (j % col_count != i % col_count, abs(j - i)))
            onward[i], onward[j] = onward[j], i
            paired.remove(j)
        return lax.ppermute(x, AXES, sorted(onward.items()))

    def send_some(x, pairs):
        return lax.ppermute(x, AXES, pairs)

    def chosen(pairs, new, old):
        here = functools.reduce(jnp.logical_or, [me == d for _, d in pairs])
        return jnp.where(here, new, old)

    vmem = pl.BlockSpec(memory_space=VMEM)
    hbm = pl.BlockSpec(memory_space=pltpu.HBM)

    held_factor = pltpu.with_memory_space_constraint(factor, pltpu.HBM)
    held_inverses = pltpu.with_memory_space_constraint(inverses, pltpu.HBM)

    half = jax.ShapeDtypeStruct((2, width, width), jnp.bfloat16)
    near, mine = pl.pallas_call(
        fetch_kernel,
        in_specs=[hbm] * 2,
        out_specs=[vmem] * 2,
        out_shape=[
            jax.ShapeDtypeStruct((width, width), F32), jax.ShapeDtypeStruct((quarter, nrhs), F32)
        ],
        scratch_shapes=[pltpu.SemaphoreType.DMA((2,))],
        compiler_params=PARAMS,
        cost_estimate=CHEAP,
        name="fetch",
    )(held_factor, pltpu.with_memory_space_constraint(rhs, pltpu.HBM))
    ready = pl.pallas_call(
        functools.partial(ready_kernel, low_homes, col_count),
        in_specs=[hbm],
        out_specs=[vmem] * 2,
        out_shape=[half] * 2,
        scratch_shapes=[VMEM((2, width, width), F32), pltpu.SemaphoreType.DMA((2,))],
        compiler_params=PARAMS,
        cost_estimate=CHEAP,
        name="ready",
    )(held_inverses)
    gathered = [
        send(
            mine,
            [(line(g, j), line(g, 0)) for g in (0, 1)]
            + [(line(2, (top - 1 - j) % steps), high_homes[0]), (line(3, top - j), high_homes[1])],
        )
        for j in range(1, steps)
    ]
    la = send(near, [(line(1, 0), low_homes[0])])
    ly = send_some(near, [(line(2, 1), low_homes[0]), (line(3, 1), low_homes[1]), (line(3, 2), high_homes[1])])

    vector = jax.ShapeDtypeStruct((nrhs, width), F32)
    order = ((low_homes[1], (0, 1, 2, 3)), (high_homes[0], (2, 1, 0, 3)), (high_homes[1], (3, 2, 1, 0)))
    turned = pl.pallas_call(
        functools.partial(turn_kernel, order, low_homes[0], col_count),
        in_specs=[vmem] * 6,
        out_specs=vmem,
        out_shape=vector,
        compiler_params=PARAMS,
        cost_estimate=CHEAP,
        name="turn",
    )(mine, *gathered, *ready)
    swapped = send(turned, [low_homes, low_homes[::-1], high_homes])
    later = lax.optimization_barrier((near, turned))[0]
    lx = send(later, [(line(2, 0), low_homes[0]), (line(3, 0), low_homes[1])])
    s_0, s_1 = pl.pallas_call(
        functools.partial(low_kernel, low_homes, col_count),
        in_specs=[vmem] * 6 + [pl.BlockSpec(memory_space=pl.ANY)],
        out_specs=[vmem] * 2,
        out_shape=[vector] * 2,
        compiler_params=PARAMS,
        cost_estimate=CHEAP,
        name="solve_low",
    )(turned, swapped, near, la, *ready, ly)
    w = pl.pallas_call(
        functools.partial(reduce_kernel, low_homes, col_count),
        in_specs=[vmem] * 4,
        out_specs=vmem,
        out_shape=vector,
        compiler_params=PARAMS,
        cost_estimate=CHEAP,
        name="reduce_low",
    )(s_0, s_1, lx, ly)
    w_1 = send(w, [(low_homes[0], high_homes[1])])
    w_2 = send(w, [(low_homes[1], high_homes[1]), (low_homes[0], high_homes[0])])
    first_slots, second_slots = ((3, 0, 3, 0), (2, 2, 1, 1)), ((0, 1, 2, 3), (1, 3, 0, 2))
    s_high = pl.pallas_call(
        functools.partial(high_kernel, high_homes, col_count),
        in_specs=[vmem] * 5 + [hbm],
        out_specs=vmem,
        out_shape=vector,
        scratch_shapes=[VMEM((2, width, width), F32), pltpu.SemaphoreType.DMA((2,))],
        compiler_params=PARAMS,
        cost_estimate=CHEAP,
        name="solve_high",
    )(turned, swapped, ly, w_1, w_2, held_inverses)

    def spread(s, homes):
        have = {k: list(homes[k]) for k in homes}
        todo = {
            k: sorted(
                [
                    (r, g) for r in range(row_count) for g in range(groups)
                    if r % 2 == homes[k][0][0] % 2 and (r, g) not in homes[k]
                ],
                key=lambda spot: -(spot[0] != homes[k][0][0]) - (spot[1] != homes[k][0][1]),
            )
            for k in homes
        }
        fan = 1 if all(len(spots) > 1 for spots in homes.values()) else 3
        firsts = [(0, dev(r, k, g)) for k in homes for r, g in homes[k]]
        far = None
        while any(todo.values()):
            held = s if far is None else chosen(firsts, s, far)
            rounds = [[] for _ in range(fan)]
            for k in homes:
                spots = list(have[k])
                for pairs in rounds:
                    for a in spots:
                        if todo[k]:
                            b = todo[k].pop()
                            have[k].append(b)
                            pairs.append((dev(a[0], k, a[1]), dev(b[0], k, b[1])))
            for pairs in rounds:
                if pairs:
                    got = send(held, pairs)
                    far = got if far is None else chosen(pairs, got, far)
        twins = {
            k: [(dev(r, k, g), dev(r ^ 1, k, g)) for r, g in have[k]] for k in homes
        }
        near_twins = [pair for k in homes for pair in twins[k][: len(homes[k])]]
        far_twins = [pair for k in homes for pair in twins[k][len(homes[k]):]]
        return s, far, send(s, near_twins), send(far, far_twins)

    spots = [(g // groups, g % groups) for g in range(4)]
    homes = (tuple(spots[:2]), tuple(spots[:2]), (spots[2],), (spots[3],))
    moved = send(s_1, [(line(g, 0), line(g, 1)) for g in (0, 1)])
    s_low = jnp.where(member == 0, s_0, moved)
    ways = spread(s_low, {0: homes[0], 1: homes[1]}) + spread(s_high, {2: homes[2], 3: homes[3]})

    far_share, part, longer = [
        jax.ShapeDtypeStruct((n, nrhs), F32)
        for n in (share, blocks * quarter + share, blocks * quarter + share + 8)
    ]

    def update(name, shapes, slots):
        return pl.pallas_call(
            functools.partial(update_kernel, (groups, row_count, share, homes, slots, blocks)),
            in_specs=[vmem] * 8 + [hbm],
            out_specs=[vmem] * len(shapes),
            out_shape=shapes,
            scratch_shapes=[
                VMEM((nrhs, width), F32),
                VMEM((quarter, nrhs), F32),
                VMEM((blocks, width, 2 * quarter), F32),
                pltpu.SemaphoreType.DMA((2 * blocks,)),
            ],
            compiler_params=PARAMS,
            cost_estimate=CHEAP,
            name=name,
        )(*ways, held_factor)

    part_a, part_b, far = update(
        "update_first", [part, longer, far_share], first_slots + ((3, 0, 0, 0),)
    )
    own, part_c = update("update_second", [part, longer], second_slots)
    across = [(r, g) for r in range(row_count) for g in range(groups)]

    def route(*hops):
        return [(dev(r, a, g), dev(r, b, g)) for a, b in hops for r, g in across]

    got_1 = send(part_a, route((3, 2), (0, 1), (1, 0), (2, 3)))
    got_4 = send(part_b, route((2, 1), (1, 2)))
    got_2 = send(part_b, route((3, 1), (1, 0), (0, 2), (2, 3)))
    got_3 = send_some(part_c, route((3, 2), (0, 1)))
    joined = pl.pallas_call(
        functools.partial(join_kernel, (groups, share)),
        in_specs=[vmem] * 2,
        out_specs=vmem,
        out_shape=part,
        compiler_params=PARAMS,
        cost_estimate=CHEAP,
        name="join",
    )(part_c, got_1)
    joined = send_some(joined, route((2, 0), (1, 3)))
    far = send(far, route((3, 0), (0, 3), (1, 2), (2, 1)))

    solved, remaining = pl.pallas_call(
        functools.partial(last_kernel, groups),
        in_specs=[vmem] * 8,
        out_specs=[vmem] * 2,
        out_shape=[
            jax.ShapeDtypeStruct((steps, share, nrhs), F32),
            jax.ShapeDtypeStruct((blocks, quarter, nrhs), F32),
        ],
        compiler_params=PARAMS,
        cost_estimate=CHEAP,
        name="add_up",
    )(rhs[:, 0, 0], own, got_1, got_2, got_3, got_4, joined, far)
    return solved, remaining[:, None, None]


def solution(mesh):
    in_specs = (P(None, "row", "col", None, None), P(None, "row", "col", None, None), P())
    out_specs = (P(None, "col", None), P(None, "row", "col", None, None))
    return jax.shard_map(
        on_device, mesh=mesh, in_specs=in_specs, out_specs=out_specs, check_vma=False
    )
```

```python
import functools

import jax
import jax.numpy as jnp
from jax import lax
from jax.experimental import pallas as pl
from jax.experimental.pallas import tpu as pltpu
from jax.sharding import PartitionSpec as P

AXES = ("row", "col")
F32 = jnp.float32
VMEM = pltpu.VMEM
PARAMS = pltpu.CompilerParams(vmem_limit_bytes=20 * 2**20)
CHEAP = pl.CostEstimate(flops=1000, bytes_accessed=1000, transcendentals=0)


def split(x):
    high = x.astype(jnp.bfloat16)
    return high, (x - high.astype(F32)).astype(jnp.bfloat16)


def product(a, b, transposed=False):
    b_high, b_low = b if isinstance(b, tuple) else split(b)
    dims = (((1,), (1 if transposed else 0,)), ((), ()))
    a_high, a_low = a if isinstance(a, tuple) else split(a)
    n = a_high.shape[0]
    both = lax.dot_general(
        jnp.concatenate([a_high, a_low], 0), b_high, dims, preferred_element_type=F32
    )
    cross = lax.dot_general(a_high, b_low, dims, preferred_element_type=F32)
    return both[:n] + (both[n:] + cross)


def position(col_count):
    return lax.axis_index("row") * col_count + lax.axis_index("col")


def fetch_kernel(factor, rhs, near, mine, sem):
    copies = [
        pltpu.make_async_copy(rhs.at[0, 0, 0], mine, sem.at[0]),
        pltpu.make_async_copy(factor.at[0, 0, 0], near, sem.at[1]),
    ]
    for copy in copies:
        copy.start()
    for copy in copies:
        copy.wait()


def ready_kernel(solvers, col_count, inverses, high, low, inv, sem):
    me = position(col_count)

    @pl.when((me == solvers[0]) | (me == solvers[1]))
    def _():
        copies = [pltpu.make_async_copy(inverses.at[i], inv.at[i], sem.at[i]) for i in range(2)]
        for copy in copies:
            copy.start()
        for i, copy in enumerate(copies):
            copy.wait()
            high[i], low[i] = split(inv[i])


def piece_columns(groups, table, quarter):
    member = lax.axis_index("col") // groups
    to = functools.reduce(jnp.add, [jnp.where(member == m, p, 0) for m, p in enumerate(table)])
    return pl.ds(pl.multiple_of(to * quarter, quarter), quarter)


def column_copies(groups, table_pair, panel, tiles, sems):
    quarter = tiles.shape[2] // 2
    return [
        [
            pltpu.make_async_copy(
                panel.at[r, 0, 0, :, piece_columns(groups, table, quarter)],
                tiles.at[r, :, pl.ds(i * quarter, quarter)],
                sems.at[2 * r + i],
            )
            for i, table in enumerate(table_pair)
        ]
        for r in range(tiles.shape[0])
    ]


def turn_kernel(order, solver, col_count, own, g1, g2, g3, high, low, out):
    me = position(col_count)

    def joined(pieces):
        return jnp.concatenate([piece[...].T for piece in pieces], axis=1)

    @pl.when(me == solver)
    def _():
        out[...] = product(joined((own, g1, g2, g3)), (high[0], low[0]), True)

    for device, places in order:
        @pl.when(me == device)
        def _(places=places):
            refs = (own, g1, g2, g3)
            out[...] = joined([refs[i] for i in places])


def low_kernel(homes, col_count, out, swapped, near, la, high, low, ly, s_a, s_b):
    del ly
    me = position(col_count)

    def work(first, right, block):
        s_a[...] = first[...]
        left = right[...] - product(first[...], block[...])
        s_b[...] = product(left, (high[1], low[1]), True)

    @pl.when(me == homes[0])
    def _():
        work(out, swapped, la)

    @pl.when(me == homes[1])
    def _():
        work(swapped, out, near)


def reduce_kernel(homes, col_count, s_a, s_b, lx, ly, w):
    me = position(col_count)

    @pl.when((me == homes[0]) | (me == homes[1]))
    def _():
        w[...] = product(s_a[...], lx[...]) + product(s_b[...], ly[...])


def high_kernel(homes, col_count, own, swapped, block, w_1, w_2, inverses, s, inv, sem):
    me = position(col_count)
    copies = [pltpu.make_async_copy(inverses.at[2 + i], inv.at[i], sem.at[i]) for i in range(2)]

    @pl.when(me == homes[0])
    def _():
        copies[0].start()
        right = own[...] - w_2[...]
        copies[0].wait()
        s[...] = product(right, inv[0], True)

    @pl.when(me == homes[1])
    def _():
        for copy in copies:
            copy.start()
        right = swapped[...] - w_1[...]
        copies[0].wait()
        first = product(right, inv[0], True)
        right = own[...] - w_2[...] - product(first, block[...])
        copies[1].wait()
        s[...] = product(right, inv[1], True)


def update_kernel(cfg, *refs):
    groups, row_count, share, homes, slots, blocks = cfg
    steps = len(homes)
    ways, panel, refs = refs[:8], refs[8], refs[9:]
    outs, shares, (s, turned, tiles, sems) = refs[:2], refs[2:-4], refs[-4:]
    copies = column_copies(groups, slots[:2], panel, tiles, sems)
    for pair in copies:
        for copy in pair:
            copy.start()
    quarter = turned.shape[0]
    row = lax.axis_index("row")
    col = lax.axis_index("col")
    member = col // groups
    group = col % groups
    columns = [piece_columns(groups, table, quarter) for table in slots]

    for half in range(2):
        planes = [m for m in range(steps) if m // (steps // 2) == half]

        def among(flip):
            return functools.reduce(jnp.logical_or, [
                (member == m) & (row == (r ^ flip)) & (group == g)
                for m in planes for r, g in homes[m]
            ])

        first, first_twin = among(0), among(1)
        here = functools.reduce(jnp.logical_or, [member == m for m in planes])
        same = here & (lax.rem(row, 2) == homes[planes[0]][0][0] % 2)
        other = here & (lax.rem(row, 2) != homes[planes[0]][0][0] % 2)
        roles = (
            first, same & jnp.logical_not(first), first_twin, other & jnp.logical_not(first_twin)
        )
        for way, role in zip(ways[4 * half:], roles):
            @pl.when(role)
            def _(src=way):
                s[...] = src[...]

    parts = split(s[...])
    for r in range(blocks):
        for copy in copies[r]:
            copy.wait()
        block_id = (r * row_count + row) * groups + group
        keep = (block_id > member).astype(F32)
        full = product(parts, tiles[r]) * keep
        for i, out in enumerate(outs):
            out[pl.ds(r * quarter, quarter), :] = full[:, i * quarter: (i + 1) * quarter]
    for place, out in zip(columns, outs + shares):
        turned[...] = s[:, place].T
        rows = pl.ds(pl.multiple_of(group * share, share), share)
        first = blocks * quarter if out.shape[0] > share else 0
        out[pl.ds(first, share), :] = turned[rows, :]


def join_kernel(cfg, mine, theirs, out):
    groups, share = cfg
    last = out.shape[0] - share
    member = lax.axis_index("col") // groups

    @pl.when((member == 1) | (member == 2))
    def _():
        out[:last, :] = mine[:last, :] + theirs[:last, :]
        out[last:, :] = mine[pl.ds(last, share), :]


def last_kernel(groups, rhs, own, got_1, got_2, got_3, got_4, joined, far, solved, out):
    blocks, quarter = rhs.shape[0], rhs.shape[1]
    last, share = blocks * quarter, solved.shape[1]
    member = lax.axis_index("col") // groups

    def finish(at, *parts):
        @pl.when(member == at)
        def _():
            for r in range(blocks):
                rows = pl.ds(r * quarter, quarter)
                total = functools.reduce(jnp.add, [part[rows, :] for part, _ in parts])
                out[r] = rhs[r] - total.T
            for part, k in parts:
                solved[k] = part[pl.ds(last, share), :]
            if at in (0, 3):
                solved[3 - at] = far[...]

    finish(0, (own, 0), (got_1, 1), (joined, 2))
    finish(1, (own, 1), (got_2, 3), (got_3, 0), (got_4, 2))
    finish(2, (own, 2), (got_2, 0), (got_3, 3), (got_4, 1))
    finish(3, (own, 3), (got_1, 2), (joined, 1))


def on_device(factor, rhs, inverses):
    steps = inverses.shape[0]
    blocks = factor.shape[0]
    width = factor.shape[3]
    quarter = rhs.shape[3]
    nrhs = rhs.shape[4]
    row_count = lax.axis_size("row")
    col_count = lax.axis_size("col")
    groups = col_count // steps
    row_pos = lax.axis_index("row")
    col_pos = lax.axis_index("col")
    member = col_pos // groups
    group = col_pos % groups
    share = width // col_count
    top = steps - 1
    me = row_pos * col_count + col_pos

    def dev(row, mem, grp):
        return row * col_count + mem * groups + grp

    def line(g, mem):
        return dev(g // groups, mem, g % groups)

    low_homes = (line(0, 0), line(1, 0))
    high_homes = (line(2, top - 1), line(3, top))

    def send(x, pairs):
        def twin(i):
            return i + col_count if (i // col_count) % 2 == 0 else i - col_count

        onward = dict(pairs)
        taken = set(onward) | set(onward.values())
        for start in sorted(set(onward) - set(onward.values())):
            stop = onward[start]
            while stop in onward:
                stop = onward[stop]
            back = [twin(stop), twin(start)]
            if twin(start) == stop or taken & set(back):
                onward[stop] = start
            else:
                onward[stop], onward[back[0]], onward[back[1]] = back[0], back[1], start
                taken |= set(back)
        left = []
        for i in range(row_count * col_count):
            if i not in onward:
                if twin(i) in taken:
                    left.append(i)
                else:
                    onward[i] = twin(i)
        paired = [i for i in sorted(onward) if onward[i] == twin(i) and i not in taken]
        for i in left:
            j = min(paired, key=lambda j: (j % col_count != i % col_count, abs(j - i)))
            onward[i], onward[j] = onward[j], i
            paired.remove(j)
        return lax.ppermute(x, AXES, sorted(onward.items()))

    def send_some(x, pairs):
        return lax.ppermute(x, AXES, pairs)

    def chosen(pairs, new, old):
        here = functools.reduce(jnp.logical_or, [me == d for _, d in pairs])
        return jnp.where(here, new, old)

    vmem = pl.BlockSpec(memory_space=VMEM)
    hbm = pl.BlockSpec(memory_space=pltpu.HBM)

    held_factor = pltpu.with_memory_space_constraint(factor, pltpu.HBM)
    held_inverses = pltpu.with_memory_space_constraint(inverses, pltpu.HBM)

    half = jax.ShapeDtypeStruct((2, width, width), jnp.bfloat16)
    near, mine = pl.pallas_call(
        fetch_kernel,
        in_specs=[hbm] * 2,
        out_specs=[vmem] * 2,
        out_shape=[
            jax.ShapeDtypeStruct((width, width), F32), jax.ShapeDtypeStruct((quarter, nrhs), F32)
        ],
        scratch_shapes=[pltpu.SemaphoreType.DMA((2,))],
        compiler_params=PARAMS,
        cost_estimate=CHEAP,
        name="fetch",
    )(held_factor, pltpu.with_memory_space_constraint(rhs, pltpu.HBM))
    ready = pl.pallas_call(
        functools.partial(ready_kernel, low_homes, col_count),
        in_specs=[hbm],
        out_specs=[vmem] * 2,
        out_shape=[half] * 2,
        scratch_shapes=[VMEM((2, width, width), F32), pltpu.SemaphoreType.DMA((2,))],
        compiler_params=PARAMS,
        cost_estimate=CHEAP,
        name="ready",
    )(held_inverses)
    gathered = [
        send(
            mine,
            [(line(g, j), line(g, 0)) for g in (0, 1)]
            + [(line(2, (top - 1 - j) % steps), high_homes[0]), (line(3, top - j), high_homes[1])],
        )
        for j in range(1, steps)
    ]
    la = send(near, [(line(1, 0), low_homes[0])])
    ly = send_some(near, [(line(2, 1), low_homes[0]), (line(3, 1), low_homes[1])])

    vector = jax.ShapeDtypeStruct((nrhs, width), F32)
    order = ((low_homes[1], (0, 1, 2, 3)), (high_homes[0], (2, 1, 0, 3)), (high_homes[1], (3, 2, 1, 0)))
    turned = pl.pallas_call(
        functools.partial(turn_kernel, order, low_homes[0], col_count),
        in_specs=[vmem] * 6,
        out_specs=vmem,
        out_shape=vector,
        compiler_params=PARAMS,
        cost_estimate=CHEAP,
        name="turn",
    )(mine, *gathered, *ready)
    swapped = send(turned, [low_homes, low_homes[::-1], high_homes])
    later = lax.optimization_barrier((near, turned))[0]
    last_block = send_some(later, [(line(3, 2), high_homes[1])])
    lx = send(later, [(line(2, 0), low_homes[0]), (line(3, 0), low_homes[1])])
    s_0, s_1 = pl.pallas_call(
        functools.partial(low_kernel, low_homes, col_count),
        in_specs=[vmem] * 6 + [pl.BlockSpec(memory_space=pl.ANY)],
        out_specs=[vmem] * 2,
        out_shape=[vector] * 2,
        compiler_params=PARAMS,
        cost_estimate=CHEAP,
        name="solve_low",
    )(turned, swapped, near, la, *ready, ly)
    w = pl.pallas_call(
        functools.partial(reduce_kernel, low_homes, col_count),
        in_specs=[vmem] * 4,
        out_specs=vmem,
        out_shape=vector,
        compiler_params=PARAMS,
        cost_estimate=CHEAP,
        name="reduce_low",
    )(s_0, s_1, lx, ly)
    w_1 = send(w, [(low_homes[0], high_homes[1])])
    w_2 = send(w, [(low_homes[1], high_homes[1]), (low_homes[0], high_homes[0])])
    first_slots, second_slots = ((3, 0, 3, 0), (2, 2, 1, 1)), ((0, 1, 2, 3), (1, 3, 0, 2))
    s_high = pl.pallas_call(
        functools.partial(high_kernel, high_homes, col_count),
        in_specs=[vmem] * 5 + [hbm],
        out_specs=vmem,
        out_shape=vector,
        scratch_shapes=[VMEM((2, width, width), F32), pltpu.SemaphoreType.DMA((2,))],
        compiler_params=PARAMS,
        cost_estimate=CHEAP,
        name="solve_high",
    )(turned, swapped, last_block, w_1, w_2, held_inverses)

    def spread(s, homes):
        have = {k: list(homes[k]) for k in homes}
        todo = {
            k: sorted(
                [
                    (r, g) for r in range(row_count) for g in range(groups)
                    if r % 2 == homes[k][0][0] % 2 and (r, g) not in homes[k]
                ],
                key=lambda spot: -(spot[0] != homes[k][0][0]) - (spot[1] != homes[k][0][1]),
            )
            for k in homes
        }
        fan = 1 if all(len(spots) > 1 for spots in homes.values()) else 3
        firsts = [(0, dev(r, k, g)) for k in homes for r, g in homes[k]]
        far = None
        while any(todo.values()):
            held = s if far is None else chosen(firsts, s, far)
            rounds = [[] for _ in range(fan)]
            for k in homes:
                spots = list(have[k])
                for pairs in rounds:
                    for a in spots:
                        if todo[k]:
                            b = todo[k].pop()
                            have[k].append(b)
                            pairs.append((dev(a[0], k, a[1]), dev(b[0], k, b[1])))
            for pairs in rounds:
                if pairs:
                    got = send(held, pairs)
                    far = got if far is None else chosen(pairs, got, far)
        twins = {
            k: [(dev(r, k, g), dev(r ^ 1, k, g)) for r, g in have[k]] for k in homes
        }
        near_twins = [pair for k in homes for pair in twins[k][: len(homes[k])]]
        far_twins = [pair for k in homes for pair in twins[k][len(homes[k]):]]
        return s, far, send(s, near_twins), send(far, far_twins)

    spots = [(g // groups, g % groups) for g in range(4)]
    homes = (tuple(spots[:2]), tuple(spots[:2]), (spots[2],), (spots[3],))
    moved = send(s_1, [(line(g, 0), line(g, 1)) for g in (0, 1)])
    s_low = jnp.where(member == 0, s_0, moved)
    ways = spread(s_low, {0: homes[0], 1: homes[1]}) + spread(s_high, {2: homes[2], 3: homes[3]})

    far_share, part, longer = [
        jax.ShapeDtypeStruct((n, nrhs), F32)
        for n in (share, blocks * quarter + share, blocks * quarter + share + 8)
    ]

    def update(name, shapes, slots):
        return pl.pallas_call(
            functools.partial(update_kernel, (groups, row_count, share, homes, slots, blocks)),
            in_specs=[vmem] * 8 + [hbm],
            out_specs=[vmem] * len(shapes),
            out_shape=shapes,
            scratch_shapes=[
                VMEM((nrhs, width), F32),
                VMEM((quarter, nrhs), F32),
                VMEM((blocks, width, 2 * quarter), F32),
                pltpu.SemaphoreType.DMA((2 * blocks,)),
            ],
            compiler_params=PARAMS,
            cost_estimate=CHEAP,
            name=name,
        )(*ways, held_factor)

    part_a, part_b, far = update(
        "update_first", [part, longer, far_share], first_slots + ((3, 0, 0, 0),)
    )
    own, part_c = update("update_second", [part, longer], second_slots)
    across = [(r, g) for r in range(row_count) for g in range(groups)]

    def route(*hops):
        return [(dev(r, a, g), dev(r, b, g)) for a, b in hops for r, g in across]

    got_1 = send(part_a, route((3, 2), (0, 1), (1, 0), (2, 3)))
    got_4 = send(part_b, route((2, 1), (1, 2)))
    got_2 = send(part_b, route((3, 1), (1, 0), (0, 2), (2, 3)))
    got_3 = send_some(part_c, route((3, 2), (0, 1)))
    joined = pl.pallas_call(
        functools.partial(join_kernel, (groups, share)),
        in_specs=[vmem] * 2,
        out_specs=vmem,
        out_shape=part,
        compiler_params=PARAMS,
        cost_estimate=CHEAP,
        name="join",
    )(part_c, got_1)
    joined = send_some(joined, route((2, 0), (1, 3)))
    far = send(far, route((3, 0), (0, 3), (1, 2), (2, 1)))

    solved, remaining = pl.pallas_call(
        functools.partial(last_kernel, groups),
        in_specs=[vmem] * 8,
        out_specs=[vmem] * 2,
        out_shape=[
            jax.ShapeDtypeStruct((steps, share, nrhs), F32),
            jax.ShapeDtypeStruct((blocks, quarter, nrhs), F32),
        ],
        compiler_params=PARAMS,
        cost_estimate=CHEAP,
        name="add_up",
    )(rhs[:, 0, 0], own, got_1, got_2, got_3, got_4, joined, far)
    return solved, remaining[:, None, None]


def solution(mesh):
    in_specs = (P(None, "row", "col", None, None), P(None, "row", "col", None, None), P())
    out_specs = (P(None, "col", None), P(None, "row", "col", None, None))
    return jax.shard_map(
        on_device, mesh=mesh, in_specs=in_specs, out_specs=out_specs, check_vma=False
    )
```

```python
import functools

import jax
import jax.numpy as jnp
from jax import lax
from jax.experimental import pallas as pl
from jax.experimental.pallas import tpu as pltpu
from jax.sharding import PartitionSpec as P

AXES = ("row", "col")
F32 = jnp.float32
VMEM = pltpu.VMEM
PARAMS = pltpu.CompilerParams(vmem_limit_bytes=12 * 2**20)
CHEAP = pl.CostEstimate(flops=1000, bytes_accessed=1000, transcendentals=0)


def split(x):
    high = x.astype(jnp.bfloat16)
    return high, (x - high.astype(F32)).astype(jnp.bfloat16)


def product(a, b, transposed=False):
    b_high, b_low = b if isinstance(b, tuple) else split(b)
    dims = (((1,), (1 if transposed else 0,)), ((), ()))
    a_high, a_low = a if isinstance(a, tuple) else split(a)
    n = a_high.shape[0]
    both = lax.dot_general(
        jnp.concatenate([a_high, a_low], 0), b_high, dims, preferred_element_type=F32
    )
    cross = lax.dot_general(a_high, b_low, dims, preferred_element_type=F32)
    return both[:n] + (both[n:] + cross)


def position(col_count):
    return lax.axis_index("row") * col_count + lax.axis_index("col")


def fetch_kernel(factor, rhs, near, mine, sem):
    copies = [
        pltpu.make_async_copy(rhs.at[0, 0, 0], mine, sem.at[0]),
        pltpu.make_async_copy(factor.at[0, 0, 0], near, sem.at[1]),
    ]
    for copy in copies:
        copy.start()
    for copy in copies:
        copy.wait()


def ready_kernel(solvers, col_count, inverses, high, low, inv, sem):
    me = position(col_count)

    @pl.when((me == solvers[0]) | (me == solvers[1]))
    def _():
        copies = [pltpu.make_async_copy(inverses.at[i], inv.at[i], sem.at[i]) for i in range(2)]
        for copy in copies:
            copy.start()
        for i, copy in enumerate(copies):
            copy.wait()
            high[i], low[i] = split(inv[i])


def piece_columns(groups, table, quarter):
    member = lax.axis_index("col") // groups
    to = functools.reduce(jnp.add, [jnp.where(member == m, p, 0) for m, p in enumerate(table)])
    return pl.ds(pl.multiple_of(to * quarter, quarter), quarter)


def column_copies(groups, table_pair, panel, tiles, sems):
    quarter = tiles.shape[2] // 2
    return [
        [
            pltpu.make_async_copy(
                panel.at[r, 0, 0, :, piece_columns(groups, table, quarter)],
                tiles.at[r, :, pl.ds(i * quarter, quarter)],
                sems.at[2 * r + i],
            )
            for i, table in enumerate(table_pair)
        ]
        for r in range(tiles.shape[0])
    ]


def turn_kernel(order, solver, col_count, own, g1, g2, g3, high, low, out):
    me = position(col_count)

    def joined(pieces):
        return jnp.concatenate([piece[...].T for piece in pieces], axis=1)

    @pl.when(me == solver)
    def _():
        out[...] = product(joined((own, g1, g2, g3)), (high[0], low[0]), True)

    for device, places in order:
        @pl.when(me == device)
        def _(places=places):
            refs = (own, g1, g2, g3)
            out[...] = joined([refs[i] for i in places])


def low_kernel(homes, col_count, out, swapped, near, la, high, low, ly, s_a, s_b):
    del ly
    me = position(col_count)

    def work(first, right, block):
        s_a[...] = first[...]
        left = right[...] - product(first[...], block[...])
        s_b[...] = product(left, (high[1], low[1]), True)

    @pl.when(me == homes[0])
    def _():
        work(out, swapped, la)

    @pl.when(me == homes[1])
    def _():
        work(swapped, out, near)


def reduce_kernel(homes, col_count, s_a, s_b, lx, ly, w, block, sem):
    me = position(col_count)

    @pl.when((me == homes[0]) | (me == homes[1]))
    def _():
        copies = [pltpu.make_async_copy(ref, block.at[i], sem.at[i]) for i, ref in enumerate((ly, lx))]
        for copy in copies:
            copy.start()
        copies[0].wait()
        later = product(s_b[...], block[0])
        copies[1].wait()
        w[...] = product(s_a[...], block[1]) + later


def high_kernel(homes, col_count, own, swapped, w_1, w_2, inverses, last_block, s, inv, block, sem):
    me = position(col_count)
    copies = [pltpu.make_async_copy(inverses.at[2 + i], inv.at[i], sem.at[i]) for i in range(2)]
    copies.append(pltpu.make_async_copy(last_block, block, sem.at[2]))

    @pl.when(me == homes[0])
    def _():
        copies[0].start()
        right = own[...] - w_2[...]
        copies[0].wait()
        s[...] = product(right, inv[0], True)

    @pl.when(me == homes[1])
    def _():
        for copy in copies:
            copy.start()
        right = swapped[...] - w_1[...]
        copies[0].wait()
        first = product(right, inv[0], True)
        copies[2].wait()
        right = own[...] - w_2[...] - product(first, block[...])
        copies[1].wait()
        s[...] = product(right, inv[1], True)


def update_kernel(cfg, *refs):
    groups, row_count, share, homes, slots, blocks = cfg
    steps = len(homes)
    ways, panel, refs = refs[:8], refs[8], refs[9:]
    outs, shares, (s, turned, tiles, sems) = refs[:2], refs[2:-4], refs[-4:]
    copies = column_copies(groups, slots[:2], panel, tiles, sems)
    for pair in copies:
        for copy in pair:
            copy.start()
    quarter = turned.shape[0]
    row = lax.axis_index("row")
    col = lax.axis_index("col")
    member = col // groups
    group = col % groups
    columns = [piece_columns(groups, table, quarter) for table in slots]

    for half in range(2):
        planes = [m for m in range(steps) if m // (steps // 2) == half]

        def among(flip):
            return functools.reduce(jnp.logical_or, [
                (member == m) & (row == (r ^ flip)) & (group == g)
                for m in planes for r, g in homes[m]
            ])

        first, first_twin = among(0), among(1)
        here = functools.reduce(jnp.logical_or, [member == m for m in planes])
        same = here & (lax.rem(row, 2) == homes[planes[0]][0][0] % 2)
        other = here & (lax.rem(row, 2) != homes[planes[0]][0][0] % 2)
        roles = (
            first, same & jnp.logical_not(first), first_twin, other & jnp.logical_not(first_twin)
        )
        for way, role in zip(ways[4 * half:], roles):
            @pl.when(role)
            def _(src=way):
                s[...] = src[...]

    parts = split(s[...])
    for r in range(blocks):
        for copy in copies[r]:
            copy.wait()
        block_id = (r * row_count + row) * groups + group
        keep = (block_id > member).astype(F32)
        full = product(parts, tiles[r]) * keep
        for i, out in enumerate(outs):
            out[pl.ds(r * quarter, quarter), :] = full[:, i * quarter: (i + 1) * quarter]
    for place, out in zip(columns, outs + shares):
        turned[...] = s[:, place].T
        rows = pl.ds(pl.multiple_of(group * share, share), share)
        first = blocks * quarter if out.shape[0] > share else 0
        out[pl.ds(first, share), :] = turned[rows, :]


def join_kernel(cfg, mine, theirs, out):
    groups, share = cfg
    last = out.shape[0] - share
    member = lax.axis_index("col") // groups

    @pl.when((member == 1) | (member == 2))
    def _():
        out[:last, :] = mine[:last, :] + theirs[:last, :]
        out[last:, :] = mine[pl.ds(last, share), :]


def last_kernel(groups, rhs, own, got_1, got_2, got_3, got_4, joined, far, solved, out):
    blocks, quarter = rhs.shape[0], rhs.shape[1]
    last, share = blocks * quarter, solved.shape[1]
    member = lax.axis_index("col") // groups

    def finish(at, *parts):
        @pl.when(member == at)
        def _():
            for r in range(blocks):
                rows = pl.ds(r * quarter, quarter)
                total = functools.reduce(jnp.add, [part[rows, :] for part, _ in parts])
                out[r] = rhs[r] - total.T
            for part, k in parts:
                solved[k] = part[pl.ds(last, share), :]
            if at in (0, 3):
                solved[3 - at] = far[...]

    finish(0, (own, 0), (got_1, 1), (joined, 2))
    finish(1, (own, 1), (got_2, 3), (got_3, 0), (got_4, 2))
    finish(2, (own, 2), (got_2, 0), (got_3, 3), (got_4, 1))
    finish(3, (own, 3), (got_1, 2), (joined, 1))


def on_device(factor, rhs, inverses):
    steps = inverses.shape[0]
    blocks = factor.shape[0]
    width = factor.shape[3]
    quarter = rhs.shape[3]
    nrhs = rhs.shape[4]
    row_count = lax.axis_size("row")
    col_count = lax.axis_size("col")
    groups = col_count // steps
    row_pos = lax.axis_index("row")
    col_pos = lax.axis_index("col")
    member = col_pos // groups
    group = col_pos % groups
    share = width // col_count
    top = steps - 1
    me = row_pos * col_count + col_pos

    def dev(row, mem, grp):
        return row * col_count + mem * groups + grp

    def line(g, mem):
        return dev(g // groups, mem, g % groups)

    low_homes = (line(0, 0), line(1, 0))
    high_homes = (line(2, top - 1), line(3, top))

    def send(x, pairs):
        def twin(i):
            return i + col_count if (i // col_count) % 2 == 0 else i - col_count

        onward = dict(pairs)
        taken = set(onward) | set(onward.values())
        for start in sorted(set(onward) - set(onward.values())):
            stop = onward[start]
            while stop in onward:
                stop = onward[stop]
            back = [twin(stop), twin(start)]
            if twin(start) == stop or taken & set(back):
                onward[stop] = start
            else:
                onward[stop], onward[back[0]], onward[back[1]] = back[0], back[1], start
                taken |= set(back)
        left = []
        for i in range(row_count * col_count):
            if i not in onward:
                if twin(i) in taken:
                    left.append(i)
                else:
                    onward[i] = twin(i)
        paired = [i for i in sorted(onward) if onward[i] == twin(i) and i not in taken]
        for i in left:
            j = min(paired, key=lambda j: (j % col_count != i % col_count, abs(j - i)))
            onward[i], onward[j] = onward[j], i
            paired.remove(j)
        return lax.ppermute(x, AXES, sorted(onward.items()))

    def send_some(x, pairs):
        return lax.ppermute(x, AXES, pairs)

    def chosen(pairs, new, old):
        here = functools.reduce(jnp.logical_or, [me == d for _, d in pairs])
        return jnp.where(here, new, old)

    vmem = pl.BlockSpec(memory_space=VMEM)
    hbm = pl.BlockSpec(memory_space=pltpu.HBM)

    held_factor = pltpu.with_memory_space_constraint(factor, pltpu.HBM)
    held_inverses = pltpu.with_memory_space_constraint(inverses, pltpu.HBM)

    half = jax.ShapeDtypeStruct((2, width, width), jnp.bfloat16)
    near, mine = pl.pallas_call(
        fetch_kernel,
        in_specs=[hbm] * 2,
        out_specs=[vmem] * 2,
        out_shape=[
            jax.ShapeDtypeStruct((width, width), F32), jax.ShapeDtypeStruct((quarter, nrhs), F32)
        ],
        scratch_shapes=[pltpu.SemaphoreType.DMA((2,))],
        compiler_params=PARAMS,
        cost_estimate=CHEAP,
        name="fetch",
    )(held_factor, pltpu.with_memory_space_constraint(rhs, pltpu.HBM))
    ready = pl.pallas_call(
        functools.partial(ready_kernel, low_homes, col_count),
        in_specs=[hbm],
        out_specs=[vmem] * 2,
        out_shape=[half] * 2,
        scratch_shapes=[VMEM((2, width, width), F32), pltpu.SemaphoreType.DMA((2,))],
        compiler_params=PARAMS,
        cost_estimate=CHEAP,
        name="ready",
    )(held_inverses)
    gathered = [
        send(
            mine,
            [(line(g, j), line(g, 0)) for g in (0, 1)]
            + [(line(2, (top - 1 - j) % steps), high_homes[0]), (line(3, top - j), high_homes[1])],
        )
        for j in range(1, steps)
    ]
    la = send(near, [(line(1, 0), low_homes[0])])
    ly = send_some(near, [(line(2, 1), low_homes[0]), (line(3, 1), low_homes[1])])

    vector = jax.ShapeDtypeStruct((nrhs, width), F32)
    order = ((low_homes[1], (0, 1, 2, 3)), (high_homes[0], (2, 1, 0, 3)), (high_homes[1], (3, 2, 1, 0)))
    turned = pl.pallas_call(
        functools.partial(turn_kernel, order, low_homes[0], col_count),
        in_specs=[vmem] * 6,
        out_specs=vmem,
        out_shape=vector,
        compiler_params=PARAMS,
        cost_estimate=CHEAP,
        name="turn",
    )(mine, *gathered, *ready)
    swapped = send(turned, [low_homes, low_homes[::-1], high_homes])
    later = lax.optimization_barrier((near, turned))[0]
    last_block = send_some(later, [(line(3, 2), high_homes[1])])
    lx = send(later, [(line(2, 0), low_homes[0]), (line(3, 0), low_homes[1])])
    s_0, s_1 = pl.pallas_call(
        functools.partial(low_kernel, low_homes, col_count),
        in_specs=[vmem] * 6 + [pl.BlockSpec(memory_space=pl.ANY)],
        out_specs=[vmem] * 2,
        out_shape=[vector] * 2,
        compiler_params=PARAMS,
        cost_estimate=CHEAP,
        name="solve_low",
    )(turned, swapped, near, la, *ready, ly)
    w = pl.pallas_call(
        functools.partial(reduce_kernel, low_homes, col_count),
        in_specs=[vmem] * 2 + [pl.BlockSpec(memory_space=pl.ANY)] * 2,
        out_specs=vmem,
        out_shape=vector,
        scratch_shapes=[VMEM((2, width, width), F32), pltpu.SemaphoreType.DMA((2,))],
        compiler_params=PARAMS,
        cost_estimate=CHEAP,
        name="reduce_low",
    )(s_0, s_1, lx, ly)
    w_1 = send(w, [(low_homes[0], high_homes[1])])
    w_2 = send(w, [(low_homes[1], high_homes[1]), (low_homes[0], high_homes[0])])
    first_slots, second_slots = ((3, 0, 3, 0), (2, 2, 1, 1)), ((0, 1, 2, 3), (1, 3, 0, 2))
    s_high = pl.pallas_call(
        functools.partial(high_kernel, high_homes, col_count),
        in_specs=[vmem] * 4 + [hbm, pl.BlockSpec(memory_space=pl.ANY)],
        out_specs=vmem,
        out_shape=vector,
        scratch_shapes=[
            VMEM((2, width, width), F32), VMEM((width, width), F32), pltpu.SemaphoreType.DMA((3,))
        ],
        compiler_params=PARAMS,
        cost_estimate=CHEAP,
        name="solve_high",
    )(turned, swapped, w_1, w_2, held_inverses, last_block)

    def spread(s, homes):
        have = {k: list(homes[k]) for k in homes}
        todo = {
            k: sorted(
                [
                    (r, g) for r in range(row_count) for g in range(groups)
                    if r % 2 == homes[k][0][0] % 2 and (r, g) not in homes[k]
                ],
                key=lambda spot: -(spot[0] != homes[k][0][0]) - (spot[1] != homes[k][0][1]),
            )
            for k in homes
        }
        fan = 1 if all(len(spots) > 1 for spots in homes.values()) else 3
        firsts = [(0, dev(r, k, g)) for k in homes for r, g in homes[k]]
        far = None
        while any(todo.values()):
            held = s if far is None else chosen(firsts, s, far)
            rounds = [[] for _ in range(fan)]
            for k in homes:
                spots = list(have[k])
                for pairs in rounds:
                    for a in spots:
                        if todo[k]:
                            b = todo[k].pop()
                            have[k].append(b)
                            pairs.append((dev(a[0], k, a[1]), dev(b[0], k, b[1])))
            for pairs in rounds:
                if pairs:
                    got = send(held, pairs)
                    far = got if far is None else chosen(pairs, got, far)
        twins = {
            k: [(dev(r, k, g), dev(r ^ 1, k, g)) for r, g in have[k]] for k in homes
        }
        near_twins = [pair for k in homes for pair in twins[k][: len(homes[k])]]
        far_twins = [pair for k in homes for pair in twins[k][len(homes[k]):]]
        return s, far, send(s, near_twins), send(far, far_twins)

    spots = [(g // groups, g % groups) for g in range(4)]
    homes = (tuple(spots[:2]), tuple(spots[:2]), (spots[2],), (spots[3],))
    moved = send(s_1, [(line(g, 0), line(g, 1)) for g in (0, 1)])
    s_low = jnp.where(member == 0, s_0, moved)
    ways = spread(s_low, {0: homes[0], 1: homes[1]}) + spread(s_high, {2: homes[2], 3: homes[3]})

    far_share, part, longer = [
        jax.ShapeDtypeStruct((n, nrhs), F32)
        for n in (share, blocks * quarter + share, blocks * quarter + share + 8)
    ]

    def update(name, shapes, slots):
        return pl.pallas_call(
            functools.partial(update_kernel, (groups, row_count, share, homes, slots, blocks)),
            in_specs=[vmem] * 8 + [hbm],
            out_specs=[vmem] * len(shapes),
            out_shape=shapes,
            scratch_shapes=[
                VMEM((nrhs, width), F32),
                VMEM((quarter, nrhs), F32),
                VMEM((blocks, width, 2 * quarter), F32),
                pltpu.SemaphoreType.DMA((2 * blocks,)),
            ],
            compiler_params=PARAMS,
            cost_estimate=CHEAP,
            name=name,
        )(*ways, held_factor)

    part_a, part_b, far = update(
        "update_first", [part, longer, far_share], first_slots + ((3, 0, 0, 0),)
    )
    own, part_c = update("update_second", [part, longer], second_slots)
    across = [(r, g) for r in range(row_count) for g in range(groups)]

    def route(*hops):
        return [(dev(r, a, g), dev(r, b, g)) for a, b in hops for r, g in across]

    got_1 = send(part_a, route((3, 2), (0, 1), (1, 0), (2, 3)))
    got_4 = send(part_b, route((2, 1), (1, 2)))
    got_2 = send(part_b, route((3, 1), (1, 0), (0, 2), (2, 3)))
    got_3 = send_some(part_c, route((3, 2), (0, 1)))
    joined = pl.pallas_call(
        functools.partial(join_kernel, (groups, share)),
        in_specs=[vmem] * 2,
        out_specs=vmem,
        out_shape=part,
        compiler_params=PARAMS,
        cost_estimate=CHEAP,
        name="join",
    )(part_c, got_1)
    joined = send_some(joined, route((2, 0), (1, 3)))
    far = send(far, route((3, 0), (0, 3), (1, 2), (2, 1)))

    solved, remaining = pl.pallas_call(
        functools.partial(last_kernel, groups),
        in_specs=[vmem] * 8,
        out_specs=[vmem] * 2,
        out_shape=[
            jax.ShapeDtypeStruct((steps, share, nrhs), F32),
            jax.ShapeDtypeStruct((blocks, quarter, nrhs), F32),
        ],
        compiler_params=PARAMS,
        cost_estimate=CHEAP,
        name="add_up",
    )(rhs[:, 0, 0], own, got_1, got_2, got_3, got_4, joined, far)
    return solved, remaining[:, None, None]


def solution(mesh):
    in_specs = (P(None, "row", "col", None, None), P(None, "row", "col", None, None), P())
    out_specs = (P(None, "col", None), P(None, "row", "col", None, None))
    return jax.shard_map(
        on_device, mesh=mesh, in_specs=in_specs, out_specs=out_specs, check_vma=False
    )
```

```python
import functools

import jax
import jax.numpy as jnp
from jax import lax
from jax.experimental import pallas as pl
from jax.experimental.pallas import tpu as pltpu
from jax.sharding import PartitionSpec as P

AXES = ("row", "col")
F32 = jnp.float32
VMEM = pltpu.VMEM
PARAMS = pltpu.CompilerParams(vmem_limit_bytes=12 * 2**20)
CHEAP = pl.CostEstimate(flops=1000, bytes_accessed=1000, transcendentals=0)


def split(x):
    high = x.astype(jnp.bfloat16)
    return high, (x - high.astype(F32)).astype(jnp.bfloat16)


def product(a, b, transposed=False):
    b_high, b_low = b if isinstance(b, tuple) else split(b)
    dims = (((1,), (1 if transposed else 0,)), ((), ()))
    a_high, a_low = a if isinstance(a, tuple) else split(a)
    n = a_high.shape[0]
    both = lax.dot_general(
        jnp.concatenate([a_high, a_low], 0), b_high, dims, preferred_element_type=F32
    )
    cross = lax.dot_general(a_high, b_low, dims, preferred_element_type=F32)
    return both[:n] + (both[n:] + cross)


def position(col_count):
    return lax.axis_index("row") * col_count + lax.axis_index("col")


def fetch_kernel(factor, rhs, near, mine, sem):
    copies = [
        pltpu.make_async_copy(rhs.at[0, 0, 0], mine, sem.at[0]),
        pltpu.make_async_copy(factor.at[0, 0, 0], near, sem.at[1]),
    ]
    for copy in copies:
        copy.start()
    for copy in copies:
        copy.wait()


def ready_kernel(solvers, col_count, inverses, high, low, inv, sem):
    me = position(col_count)

    @pl.when((me == solvers[0]) | (me == solvers[1]))
    def _():
        copies = [pltpu.make_async_copy(inverses.at[i], inv.at[i], sem.at[i]) for i in range(2)]
        for copy in copies:
            copy.start()
        for i, copy in enumerate(copies):
            copy.wait()
            high[i], low[i] = split(inv[i])


def piece_columns(groups, table, quarter):
    member = lax.axis_index("col") // groups
    to = functools.reduce(jnp.add, [jnp.where(member == m, p, 0) for m, p in enumerate(table)])
    return pl.ds(pl.multiple_of(to * quarter, quarter), quarter)


def column_copies(groups, table_pair, panel, tiles, sems):
    quarter = tiles.shape[2] // 2
    return [
        [
            pltpu.make_async_copy(
                panel.at[r, 0, 0, :, piece_columns(groups, table, quarter)],
                tiles.at[r, :, pl.ds(i * quarter, quarter)],
                sems.at[2 * r + i],
            )
            for i, table in enumerate(table_pair)
        ]
        for r in range(tiles.shape[0])
    ]


def turn_kernel(order, solver, col_count, own, g1, g2, g3, high, low, out):
    me = position(col_count)

    def joined(pieces):
        return jnp.concatenate([piece[...].T for piece in pieces], axis=1)

    @pl.when(me == solver)
    def _():
        out[...] = product(joined((own, g1, g2, g3)), (high[0], low[0]), True)

    for device, places in order:
        @pl.when(me == device)
        def _(places=places):
            refs = (own, g1, g2, g3)
            out[...] = joined([refs[i] for i in places])


def low_kernel(homes, col_count, out, swapped, near, la, high, low, ly, s_a, s_b):
    del ly
    me = position(col_count)

    def work(first, right, block):
        s_a[...] = first[...]
        left = right[...] - product(first[...], block[...])
        s_b[...] = product(left, (high[1], low[1]), True)

    @pl.when(me == homes[0])
    def _():
        work(out, swapped, la)

    @pl.when(me == homes[1])
    def _():
        work(swapped, out, near)


def reduce_kernel(homes, col_count, s_a, s_b, lx, ly, w, block, sem):
    me = position(col_count)

    @pl.when((me == homes[0]) | (me == homes[1]))
    def _():
        copies = [pltpu.make_async_copy(ref, block.at[i], sem.at[i]) for i, ref in enumerate((ly, lx))]
        for copy in copies:
            copy.start()
        copies[0].wait()
        later = product(s_b[...], block[0])
        copies[1].wait()
        w[...] = product(s_a[...], block[1]) + later


def high_kernel(homes, col_count, own, swapped, w_1, w_2, inverses, last_block, s, inv, block, sem):
    me = position(col_count)
    copies = [pltpu.make_async_copy(inverses.at[2 + i], inv.at[i], sem.at[i]) for i in range(2)]
    copies.append(pltpu.make_async_copy(last_block, block, sem.at[2]))

    @pl.when(me == homes[0])
    def _():
        copies[0].start()
        right = own[...] - w_2[...]
        copies[0].wait()
        s[...] = product(right, inv[0], True)

    @pl.when(me == homes[1])
    def _():
        for copy in copies:
            copy.start()
        right = swapped[...] - w_1[...]
        copies[0].wait()
        first = product(right, inv[0], True)
        copies[2].wait()
        right = own[...] - w_2[...] - product(first, block[...])
        copies[1].wait()
        s[...] = product(right, inv[1], True)


def update_kernel(cfg, *refs):
    groups, row_count, share, homes, slots, blocks = cfg
    steps = len(homes)
    ways, panel, refs = refs[:8], refs[8], refs[9:]
    outs, shares, (s, turned, tiles, sems) = refs[:2], refs[2:-4], refs[-4:]
    copies = column_copies(groups, slots[:2], panel, tiles, sems)
    for pair in copies:
        for copy in pair:
            copy.start()
    quarter = turned.shape[0]
    row = lax.axis_index("row")
    col = lax.axis_index("col")
    member = col // groups
    group = col % groups
    columns = [piece_columns(groups, table, quarter) for table in slots]

    for half in range(2):
        planes = [m for m in range(steps) if m // (steps // 2) == half]

        def among(flip):
            return functools.reduce(jnp.logical_or, [
                (member == m) & (row == (r ^ flip)) & (group == g)
                for m in planes for r, g in homes[m]
            ])

        first, first_twin = among(0), among(1)
        here = functools.reduce(jnp.logical_or, [member == m for m in planes])
        same = here & (lax.rem(row, 2) == homes[planes[0]][0][0] % 2)
        other = here & (lax.rem(row, 2) != homes[planes[0]][0][0] % 2)
        roles = (
            first, same & jnp.logical_not(first), first_twin, other & jnp.logical_not(first_twin)
        )
        for way, role in zip(ways[4 * half:], roles):
            @pl.when(role)
            def _(src=way):
                s[...] = src[...]

    parts = split(s[...])
    for r in range(blocks):
        for copy in copies[r]:
            copy.wait()
        block_id = (r * row_count + row) * groups + group
        keep = (block_id > member).astype(F32)
        full = product(parts, tiles[r]) * keep
        for i, out in enumerate(outs):
            out[pl.ds(r * quarter, quarter), :] = full[:, i * quarter: (i + 1) * quarter]
    for place, out in zip(columns, outs + shares):
        turned[...] = s[:, place].T
        rows = pl.ds(pl.multiple_of(group * share, share), share)
        first = blocks * quarter if out.shape[0] > share else 0
        out[pl.ds(first, share), :] = turned[rows, :]


def join_kernel(cfg, mine, theirs, out):
    groups, share = cfg
    last = out.shape[0] - share
    member = lax.axis_index("col") // groups

    @pl.when((member == 1) | (member == 2))
    def _():
        out[:last, :] = mine[:last, :] + theirs[:last, :]
        out[last:, :] = mine[pl.ds(last, share), :]


def last_kernel(groups, rhs, own, got_1, got_2, got_3, got_4, joined, far, solved, out):
    blocks, quarter = rhs.shape[0], rhs.shape[1]
    last, share = blocks * quarter, solved.shape[1]
    member = lax.axis_index("col") // groups

    def finish(at, *parts):
        @pl.when(member == at)
        def _():
            for r in range(blocks):
                rows = pl.ds(r * quarter, quarter)
                total = functools.reduce(jnp.add, [part[rows, :] for part, _ in parts])
                out[r] = rhs[r] - total.T
            for part, k in parts:
                solved[k] = part[pl.ds(last, share), :]
            if at in (0, 3):
                solved[3 - at] = far[...]

    finish(0, (own, 0), (got_1, 1), (joined, 2))
    finish(1, (own, 1), (got_2, 3), (got_3, 0), (got_4, 2))
    finish(2, (own, 2), (got_2, 0), (got_3, 3), (got_4, 1))
    finish(3, (own, 3), (got_1, 2), (joined, 1))


def on_device(factor, rhs, inverses):
    steps = inverses.shape[0]
    blocks = factor.shape[0]
    width = factor.shape[3]
    quarter = rhs.shape[3]
    nrhs = rhs.shape[4]
    row_count = lax.axis_size("row")
    col_count = lax.axis_size("col")
    groups = col_count // steps
    row_pos = lax.axis_index("row")
    col_pos = lax.axis_index("col")
    member = col_pos // groups
    group = col_pos % groups
    share = width // col_count
    top = steps - 1
    me = row_pos * col_count + col_pos

    def dev(row, mem, grp):
        return row * col_count + mem * groups + grp

    def line(g, mem):
        return dev(g // groups, mem, g % groups)

    low_homes = (line(0, 0), line(1, 0))
    high_homes = (line(2, top - 1), line(3, top))

    def send(x, pairs):
        def twin(i):
            return i + col_count if (i // col_count) % 2 == 0 else i - col_count

        onward = dict(pairs)
        taken = set(onward) | set(onward.values())
        for start in sorted(set(onward) - set(onward.values())):
            stop = onward[start]
            while stop in onward:
                stop = onward[stop]
            back = [twin(stop), twin(start)]
            if twin(start) == stop or taken & set(back):
                onward[stop] = start
            else:
                onward[stop], onward[back[0]], onward[back[1]] = back[0], back[1], start
                taken |= set(back)
        left = []
        for i in range(row_count * col_count):
            if i not in onward:
                if twin(i) in taken:
                    left.append(i)
                else:
                    onward[i] = twin(i)
        paired = [i for i in sorted(onward) if onward[i] == twin(i) and i not in taken]
        for i in left:
            j = min(paired, key=lambda j: (j % col_count != i % col_count, abs(j - i)))
            onward[i], onward[j] = onward[j], i
            paired.remove(j)
        return lax.ppermute(x, AXES, sorted(onward.items()))

    def send_some(x, pairs):
        return lax.ppermute(x, AXES, pairs)

    def chosen(pairs, new, old):
        here = functools.reduce(jnp.logical_or, [me == d for _, d in pairs])
        return jnp.where(here, new, old)

    vmem = pl.BlockSpec(memory_space=VMEM)
    hbm = pl.BlockSpec(memory_space=pltpu.HBM)

    held_factor = pltpu.with_memory_space_constraint(factor, pltpu.HBM)
    held_inverses = pltpu.with_memory_space_constraint(inverses, pltpu.HBM)

    half = jax.ShapeDtypeStruct((2, width, width), jnp.bfloat16)
    near, mine = pl.pallas_call(
        fetch_kernel,
        in_specs=[hbm] * 2,
        out_specs=[vmem] * 2,
        out_shape=[
            jax.ShapeDtypeStruct((width, width), F32), jax.ShapeDtypeStruct((quarter, nrhs), F32)
        ],
        scratch_shapes=[pltpu.SemaphoreType.DMA((2,))],
        compiler_params=PARAMS,
        cost_estimate=CHEAP,
        name="fetch",
    )(held_factor, pltpu.with_memory_space_constraint(rhs, pltpu.HBM))
    ready = pl.pallas_call(
        functools.partial(ready_kernel, low_homes, col_count),
        in_specs=[hbm],
        out_specs=[vmem] * 2,
        out_shape=[half] * 2,
        scratch_shapes=[VMEM((2, width, width), F32), pltpu.SemaphoreType.DMA((2,))],
        compiler_params=PARAMS,
        cost_estimate=CHEAP,
        name="ready",
    )(held_inverses)
    gathered = [
        send(
            mine,
            [(line(g, j), line(g, 0)) for g in (0, 1)]
            + [(line(2, (top - 1 - j) % steps), high_homes[0]), (line(3, top - j), high_homes[1])],
        )
        for j in range(1, steps)
    ]
    la = send(near, [(line(1, 0), low_homes[0])])
    ly = send_some(near, [(line(2, 1), low_homes[0]), (line(3, 1), low_homes[1])])

    vector = VMEM((nrhs, width), F32)
    order = ((low_homes[1], (0, 1, 2, 3)), (high_homes[0], (2, 1, 0, 3)), (high_homes[1], (3, 2, 1, 0)))
    turned = pl.pallas_call(
        functools.partial(turn_kernel, order, low_homes[0], col_count),
        in_specs=[vmem] * 6,
        out_specs=vmem,
        out_shape=vector,
        compiler_params=PARAMS,
        cost_estimate=CHEAP,
        name="turn",
    )(mine, *gathered, *ready)
    swapped = send(turned, [low_homes, low_homes[::-1], high_homes])
    later = lax.optimization_barrier((near, turned))[0]
    last_block = send_some(later, [(line(3, 2), high_homes[1])])
    lx = send(later, [(line(2, 0), low_homes[0]), (line(3, 0), low_homes[1])])
    s_0, s_1 = pl.pallas_call(
        functools.partial(low_kernel, low_homes, col_count),
        in_specs=[vmem] * 6 + [pl.BlockSpec(memory_space=pl.ANY)],
        out_specs=[vmem] * 2,
        out_shape=[vector] * 2,
        compiler_params=PARAMS,
        cost_estimate=CHEAP,
        name="solve_low",
    )(turned, swapped, near, la, *ready, ly)
    w = pl.pallas_call(
        functools.partial(reduce_kernel, low_homes, col_count),
        in_specs=[vmem] * 2 + [pl.BlockSpec(memory_space=pl.ANY)] * 2,
        out_specs=vmem,
        out_shape=vector,
        scratch_shapes=[VMEM((2, width, width), F32), pltpu.SemaphoreType.DMA((2,))],
        compiler_params=PARAMS,
        cost_estimate=CHEAP,
        name="reduce_low",
    )(s_0, s_1, lx, ly)
    w_1 = send(w, [(low_homes[0], high_homes[1])])
    w_2 = send(w, [(low_homes[1], high_homes[1]), (low_homes[0], high_homes[0])])
    first_slots, second_slots = ((3, 0, 3, 0), (2, 2, 1, 1)), ((0, 1, 2, 3), (1, 3, 0, 2))
    s_high = pl.pallas_call(
        functools.partial(high_kernel, high_homes, col_count),
        in_specs=[vmem] * 4 + [hbm, pl.BlockSpec(memory_space=pl.ANY)],
        out_specs=vmem,
        out_shape=vector,
        scratch_shapes=[
            VMEM((2, width, width), F32), VMEM((width, width), F32), pltpu.SemaphoreType.DMA((3,))
        ],
        compiler_params=PARAMS,
        cost_estimate=CHEAP,
        name="solve_high",
    )(turned, swapped, w_1, w_2, held_inverses, last_block)

    def spread(s, homes):
        have = {k: list(homes[k]) for k in homes}
        todo = {
            k: sorted(
                [
                    (r, g) for r in range(row_count) for g in range(groups)
                    if r % 2 == homes[k][0][0] % 2 and (r, g) not in homes[k]
                ],
                key=lambda spot: -(spot[0] != homes[k][0][0]) - (spot[1] != homes[k][0][1]),
            )
            for k in homes
        }
        fan = 1 if all(len(spots) > 1 for spots in homes.values()) else 3
        firsts = [(0, dev(r, k, g)) for k in homes for r, g in homes[k]]
        far = None
        while any(todo.values()):
            held = s if far is None else chosen(firsts, s, far)
            rounds = [[] for _ in range(fan)]
            for k in homes:
                spots = list(have[k])
                for pairs in rounds:
                    for a in spots:
                        if todo[k]:
                            b = todo[k].pop()
                            have[k].append(b)
                            pairs.append((dev(a[0], k, a[1]), dev(b[0], k, b[1])))
            for pairs in rounds:
                if pairs:
                    got = send(held, pairs)
                    far = got if far is None else chosen(pairs, got, far)
        twins = {
            k: [(dev(r, k, g), dev(r ^ 1, k, g)) for r, g in have[k]] for k in homes
        }
        near_twins = [pair for k in homes for pair in twins[k][: len(homes[k])]]
        far_twins = [pair for k in homes for pair in twins[k][len(homes[k]):]]
        return s, far, send(s, near_twins), send(far, far_twins)

    spots = [(g // groups, g % groups) for g in range(4)]
    homes = (tuple(spots[:2]), tuple(spots[:2]), (spots[2],), (spots[3],))
    moved = send(s_1, [(line(g, 0), line(g, 1)) for g in (0, 1)])
    s_low = jnp.where(member == 0, s_0, moved)
    ways = spread(s_low, {0: homes[0], 1: homes[1]}) + spread(s_high, {2: homes[2], 3: homes[3]})

    far_share, part, longer = [
        jax.ShapeDtypeStruct((n, nrhs), F32)
        for n in (share, blocks * quarter + share, blocks * quarter + share + 8)
    ]

    def update(name, shapes, slots):
        return pl.pallas_call(
            functools.partial(update_kernel, (groups, row_count, share, homes, slots, blocks)),
            in_specs=[vmem] * 8 + [hbm],
            out_specs=[vmem] * len(shapes),
            out_shape=shapes,
            scratch_shapes=[
                VMEM((nrhs, width), F32),
                VMEM((quarter, nrhs), F32),
                VMEM((blocks, width, 2 * quarter), F32),
                pltpu.SemaphoreType.DMA((2 * blocks,)),
            ],
            compiler_params=PARAMS,
            cost_estimate=CHEAP,
            name=name,
        )(*ways, held_factor)

    part_a, part_b, far = update(
        "update_first", [part, longer, far_share], first_slots + ((3, 0, 0, 0),)
    )
    own, part_c = update("update_second", [part, longer], second_slots)
    across = [(r, g) for r in range(row_count) for g in range(groups)]

    def route(*hops):
        return [(dev(r, a, g), dev(r, b, g)) for a, b in hops for r, g in across]

    got_1 = send(part_a, route((3, 2), (0, 1), (1, 0), (2, 3)))
    got_4 = send(part_b, route((2, 1), (1, 2)))
    got_2 = send(part_b, route((3, 1), (1, 0), (0, 2), (2, 3)))
    got_3 = send_some(part_c, route((3, 2), (0, 1)))
    joined = pl.pallas_call(
        functools.partial(join_kernel, (groups, share)),
        in_specs=[vmem] * 2,
        out_specs=vmem,
        out_shape=part,
        compiler_params=PARAMS,
        cost_estimate=CHEAP,
        name="join",
    )(part_c, got_1)
    joined = send_some(joined, route((2, 0), (1, 3)))
    far = send(far, route((3, 0), (0, 3), (1, 2), (2, 1)))

    solved, remaining = pl.pallas_call(
        functools.partial(last_kernel, groups),
        in_specs=[vmem] * 8,
        out_specs=[vmem] * 2,
        out_shape=[
            jax.ShapeDtypeStruct((steps, share, nrhs), F32),
            jax.ShapeDtypeStruct((blocks, quarter, nrhs), F32),
        ],
        compiler_params=PARAMS,
        cost_estimate=CHEAP,
        name="add_up",
    )(rhs[:, 0, 0], own, got_1, got_2, got_3, got_4, joined, far)
    return solved, remaining[:, None, None]


def solution(mesh):
    in_specs = (P(None, "row", "col", None, None), P(None, "row", "col", None, None), P())
    out_specs = (P(None, "col", None), P(None, "row", "col", None, None))
    return jax.shard_map(
        on_device, mesh=mesh, in_specs=in_specs, out_specs=out_specs, check_vma=False
    )
```

```python
import functools

import jax
import jax.numpy as jnp
from jax import lax
from jax.experimental import pallas as pl
from jax.experimental.pallas import tpu as pltpu
from jax.sharding import PartitionSpec as P

AXES = ("row", "col")
F32 = jnp.float32
VMEM = pltpu.VMEM
PARAMS = pltpu.CompilerParams(vmem_limit_bytes=12 * 2**20)
CHEAP = pl.CostEstimate(flops=1000, bytes_accessed=1000, transcendentals=0)


def split(x):
    high = x.astype(jnp.bfloat16)
    return high, (x - high.astype(F32)).astype(jnp.bfloat16)


def product(a, b, transposed=False):
    b_high, b_low = b if isinstance(b, tuple) else split(b)
    dims = (((1,), (1 if transposed else 0,)), ((), ()))
    a_high, a_low = a if isinstance(a, tuple) else split(a)
    n = a_high.shape[0]
    both = lax.dot_general(
        jnp.concatenate([a_high, a_low], 0), b_high, dims, preferred_element_type=F32
    )
    cross = lax.dot_general(a_high, b_low, dims, preferred_element_type=F32)
    return both[:n] + (both[n:] + cross)


def position(col_count):
    return lax.axis_index("row") * col_count + lax.axis_index("col")


def fetch_kernel(factor, rhs, near, mine, sem):
    copies = [
        pltpu.make_async_copy(rhs.at[0, 0, 0], mine, sem.at[0]),
        pltpu.make_async_copy(factor.at[0, 0, 0], near, sem.at[1]),
    ]
    for copy in copies:
        copy.start()
    for copy in copies:
        copy.wait()


def ready_kernel(solvers, col_count, inverses, high, low, inv, sem):
    me = position(col_count)

    @pl.when((me == solvers[0]) | (me == solvers[1]))
    def _():
        copies = [pltpu.make_async_copy(inverses.at[i], inv.at[i], sem.at[i]) for i in range(2)]
        for copy in copies:
            copy.start()
        for i, copy in enumerate(copies):
            copy.wait()
            high[i], low[i] = split(inv[i])


def piece_columns(groups, table, quarter):
    member = lax.axis_index("col") // groups
    to = functools.reduce(jnp.add, [jnp.where(member == m, p, 0) for m, p in enumerate(table)])
    return pl.ds(pl.multiple_of(to * quarter, quarter), quarter)


def column_copies(groups, table_pair, panel, tiles, sems):
    quarter = tiles.shape[2] // 2
    return [
        [
            pltpu.make_async_copy(
                panel.at[r, 0, 0, :, piece_columns(groups, table, quarter)],
                tiles.at[r, :, pl.ds(i * quarter, quarter)],
                sems.at[2 * r + i],
            )
            for i, table in enumerate(table_pair)
        ]
        for r in range(tiles.shape[0])
    ]


def turn_kernel(order, solver, col_count, own, g1, g2, g3, high, low, out):
    me = position(col_count)

    def joined(pieces):
        return jnp.concatenate([piece[...].T for piece in pieces], axis=1)

    @pl.when(me == solver)
    def _():
        out[...] = product(joined((own, g1, g2, g3)), (high[0], low[0]), True)

    for device, places in order:
        @pl.when(me == device)
        def _(places=places):
            refs = (own, g1, g2, g3)
            out[...] = joined([refs[i] for i in places])


def low_kernel(homes, col_count, out, swapped, near, la, high, low, ly, s_a, s_b):
    del ly
    me = position(col_count)

    def work(first, right, block):
        s_a[...] = first[...]
        left = right[...] - product(first[...], block[...])
        s_b[...] = product(left, (high[1], low[1]), True)

    @pl.when(me == homes[0])
    def _():
        work(out, swapped, la)

    @pl.when(me == homes[1])
    def _():
        work(swapped, out, near)


def reduce_kernel(homes, col_count, s_a, s_b, lx, ly, w, block, sem):
    me = position(col_count)

    @pl.when((me == homes[0]) | (me == homes[1]))
    def _():
        copies = [pltpu.make_async_copy(ref, block.at[i], sem.at[i]) for i, ref in enumerate((ly, lx))]
        for copy in copies:
            copy.start()
        copies[0].wait()
        later = product(s_b[...], block[0])
        copies[1].wait()
        w[...] = product(s_a[...], block[1]) + later


def high_kernel(homes, col_count, own, swapped, w_1, w_2, inverses, last_block, s, inv, block, sem):
    me = position(col_count)
    copies = [pltpu.make_async_copy(inverses.at[2 + i], inv.at[i], sem.at[i]) for i in range(2)]
    copies.append(pltpu.make_async_copy(last_block, block, sem.at[2]))

    @pl.when(me == homes[0])
    def _():
        copies[0].start()
        right = own[...] - w_2[...]
        copies[0].wait()
        s[...] = product(right, inv[0], True)

    @pl.when(me == homes[1])
    def _():
        for copy in copies:
            copy.start()
        right = swapped[...] - w_1[...]
        copies[0].wait()
        first = product(right, inv[0], True)
        copies[2].wait()
        right = own[...] - w_2[...] - product(first, block[...])
        copies[1].wait()
        s[...] = product(right, inv[1], True)


def update_kernel(cfg, *refs):
    groups, row_count, share, homes, slots, blocks = cfg
    steps = len(homes)
    ways, panel, refs = refs[:8], refs[8], refs[9:]
    outs, shares, (s, turned, tiles, sems) = refs[:2], refs[2:-4], refs[-4:]
    copies = column_copies(groups, slots[:2], panel, tiles, sems)
    for pair in copies:
        for copy in pair:
            copy.start()
    quarter = turned.shape[0]
    row = lax.axis_index("row")
    col = lax.axis_index("col")
    member = col // groups
    group = col % groups
    columns = [piece_columns(groups, table, quarter) for table in slots]

    for half in range(2):
        planes = [m for m in range(steps) if m // (steps // 2) == half]

        def among(flip):
            return functools.reduce(jnp.logical_or, [
                (member == m) & (row == (r ^ flip)) & (group == g)
                for m in planes for r, g in homes[m]
            ])

        first, first_twin = among(0), among(1)
        here = functools.reduce(jnp.logical_or, [member == m for m in planes])
        same = here & (lax.rem(row, 2) == homes[planes[0]][0][0] % 2)
        other = here & (lax.rem(row, 2) != homes[planes[0]][0][0] % 2)
        roles = (
            first, same & jnp.logical_not(first), first_twin, other & jnp.logical_not(first_twin)
        )
        for way, role in zip(ways[4 * half:], roles):
            @pl.when(role)
            def _(src=way):
                s[...] = src[...]

    parts = split(s[...])
    for r in range(blocks):
        for copy in copies[r]:
            copy.wait()
        block_id = (r * row_count + row) * groups + group
        keep = (block_id > member).astype(F32)
        full = product(parts, tiles[r]) * keep
        for i, out in enumerate(outs):
            out[pl.ds(r * quarter, quarter), :] = full[:, i * quarter: (i + 1) * quarter]
    for place, out in zip(columns, outs + shares):
        turned[...] = s[:, place].T
        rows = pl.ds(pl.multiple_of(group * share, share), share)
        first = blocks * quarter if out.shape[0] > share else 0
        out[pl.ds(first, share), :] = turned[rows, :]


def join_kernel(cfg, mine, theirs, out):
    groups, share = cfg
    last = out.shape[0] - share
    member = lax.axis_index("col") // groups

    @pl.when((member == 1) | (member == 2))
    def _():
        out[:last, :] = mine[:last, :] + theirs[:last, :]
        out[last:, :] = mine[pl.ds(last, share), :]


def last_kernel(groups, rhs, own, got_1, got_2, got_3, got_4, joined, far, solved, out):
    blocks, quarter = rhs.shape[0], rhs.shape[1]
    last, share = blocks * quarter, solved.shape[1]
    member = lax.axis_index("col") // groups

    def finish(at, *parts):
        @pl.when(member == at)
        def _():
            for r in range(blocks):
                rows = pl.ds(r * quarter, quarter)
                total = functools.reduce(jnp.add, [part[rows, :] for part, _ in parts])
                out[r] = rhs[r] - total.T
            for part, k in parts:
                solved[k] = part[pl.ds(last, share), :]
            if at in (0, 3):
                solved[3 - at] = far[...]

    finish(0, (own, 0), (got_1, 1), (joined, 2))
    finish(1, (own, 1), (got_2, 3), (got_3, 0), (got_4, 2))
    finish(2, (own, 2), (got_2, 0), (got_3, 3), (got_4, 1))
    finish(3, (own, 3), (got_1, 2), (joined, 1))


def on_device(factor, rhs, inverses):
    steps = inverses.shape[0]
    blocks = factor.shape[0]
    width = factor.shape[3]
    quarter = rhs.shape[3]
    nrhs = rhs.shape[4]
    row_count = lax.axis_size("row")
    col_count = lax.axis_size("col")
    groups = col_count // steps
    row_pos = lax.axis_index("row")
    col_pos = lax.axis_index("col")
    member = col_pos // groups
    group = col_pos % groups
    share = width // col_count
    top = steps - 1
    me = row_pos * col_count + col_pos

    def dev(row, mem, grp):
        return row * col_count + mem * groups + grp

    def line(g, mem):
        return dev(g // groups, mem, g % groups)

    low_homes = (line(0, 0), line(1, 0))
    high_homes = (line(2, top - 1), line(3, top))

    def send(x, pairs):
        def twin(i):
            return i + col_count if (i // col_count) % 2 == 0 else i - col_count

        onward = dict(pairs)
        taken = set(onward) | set(onward.values())
        for start in sorted(set(onward) - set(onward.values())):
            stop = onward[start]
            while stop in onward:
                stop = onward[stop]
            back = [twin(stop), twin(start)]
            if twin(start) == stop or taken & set(back):
                onward[stop] = start
            else:
                onward[stop], onward[back[0]], onward[back[1]] = back[0], back[1], start
                taken |= set(back)
        left = []
        for i in range(row_count * col_count):
            if i not in onward:
                if twin(i) in taken:
                    left.append(i)
                else:
                    onward[i] = twin(i)
        paired = [i for i in sorted(onward) if onward[i] == twin(i) and i not in taken]
        for i in left:
            j = min(paired, key=lambda j: (j % col_count != i % col_count, abs(j - i)))
            onward[i], onward[j] = onward[j], i
            paired.remove(j)
        return lax.ppermute(x, AXES, sorted(onward.items()))

    def send_some(x, pairs):
        return lax.ppermute(x, AXES, pairs)

    def chosen(pairs, new, old):
        here = functools.reduce(jnp.logical_or, [me == d for _, d in pairs])
        return jnp.where(here, new, old)

    vmem = pl.BlockSpec(memory_space=VMEM)
    hbm = pl.BlockSpec(memory_space=pltpu.HBM)

    held_factor = pltpu.with_memory_space_constraint(factor, pltpu.HBM)
    held_inverses = pltpu.with_memory_space_constraint(inverses, pltpu.HBM)

    half = jax.ShapeDtypeStruct((2, width, width), jnp.bfloat16)
    near, mine = pl.pallas_call(
        fetch_kernel,
        in_specs=[hbm] * 2,
        out_specs=[vmem] * 2,
        out_shape=[
            jax.ShapeDtypeStruct((width, width), F32), jax.ShapeDtypeStruct((quarter, nrhs), F32)
        ],
        scratch_shapes=[pltpu.SemaphoreType.DMA((2,))],
        compiler_params=PARAMS,
        cost_estimate=CHEAP,
        name="fetch",
    )(held_factor, pltpu.with_memory_space_constraint(rhs, pltpu.HBM))
    ready = pl.pallas_call(
        functools.partial(ready_kernel, low_homes, col_count),
        in_specs=[hbm],
        out_specs=[vmem] * 2,
        out_shape=[half] * 2,
        scratch_shapes=[VMEM((2, width, width), F32), pltpu.SemaphoreType.DMA((2,))],
        compiler_params=PARAMS,
        cost_estimate=CHEAP,
        name="ready",
    )(held_inverses)
    gathered = [
        send(
            mine,
            [(line(g, j), line(g, 0)) for g in (0, 1)]
            + [(line(2, (top - 1 - j) % steps), high_homes[0]), (line(3, top - j), high_homes[1])],
        )
        for j in range(1, steps)
    ]
    la = send(near, [(line(1, 0), low_homes[0])])
    ly = send_some(near, [(line(2, 1), low_homes[0]), (line(3, 1), low_homes[1])])

    vector = VMEM((nrhs, width), F32)
    order = ((low_homes[1], (0, 1, 2, 3)), (high_homes[0], (2, 1, 0, 3)), (high_homes[1], (3, 2, 1, 0)))
    turned = pl.pallas_call(
        functools.partial(turn_kernel, order, low_homes[0], col_count),
        in_specs=[vmem] * 6,
        out_specs=vmem,
        out_shape=vector,
        compiler_params=PARAMS,
        cost_estimate=CHEAP,
        name="turn",
    )(mine, *gathered, *ready)
    swapped = send(turned, [low_homes, low_homes[::-1], high_homes])
    later = lax.optimization_barrier((near, turned))[0]
    last_block = send_some(later, [(line(3, 2), high_homes[1])])
    last_block = pltpu.with_memory_space_constraint(last_block, pltpu.HBM)
    lx = send(later, [(line(2, 0), low_homes[0]), (line(3, 0), low_homes[1])])
    s_0, s_1 = pl.pallas_call(
        functools.partial(low_kernel, low_homes, col_count),
        in_specs=[vmem] * 6 + [pl.BlockSpec(memory_space=pl.ANY)],
        out_specs=[vmem] * 2,
        out_shape=[vector] * 2,
        compiler_params=PARAMS,
        cost_estimate=CHEAP,
        name="solve_low",
    )(turned, swapped, near, la, *ready, ly)
    w = pl.pallas_call(
        functools.partial(reduce_kernel, low_homes, col_count),
        in_specs=[vmem] * 2 + [pl.BlockSpec(memory_space=pl.ANY)] * 2,
        out_specs=vmem,
        out_shape=vector,
        scratch_shapes=[VMEM((2, width, width), F32), pltpu.SemaphoreType.DMA((2,))],
        compiler_params=PARAMS,
        cost_estimate=CHEAP,
        name="reduce_low",
    )(s_0, s_1, lx, ly)
    w_1 = send(w, [(low_homes[0], high_homes[1])])
    w_2 = send(w, [(low_homes[1], high_homes[1]), (low_homes[0], high_homes[0])])
    first_slots, second_slots = ((3, 0, 3, 0), (2, 2, 1, 1)), ((0, 1, 2, 3), (1, 3, 0, 2))
    s_high = pl.pallas_call(
        functools.partial(high_kernel, high_homes, col_count),
        in_specs=[vmem] * 4 + [hbm, pl.BlockSpec(memory_space=pl.ANY)],
        out_specs=vmem,
        out_shape=vector,
        scratch_shapes=[
            VMEM((2, width, width), F32), VMEM((width, width), F32), pltpu.SemaphoreType.DMA((3,))
        ],
        compiler_params=PARAMS,
        cost_estimate=CHEAP,
        name="solve_high",
    )(turned, swapped, w_1, w_2, held_inverses, last_block)

    def spread(s, homes):
        have = {k: list(homes[k]) for k in homes}
        todo = {
            k: sorted(
                [
                    (r, g) for r in range(row_count) for g in range(groups)
                    if r % 2 == homes[k][0][0] % 2 and (r, g) not in homes[k]
                ],
                key=lambda spot: -(spot[0] != homes[k][0][0]) - (spot[1] != homes[k][0][1]),
            )
            for k in homes
        }
        fan = 1 if all(len(spots) > 1 for spots in homes.values()) else 3
        firsts = [(0, dev(r, k, g)) for k in homes for r, g in homes[k]]
        far = None
        while any(todo.values()):
            held = s if far is None else chosen(firsts, s, far)
            rounds = [[] for _ in range(fan)]
            for k in homes:
                spots = list(have[k])
                for pairs in rounds:
                    for a in spots:
                        if todo[k]:
                            b = todo[k].pop()
                            have[k].append(b)
                            pairs.append((dev(a[0], k, a[1]), dev(b[0], k, b[1])))
            for pairs in rounds:
                if pairs:
                    got = send(held, pairs)
                    far = got if far is None else chosen(pairs, got, far)
        twins = {
            k: [(dev(r, k, g), dev(r ^ 1, k, g)) for r, g in have[k]] for k in homes
        }
        near_twins = [pair for k in homes for pair in twins[k][: len(homes[k])]]
        far_twins = [pair for k in homes for pair in twins[k][len(homes[k]):]]
        return s, far, send(s, near_twins), send(far, far_twins)

    spots = [(g // groups, g % groups) for g in range(4)]
    homes = (tuple(spots[:2]), tuple(spots[:2]), (spots[2],), (spots[3],))
    moved = send(s_1, [(line(g, 0), line(g, 1)) for g in (0, 1)])
    s_low = jnp.where(member == 0, s_0, moved)
    ways = spread(s_low, {0: homes[0], 1: homes[1]}) + spread(s_high, {2: homes[2], 3: homes[3]})

    far_share, part, longer = [
        jax.ShapeDtypeStruct((n, nrhs), F32)
        for n in (share, blocks * quarter + share, blocks * quarter + share + 8)
    ]

    def update(name, shapes, slots):
        return pl.pallas_call(
            functools.partial(update_kernel, (groups, row_count, share, homes, slots, blocks)),
            in_specs=[vmem] * 8 + [hbm],
            out_specs=[vmem] * len(shapes),
            out_shape=shapes,
            scratch_shapes=[
                VMEM((nrhs, width), F32),
                VMEM((quarter, nrhs), F32),
                VMEM((blocks, width, 2 * quarter), F32),
                pltpu.SemaphoreType.DMA((2 * blocks,)),
            ],
            compiler_params=PARAMS,
            cost_estimate=CHEAP,
            name=name,
        )(*ways, held_factor)

    part_a, part_b, far = update(
        "update_first", [part, longer, far_share], first_slots + ((3, 0, 0, 0),)
    )
    own, part_c = update("update_second", [part, longer], second_slots)
    across = [(r, g) for r in range(row_count) for g in range(groups)]

    def route(*hops):
        return [(dev(r, a, g), dev(r, b, g)) for a, b in hops for r, g in across]

    got_1 = send(part_a, route((3, 2), (0, 1), (1, 0), (2, 3)))
    got_4 = send(part_b, route((2, 1), (1, 2)))
    got_2 = send(part_b, route((3, 1), (1, 0), (0, 2), (2, 3)))
    got_3 = send_some(part_c, route((3, 2), (0, 1)))
    joined = pl.pallas_call(
        functools.partial(join_kernel, (groups, share)),
        in_specs=[vmem] * 2,
        out_specs=vmem,
        out_shape=part,
        compiler_params=PARAMS,
        cost_estimate=CHEAP,
        name="join",
    )(part_c, got_1)
    joined = send_some(joined, route((2, 0), (1, 3)))
    far = send(far, route((3, 0), (0, 3), (1, 2), (2, 1)))

    solved, remaining = pl.pallas_call(
        functools.partial(last_kernel, groups),
        in_specs=[vmem] * 8,
        out_specs=[vmem] * 2,
        out_shape=[
            jax.ShapeDtypeStruct((steps, share, nrhs), F32),
            jax.ShapeDtypeStruct((blocks, quarter, nrhs), F32),
        ],
        compiler_params=PARAMS,
        cost_estimate=CHEAP,
        name="add_up",
    )(rhs[:, 0, 0], own, got_1, got_2, got_3, got_4, joined, far)
    return solved, remaining[:, None, None]


def solution(mesh):
    in_specs = (P(None, "row", "col", None, None), P(None, "row", "col", None, None), P())
    out_specs = (P(None, "col", None), P(None, "row", "col", None, None))
    return jax.shard_map(
        on_device, mesh=mesh, in_specs=in_specs, out_specs=out_specs, check_vma=False
    )
```

```python
import functools

import jax
import jax.numpy as jnp
from jax import lax
from jax.experimental import pallas as pl
from jax.experimental.pallas import tpu as pltpu
from jax.sharding import PartitionSpec as P

AXES = ("row", "col")
F32 = jnp.float32
VMEM = pltpu.VMEM
PARAMS = pltpu.CompilerParams(vmem_limit_bytes=12 * 2**20)
CHEAP = pl.CostEstimate(flops=1000, bytes_accessed=1000, transcendentals=0)


def split(x):
    high = x.astype(jnp.bfloat16)
    return high, (x - high.astype(F32)).astype(jnp.bfloat16)


def product(a, b, transposed=False):
    b_high, b_low = b if isinstance(b, tuple) else split(b)
    dims = (((1,), (1 if transposed else 0,)), ((), ()))
    a_high, a_low = a if isinstance(a, tuple) else split(a)
    n = a_high.shape[0]
    both = lax.dot_general(
        jnp.concatenate([a_high, a_low], 0), b_high, dims, preferred_element_type=F32
    )
    cross = lax.dot_general(a_high, b_low, dims, preferred_element_type=F32)
    return both[:n] + (both[n:] + cross)


def position(col_count):
    return lax.axis_index("row") * col_count + lax.axis_index("col")


def fetch_kernel(factor, rhs, near, mine, sem):
    copies = [
        pltpu.make_async_copy(rhs.at[0, 0, 0], mine, sem.at[0]),
        pltpu.make_async_copy(factor.at[0, 0, 0], near, sem.at[1]),
    ]
    for copy in copies:
        copy.start()
    for copy in copies:
        copy.wait()


def ready_kernel(solvers, col_count, inverses, high, low, inv, sem):
    me = position(col_count)

    @pl.when((me == solvers[0]) | (me == solvers[1]))
    def _():
        copies = [pltpu.make_async_copy(inverses.at[i], inv.at[i], sem.at[i]) for i in range(2)]
        for copy in copies:
            copy.start()
        for i, copy in enumerate(copies):
            copy.wait()
            high[i], low[i] = split(inv[i])


def piece_columns(groups, table, quarter):
    member = lax.axis_index("col") // groups
    to = functools.reduce(jnp.add, [jnp.where(member == m, p, 0) for m, p in enumerate(table)])
    return pl.ds(pl.multiple_of(to * quarter, quarter), quarter)


def column_copies(groups, table_pair, panel, tiles, sems):
    quarter = tiles.shape[2] // 2
    return [
        [
            pltpu.make_async_copy(
                panel.at[r, 0, 0, :, piece_columns(groups, table, quarter)],
                tiles.at[r, :, pl.ds(i * quarter, quarter)],
                sems.at[2 * r + i],
            )
            for i, table in enumerate(table_pair)
        ]
        for r in range(tiles.shape[0])
    ]


def turn_kernel(order, solver, col_count, own, g1, g2, g3, high, low, out):
    me = position(col_count)

    def joined(pieces):
        return jnp.concatenate([piece[...].T for piece in pieces], axis=1)

    @pl.when(me == solver)
    def _():
        out[...] = product(joined((own, g1, g2, g3)), (high[0], low[0]), True)

    for device, places in order:
        @pl.when(me == device)
        def _(places=places):
            refs = (own, g1, g2, g3)
            out[...] = joined([refs[i] for i in places])


def low_kernel(homes, col_count, out, swapped, near, la, high, low, ly, s_a, s_b):
    del ly
    me = position(col_count)

    def work(first, right, block):
        s_a[...] = first[...]
        left = right[...] - product(first[...], block[...])
        s_b[...] = product(left, (high[1], low[1]), True)

    @pl.when(me == homes[0])
    def _():
        work(out, swapped, la)

    @pl.when(me == homes[1])
    def _():
        work(swapped, out, near)


def reduce_kernel(homes, col_count, s_a, s_b, lx, ly, w, block, sem):
    me = position(col_count)

    @pl.when((me == homes[0]) | (me == homes[1]))
    def _():
        copies = [pltpu.make_async_copy(ref, block.at[i], sem.at[i]) for i, ref in enumerate((ly, lx))]
        for copy in copies:
            copy.start()
        copies[0].wait()
        later = product(s_b[...], block[0])
        copies[1].wait()
        w[...] = product(s_a[...], block[1]) + later


def high_kernel(homes, col_count, own, swapped, w_1, w_2, inverses, last_block, s, inv, block, sem):
    me = position(col_count)
    copies = [pltpu.make_async_copy(inverses.at[2 + i], inv.at[i], sem.at[i]) for i in range(2)]
    copies.append(pltpu.make_async_copy(last_block, block, sem.at[2]))

    @pl.when(me == homes[0])
    def _():
        copies[0].start()
        right = own[...] - w_2[...]
        copies[0].wait()
        s[...] = product(right, inv[0], True)

    @pl.when(me == homes[1])
    def _():
        for copy in copies:
            copy.start()
        right = swapped[...] - w_1[...]
        copies[0].wait()
        first = product(right, inv[0], True)
        copies[2].wait()
        right = own[...] - w_2[...] - product(first, block[...])
        copies[1].wait()
        s[...] = product(right, inv[1], True)


def update_kernel(cfg, *refs):
    groups, row_count, share, homes, slots, blocks = cfg
    steps = len(homes)
    ways, panel, refs = refs[:8], refs[8], refs[9:]
    outs, shares, (s, turned, tiles, sems) = refs[:2], refs[2:-4], refs[-4:]
    copies = column_copies(groups, slots[:2], panel, tiles, sems)
    for pair in copies:
        for copy in pair:
            copy.start()
    quarter = turned.shape[0]
    row = lax.axis_index("row")
    col = lax.axis_index("col")
    member = col // groups
    group = col % groups
    columns = [piece_columns(groups, table, quarter) for table in slots]

    for half in range(2):
        planes = [m for m in range(steps) if m // (steps // 2) == half]

        def among(flip):
            return functools.reduce(jnp.logical_or, [
                (member == m) & (row == (r ^ flip)) & (group == g)
                for m in planes for r, g in homes[m]
            ])

        first, first_twin = among(0), among(1)
        here = functools.reduce(jnp.logical_or, [member == m for m in planes])
        same = here & (lax.rem(row, 2) == homes[planes[0]][0][0] % 2)
        other = here & (lax.rem(row, 2) != homes[planes[0]][0][0] % 2)
        roles = (
            first, same & jnp.logical_not(first), first_twin, other & jnp.logical_not(first_twin)
        )
        for way, role in zip(ways[4 * half:], roles):
            @pl.when(role)
            def _(src=way):
                s[...] = src[...]

    parts = split(s[...])
    for r in range(blocks):
        for copy in copies[r]:
            copy.wait()
        block_id = (r * row_count + row) * groups + group
        keep = (block_id > member).astype(F32)
        full = product(parts, tiles[r]) * keep
        for i, out in enumerate(outs):
            out[pl.ds(r * quarter, quarter), :] = full[:, i * quarter: (i + 1) * quarter]
    for place, out in zip(columns, outs + shares):
        turned[...] = s[:, place].T
        rows = pl.ds(pl.multiple_of(group * share, share), share)
        first = blocks * quarter if out.shape[0] > share else 0
        out[pl.ds(first, share), :] = turned[rows, :]


def join_kernel(cfg, mine, theirs, out):
    groups, share = cfg
    last = out.shape[0] - share
    member = lax.axis_index("col") // groups

    @pl.when((member == 1) | (member == 2))
    def _():
        out[:last, :] = mine[:last, :] + theirs[:last, :]
        out[last:, :] = mine[pl.ds(last, share), :]


def last_kernel(groups, rhs, own, got_1, got_2, got_3, got_4, joined, far, solved, out):
    blocks, quarter = rhs.shape[0], rhs.shape[1]
    last, share = blocks * quarter, solved.shape[1]
    member = lax.axis_index("col") // groups

    def finish(at, *parts):
        @pl.when(member == at)
        def _():
            for r in range(blocks):
                rows = pl.ds(r * quarter, quarter)
                total = functools.reduce(jnp.add, [part[rows, :] for part, _ in parts])
                out[r] = rhs[r] - total.T
            for part, k in parts:
                solved[k] = part[pl.ds(last, share), :]
            if at in (0, 3):
                solved[3 - at] = far[...]

    finish(0, (own, 0), (got_1, 1), (joined, 2))
    finish(1, (own, 1), (got_2, 3), (got_3, 0), (got_4, 2))
    finish(2, (own, 2), (got_2, 0), (got_3, 3), (got_4, 1))
    finish(3, (own, 3), (got_1, 2), (joined, 1))


def on_device(factor, rhs, inverses):
    steps = inverses.shape[0]
    blocks = factor.shape[0]
    width = factor.shape[3]
    quarter = rhs.shape[3]
    nrhs = rhs.shape[4]
    row_count = lax.axis_size("row")
    col_count = lax.axis_size("col")
    groups = col_count // steps
    row_pos = lax.axis_index("row")
    col_pos = lax.axis_index("col")
    member = col_pos // groups
    group = col_pos % groups
    share = width // col_count
    top = steps - 1
    me = row_pos * col_count + col_pos

    def dev(row, mem, grp):
        return row * col_count + mem * groups + grp

    def line(g, mem):
        return dev(g // groups, mem, g % groups)

    low_homes = (line(0, 0), line(1, 0))
    high_homes = (line(2, top - 1), line(3, top))

    def send(x, pairs):
        def twin(i):
            return i + col_count if (i // col_count) % 2 == 0 else i - col_count

        onward = dict(pairs)
        taken = set(onward) | set(onward.values())
        for start in sorted(set(onward) - set(onward.values())):
            stop = onward[start]
            while stop in onward:
                stop = onward[stop]
            back = [twin(stop), twin(start)]
            if twin(start) == stop or taken & set(back):
                onward[stop] = start
            else:
                onward[stop], onward[back[0]], onward[back[1]] = back[0], back[1], start
                taken |= set(back)
        left = []
        for i in range(row_count * col_count):
            if i not in onward:
                if twin(i) in taken:
                    left.append(i)
                else:
                    onward[i] = twin(i)
        paired = [i for i in sorted(onward) if onward[i] == twin(i) and i not in taken]
        for i in left:
            j = min(paired, key=lambda j: (j % col_count != i % col_count, abs(j - i)))
            onward[i], onward[j] = onward[j], i
            paired.remove(j)
        return lax.ppermute(x, AXES, sorted(onward.items()))

    def send_some(x, pairs):
        return lax.ppermute(x, AXES, pairs)

    def chosen(pairs, new, old):
        here = functools.reduce(jnp.logical_or, [me == d for _, d in pairs])
        return jnp.where(here, new, old)

    vmem = pl.BlockSpec(memory_space=VMEM)
    hbm = pl.BlockSpec(memory_space=pltpu.HBM)

    held_factor = pltpu.with_memory_space_constraint(factor, pltpu.HBM)
    held_inverses = pltpu.with_memory_space_constraint(inverses, pltpu.HBM)

    half = jax.ShapeDtypeStruct((2, width, width), jnp.bfloat16)
    near, mine = pl.pallas_call(
        fetch_kernel,
        in_specs=[hbm] * 2,
        out_specs=[vmem] * 2,
        out_shape=[
            jax.ShapeDtypeStruct((width, width), F32), jax.ShapeDtypeStruct((quarter, nrhs), F32)
        ],
        scratch_shapes=[pltpu.SemaphoreType.DMA((2,))],
        compiler_params=PARAMS,
        cost_estimate=CHEAP,
        name="fetch",
    )(held_factor, pltpu.with_memory_space_constraint(rhs, pltpu.HBM))
    ready = pl.pallas_call(
        functools.partial(ready_kernel, low_homes, col_count),
        in_specs=[hbm],
        out_specs=[vmem] * 2,
        out_shape=[half] * 2,
        scratch_shapes=[VMEM((2, width, width), F32), pltpu.SemaphoreType.DMA((2,))],
        compiler_params=PARAMS,
        cost_estimate=CHEAP,
        name="ready",
    )(held_inverses)
    gathered = [
        send(
            mine,
            [(line(g, j), line(g, 0)) for g in (0, 1)]
            + [(line(2, (top - 1 - j) % steps), high_homes[0]), (line(3, top - j), high_homes[1])],
        )
        for j in range(1, steps)
    ]
    la = send(near, [(line(1, 0), low_homes[0])])
    ly = send_some(near, [(line(2, 1), low_homes[0]), (line(3, 1), low_homes[1])])

    vector = VMEM((nrhs, width), F32)
    order = ((low_homes[1], (0, 1, 2, 3)), (high_homes[0], (2, 1, 0, 3)), (high_homes[1], (3, 2, 1, 0)))
    turned = pl.pallas_call(
        functools.partial(turn_kernel, order, low_homes[0], col_count),
        in_specs=[vmem] * 6,
        out_specs=vmem,
        out_shape=vector,
        compiler_params=PARAMS,
        cost_estimate=CHEAP,
        name="turn",
    )(mine, *gathered, *ready)
    swapped = send(turned, [low_homes, low_homes[::-1], high_homes])
    later = lax.optimization_barrier((near, turned))[0]
    last_block = send_some(later, [(line(3, 2), high_homes[1])])
    last_block = pltpu.with_memory_space_constraint(last_block, pltpu.HBM)
    lx = send(later, [(line(2, 0), low_homes[0]), (line(3, 0), low_homes[1])])
    s_0, s_1 = pl.pallas_call(
        functools.partial(low_kernel, low_homes, col_count),
        in_specs=[vmem] * 6 + [pl.BlockSpec(memory_space=pl.ANY)],
        out_specs=[vmem] * 2,
        out_shape=[vector] * 2,
        compiler_params=PARAMS,
        cost_estimate=CHEAP,
        name="solve_low",
    )(turned, swapped, near, la, *ready, ly)
    w = pl.pallas_call(
        functools.partial(reduce_kernel, low_homes, col_count),
        in_specs=[vmem] * 2 + [pl.BlockSpec(memory_space=pl.ANY)] * 2,
        out_specs=vmem,
        out_shape=vector,
        scratch_shapes=[VMEM((2, width, width), F32), pltpu.SemaphoreType.DMA((2,))],
        compiler_params=PARAMS,
        cost_estimate=CHEAP,
        name="reduce_low",
    )(s_0, s_1, lx, ly)
    w_1 = send(w, [(low_homes[0], high_homes[1])])
    w_2 = send(w, [(low_homes[1], high_homes[1]), (low_homes[0], high_homes[0])])
    first_slots, second_slots = ((3, 0, 3, 0), (2, 2, 1, 1)), ((0, 1, 2, 3), (1, 3, 0, 2))
    s_high = pl.pallas_call(
        functools.partial(high_kernel, high_homes, col_count),
        in_specs=[vmem] * 4 + [hbm, pl.BlockSpec(memory_space=pl.ANY)],
        out_specs=vmem,
        out_shape=vector,
        scratch_shapes=[
            VMEM((2, width, width), F32), VMEM((width, width), F32), pltpu.SemaphoreType.DMA((3,))
        ],
        compiler_params=PARAMS,
        cost_estimate=CHEAP,
        name="solve_high",
    )(turned, swapped, w_1, w_2, held_inverses, last_block)

    def spread(s, homes):
        have = {k: list(homes[k]) for k in homes}
        todo = {
            k: sorted(
                [
                    (r, g) for r in range(row_count) for g in range(groups)
                    if r % 2 == homes[k][0][0] % 2 and (r, g) not in homes[k]
                ],
                key=lambda spot: -(spot[0] != homes[k][0][0]) - (spot[1] != homes[k][0][1]),
            )
            for k in homes
        }
        fan = 1 if all(len(spots) > 1 for spots in homes.values()) else 3
        firsts = [(0, dev(r, k, g)) for k in homes for r, g in homes[k]]
        far = None
        while any(todo.values()):
            held = s if far is None else chosen(firsts, s, far)
            rounds = [[] for _ in range(fan)]
            for k in homes:
                spots = list(have[k])
                for pairs in rounds:
                    for a in spots:
                        if todo[k]:
                            b = todo[k].pop()
                            have[k].append(b)
                            pairs.append((dev(a[0], k, a[1]), dev(b[0], k, b[1])))
            for pairs in rounds:
                if pairs:
                    got = send(held, pairs)
                    far = got if far is None else chosen(pairs, got, far)
        twins = {
            k: [(dev(r, k, g), dev(r ^ 1, k, g)) for r, g in have[k]] for k in homes
        }
        near_twins = [pair for k in homes for pair in twins[k][: len(homes[k])]]
        far_twins = [pair for k in homes for pair in twins[k][len(homes[k]):]]
        return s, far, send(s, near_twins), send(far, far_twins)

    spots = [(g // groups, g % groups) for g in range(4)]
    homes = (tuple(spots[:2]), tuple(spots[:2]), (spots[2],), (spots[3],))
    moved = send(lax.optimization_barrier((s_1, w))[0], [(line(g, 0), line(g, 1)) for g in (0, 1)])
    s_low = jnp.where(member == 0, s_0, moved)
    ways = spread(s_low, {0: homes[0], 1: homes[1]}) + spread(s_high, {2: homes[2], 3: homes[3]})

    far_share, part, longer = [
        jax.ShapeDtypeStruct((n, nrhs), F32)
        for n in (share, blocks * quarter + share, blocks * quarter + share + 8)
    ]

    def update(name, shapes, slots):
        return pl.pallas_call(
            functools.partial(update_kernel, (groups, row_count, share, homes, slots, blocks)),
            in_specs=[vmem] * 8 + [hbm],
            out_specs=[vmem] * len(shapes),
            out_shape=shapes,
            scratch_shapes=[
                VMEM((nrhs, width), F32),
                VMEM((quarter, nrhs), F32),
                VMEM((blocks, width, 2 * quarter), F32),
                pltpu.SemaphoreType.DMA((2 * blocks,)),
            ],
            compiler_params=PARAMS,
            cost_estimate=CHEAP,
            name=name,
        )(*ways, held_factor)

    part_a, part_b, far = update(
        "update_first", [part, longer, far_share], first_slots + ((3, 0, 0, 0),)
    )
    own, part_c = update("update_second", [part, longer], second_slots)
    across = [(r, g) for r in range(row_count) for g in range(groups)]

    def route(*hops):
        return [(dev(r, a, g), dev(r, b, g)) for a, b in hops for r, g in across]

    got_1 = send(part_a, route((3, 2), (0, 1), (1, 0), (2, 3)))
    got_4 = send(part_b, route((2, 1), (1, 2)))
    got_2 = send(part_b, route((3, 1), (1, 0), (0, 2), (2, 3)))
    got_3 = send_some(part_c, route((3, 2), (0, 1)))
    joined = pl.pallas_call(
        functools.partial(join_kernel, (groups, share)),
        in_specs=[vmem] * 2,
        out_specs=vmem,
        out_shape=part,
        compiler_params=PARAMS,
        cost_estimate=CHEAP,
        name="join",
    )(part_c, got_1)
    joined = send_some(joined, route((2, 0), (1, 3)))
    far = send(far, route((3, 0), (0, 3), (1, 2), (2, 1)))

    solved, remaining = pl.pallas_call(
        functools.partial(last_kernel, groups),
        in_specs=[vmem] * 8,
        out_specs=[vmem] * 2,
        out_shape=[
            jax.ShapeDtypeStruct((steps, share, nrhs), F32),
            jax.ShapeDtypeStruct((blocks, quarter, nrhs), F32),
        ],
        compiler_params=PARAMS,
        cost_estimate=CHEAP,
        name="add_up",
    )(rhs[:, 0, 0], own, got_1, got_2, got_3, got_4, joined, far)
    return solved, remaining[:, None, None]


def solution(mesh):
    in_specs = (P(None, "row", "col", None, None), P(None, "row", "col", None, None), P())
    out_specs = (P(None, "col", None), P(None, "row", "col", None, None))
    return jax.shard_map(
        on_device, mesh=mesh, in_specs=in_specs, out_specs=out_specs, check_vma=False
    )
```

```python
import functools

import jax
import jax.numpy as jnp
from jax import lax
from jax.experimental import pallas as pl
from jax.experimental.pallas import tpu as pltpu
from jax.sharding import PartitionSpec as P

AXES = ("row", "col")
F32 = jnp.float32
VMEM = pltpu.VMEM
PARAMS = pltpu.CompilerParams(vmem_limit_bytes=12 * 2**20)
CHEAP = pl.CostEstimate(flops=1000, bytes_accessed=1000, transcendentals=0)


def split(x):
    high = x.astype(jnp.bfloat16)
    return high, (x - high.astype(F32)).astype(jnp.bfloat16)


def product(a, b, transposed=False):
    b_high, b_low = b if isinstance(b, tuple) else split(b)
    dims = (((1,), (1 if transposed else 0,)), ((), ()))
    a_high, a_low = a if isinstance(a, tuple) else split(a)
    n = a_high.shape[0]
    both = lax.dot_general(
        jnp.concatenate([a_high, a_low], 0), b_high, dims, preferred_element_type=F32
    )
    cross = lax.dot_general(a_high, b_low, dims, preferred_element_type=F32)
    return both[:n] + (both[n:] + cross)


def position(col_count):
    return lax.axis_index("row") * col_count + lax.axis_index("col")


def fetch_kernel(factor, rhs, near, mine, sem):
    copies = [
        pltpu.make_async_copy(rhs.at[0, 0, 0], mine, sem.at[0]),
        pltpu.make_async_copy(factor.at[0, 0, 0], near, sem.at[1]),
    ]
    for copy in copies:
        copy.start()
    for copy in copies:
        copy.wait()


def ready_kernel(solvers, col_count, inverses, high, low, inv, sem):
    me = position(col_count)

    @pl.when((me == solvers[0]) | (me == solvers[1]))
    def _():
        copies = [pltpu.make_async_copy(inverses.at[i], inv.at[i], sem.at[i]) for i in range(2)]
        for copy in copies:
            copy.start()
        for i, copy in enumerate(copies):
            copy.wait()
            high[i], low[i] = split(inv[i])


def piece_columns(groups, table, quarter):
    member = lax.axis_index("col") // groups
    to = functools.reduce(jnp.add, [jnp.where(member == m, p, 0) for m, p in enumerate(table)])
    return pl.ds(pl.multiple_of(to * quarter, quarter), quarter)


def column_copies(groups, table_pair, panel, tiles, sems):
    quarter = tiles.shape[2] // 2
    return [
        [
            pltpu.make_async_copy(
                panel.at[r, 0, 0, :, piece_columns(groups, table, quarter)],
                tiles.at[r, :, pl.ds(i * quarter, quarter)],
                sems.at[2 * r + i],
            )
            for i, table in enumerate(table_pair)
        ]
        for r in range(tiles.shape[0])
    ]


def turn_kernel(order, solver, col_count, own, g1, g2, g3, high, low, out):
    me = position(col_count)

    def joined(pieces):
        return jnp.concatenate([piece[...].T for piece in pieces], axis=1)

    @pl.when(me == solver)
    def _():
        out[...] = product(joined((own, g1, g2, g3)), (high[0], low[0]), True)

    for device, places in order:
        @pl.when(me == device)
        def _(places=places):
            refs = (own, g1, g2, g3)
            out[...] = joined([refs[i] for i in places])


def low_kernel(homes, col_count, out, swapped, near, la, high, low, ly, s_a, s_b):
    del ly
    me = position(col_count)

    def work(first, right, block):
        s_a[...] = first[...]
        left = right[...] - product(first[...], block[...])
        s_b[...] = product(left, (high[1], low[1]), True)

    @pl.when(me == homes[0])
    def _():
        work(out, swapped, la)

    @pl.when(me == homes[1])
    def _():
        work(swapped, out, near)


def reduce_kernel(homes, col_count, s_a, s_b, lx, ly, w, block, sem):
    me = position(col_count)

    @pl.when((me == homes[0]) | (me == homes[1]))
    def _():
        copies = [pltpu.make_async_copy(ref, block.at[i], sem.at[i]) for i, ref in enumerate((ly, lx))]
        for copy in copies:
            copy.start()
        copies[0].wait()
        later = product(s_b[...], block[0])
        copies[1].wait()
        w[...] = product(s_a[...], block[1]) + later


def high_kernel(homes, col_count, own, swapped, w_1, w_2, inverses, last_block, s, inv, block, sem):
    me = position(col_count)
    copies = [pltpu.make_async_copy(inverses.at[2 + i], inv.at[i], sem.at[i]) for i in range(2)]
    copies.append(pltpu.make_async_copy(last_block, block, sem.at[2]))

    @pl.when(me == homes[0])
    def _():
        copies[0].start()
        right = own[...] - w_2[...]
        copies[0].wait()
        s[...] = product(right, inv[0], True)

    @pl.when(me == homes[1])
    def _():
        for copy in copies:
            copy.start()
        right = swapped[...] - w_1[...]
        copies[0].wait()
        first = product(right, inv[0], True)
        copies[2].wait()
        right = own[...] - w_2[...] - product(first, block[...])
        copies[1].wait()
        s[...] = product(right, inv[1], True)


def update_kernel(cfg, *refs):
    groups, row_count, share, homes, slots, blocks = cfg
    steps = len(homes)
    ways, panel, refs = refs[:8], refs[8], refs[9:]
    outs, shares, (s, turned, tiles, sems) = refs[:2], refs[2:-4], refs[-4:]
    copies = column_copies(groups, slots[:2], panel, tiles, sems)
    for pair in copies:
        for copy in pair:
            copy.start()
    quarter = turned.shape[0]
    row = lax.axis_index("row")
    col = lax.axis_index("col")
    member = col // groups
    group = col % groups
    columns = [piece_columns(groups, table, quarter) for table in slots]

    for half in range(2):
        planes = [m for m in range(steps) if m // (steps // 2) == half]

        def among(flip):
            return functools.reduce(jnp.logical_or, [
                (member == m) & (row == (r ^ flip)) & (group == g)
                for m in planes for r, g in homes[m]
            ])

        first, first_twin = among(0), among(1)
        here = functools.reduce(jnp.logical_or, [member == m for m in planes])
        same = here & (lax.rem(row, 2) == homes[planes[0]][0][0] % 2)
        other = here & (lax.rem(row, 2) != homes[planes[0]][0][0] % 2)
        roles = (
            first, same & jnp.logical_not(first), first_twin, other & jnp.logical_not(first_twin)
        )
        for way, role in zip(ways[4 * half:], roles):
            @pl.when(role)
            def _(src=way):
                s[...] = src[...]

    parts = split(s[...])
    for r in range(blocks):
        for copy in copies[r]:
            copy.wait()
        block_id = (r * row_count + row) * groups + group
        keep = (block_id > member).astype(F32)
        full = product(parts, tiles[r]) * keep
        for i, out in enumerate(outs):
            out[pl.ds(r * quarter, quarter), :] = full[:, i * quarter: (i + 1) * quarter]
    for place, out in zip(columns, outs + shares):
        turned[...] = s[:, place].T
        rows = pl.ds(pl.multiple_of(group * share, share), share)
        first = blocks * quarter if out.shape[0] > share else 0
        out[pl.ds(first, share), :] = turned[rows, :]


def join_kernel(cfg, mine, theirs, out):
    groups, share = cfg
    last = out.shape[0] - share
    member = lax.axis_index("col") // groups

    @pl.when((member == 1) | (member == 2))
    def _():
        out[:last, :] = mine[:last, :] + theirs[:last, :]
        out[last:, :] = mine[pl.ds(last, share), :]


def last_kernel(groups, rhs, own, got_1, got_2, got_3, got_4, joined, far, solved, out):
    blocks, quarter = rhs.shape[0], rhs.shape[1]
    last, share = blocks * quarter, solved.shape[1]
    member = lax.axis_index("col") // groups

    def finish(at, *parts):
        @pl.when(member == at)
        def _():
            for r in range(blocks):
                rows = pl.ds(r * quarter, quarter)
                total = functools.reduce(jnp.add, [part[rows, :] for part, _ in parts])
                out[r] = rhs[r] - total.T
            for part, k in parts:
                solved[k] = part[pl.ds(last, share), :]
            if at in (0, 3):
                solved[3 - at] = far[...]

    finish(0, (own, 0), (got_1, 1), (joined, 2))
    finish(1, (own, 1), (got_2, 3), (got_3, 0), (got_4, 2))
    finish(2, (own, 2), (got_2, 0), (got_3, 3), (got_4, 1))
    finish(3, (own, 3), (got_1, 2), (joined, 1))


def on_device(factor, rhs, inverses):
    steps = inverses.shape[0]
    blocks = factor.shape[0]
    width = factor.shape[3]
    quarter = rhs.shape[3]
    nrhs = rhs.shape[4]
    row_count = lax.axis_size("row")
    col_count = lax.axis_size("col")
    groups = col_count // steps
    row_pos = lax.axis_index("row")
    col_pos = lax.axis_index("col")
    member = col_pos // groups
    group = col_pos % groups
    share = width // col_count
    top = steps - 1
    me = row_pos * col_count + col_pos

    def dev(row, mem, grp):
        return row * col_count + mem * groups + grp

    def line(g, mem):
        return dev(g // groups, mem, g % groups)

    low_homes = (line(0, 0), line(1, 0))
    high_homes = (line(2, top - 1), line(3, top))

    def send(x, pairs):
        def twin(i):
            return i + col_count if (i // col_count) % 2 == 0 else i - col_count

        onward = dict(pairs)
        taken = set(onward) | set(onward.values())
        for start in sorted(set(onward) - set(onward.values())):
            stop = onward[start]
            while stop in onward:
                stop = onward[stop]
            back = [twin(stop), twin(start)]
            if twin(start) == stop or taken & set(back):
                onward[stop] = start
            else:
                onward[stop], onward[back[0]], onward[back[1]] = back[0], back[1], start
                taken |= set(back)
        left = []
        for i in range(row_count * col_count):
            if i not in onward:
                if twin(i) in taken:
                    left.append(i)
                else:
                    onward[i] = twin(i)
        paired = [i for i in sorted(onward) if onward[i] == twin(i) and i not in taken]
        for i in left:
            j = min(paired, key=lambda j: (j % col_count != i % col_count, abs(j - i)))
            onward[i], onward[j] = onward[j], i
            paired.remove(j)
        return lax.ppermute(x, AXES, sorted(onward.items()))

    def send_some(x, pairs):
        return lax.ppermute(x, AXES, pairs)

    def chosen(pairs, new, old):
        here = functools.reduce(jnp.logical_or, [me == d for _, d in pairs])
        return jnp.where(here, new, old)

    vmem = pl.BlockSpec(memory_space=VMEM)
    hbm = pl.BlockSpec(memory_space=pltpu.HBM)

    held_factor = pltpu.with_memory_space_constraint(factor, pltpu.HBM)
    held_inverses = pltpu.with_memory_space_constraint(inverses, pltpu.HBM)

    half = jax.ShapeDtypeStruct((2, width, width), jnp.bfloat16)
    near, mine = pl.pallas_call(
        fetch_kernel,
        in_specs=[hbm] * 2,
        out_specs=[vmem] * 2,
        out_shape=[
            jax.ShapeDtypeStruct((width, width), F32), jax.ShapeDtypeStruct((quarter, nrhs), F32)
        ],
        scratch_shapes=[pltpu.SemaphoreType.DMA((2,))],
        compiler_params=PARAMS,
        cost_estimate=CHEAP,
        name="fetch",
    )(held_factor, pltpu.with_memory_space_constraint(rhs, pltpu.HBM))
    ready = pl.pallas_call(
        functools.partial(ready_kernel, low_homes, col_count),
        in_specs=[hbm],
        out_specs=[vmem] * 2,
        out_shape=[half] * 2,
        scratch_shapes=[VMEM((2, width, width), F32), pltpu.SemaphoreType.DMA((2,))],
        compiler_params=PARAMS,
        cost_estimate=CHEAP,
        name="ready",
    )(held_inverses)
    gathered = [
        send(
            mine,
            [(line(g, j), line(g, 0)) for g in (0, 1)]
            + [(line(2, (top - 1 - j) % steps), high_homes[0]), (line(3, top - j), high_homes[1])],
        )
        for j in range(1, steps)
    ]
    la = send(near, [(line(1, 0), low_homes[0])])
    ly = send_some(near, [(line(2, 1), low_homes[0]), (line(3, 1), low_homes[1])])

    vector = VMEM((nrhs, width), F32)
    order = ((low_homes[1], (0, 1, 2, 3)), (high_homes[0], (2, 1, 0, 3)), (high_homes[1], (3, 2, 1, 0)))
    turned = pl.pallas_call(
        functools.partial(turn_kernel, order, low_homes[0], col_count),
        in_specs=[vmem] * 6,
        out_specs=vmem,
        out_shape=vector,
        compiler_params=PARAMS,
        cost_estimate=CHEAP,
        name="turn",
    )(mine, *gathered, *ready)
    swapped = send(turned, [low_homes, low_homes[::-1], high_homes])
    later = lax.optimization_barrier((near, turned))[0]
    last_block = send_some(later, [(line(3, 2), high_homes[1])])
    last_block = pltpu.with_memory_space_constraint(last_block, pltpu.HBM)
    lx = send(later, [(line(2, 0), low_homes[0]), (line(3, 0), low_homes[1])])
    s_0, s_1 = pl.pallas_call(
        functools.partial(low_kernel, low_homes, col_count),
        in_specs=[vmem] * 6 + [pl.BlockSpec(memory_space=pl.ANY)],
        out_specs=[vmem] * 2,
        out_shape=[vector] * 2,
        compiler_params=PARAMS,
        cost_estimate=CHEAP,
        name="solve_low",
    )(turned, swapped, near, la, *ready, ly)
    w = pl.pallas_call(
        functools.partial(reduce_kernel, low_homes, col_count),
        in_specs=[vmem] * 2 + [pl.BlockSpec(memory_space=pl.ANY)] * 2,
        out_specs=vmem,
        out_shape=vector,
        scratch_shapes=[VMEM((2, width, width), F32), pltpu.SemaphoreType.DMA((2,))],
        compiler_params=PARAMS,
        cost_estimate=CHEAP,
        name="reduce_low",
    )(s_0, s_1, lx, ly)
    w_1 = send(w, [(low_homes[0], high_homes[1])])
    w_2 = send(w, [(low_homes[1], high_homes[1]), (low_homes[0], high_homes[0])])
    first_slots, second_slots = ((3, 0, 3, 0), (2, 2, 1, 1)), ((0, 1, 2, 3), (1, 3, 0, 2))
    s_high = pl.pallas_call(
        functools.partial(high_kernel, high_homes, col_count),
        in_specs=[vmem] * 4 + [hbm, pl.BlockSpec(memory_space=pl.ANY)],
        out_specs=vmem,
        out_shape=vector,
        scratch_shapes=[
            VMEM((2, width, width), F32), VMEM((width, width), F32), pltpu.SemaphoreType.DMA((3,))
        ],
        compiler_params=PARAMS,
        cost_estimate=CHEAP,
        name="solve_high",
    )(turned, swapped, w_1, w_2, held_inverses, last_block)

    def spread(s, homes):
        have = {k: list(homes[k]) for k in homes}
        todo = {
            k: sorted(
                [
                    (r, g) for r in range(row_count) for g in range(groups)
                    if r % 2 == homes[k][0][0] % 2 and (r, g) not in homes[k]
                ],
                key=lambda spot: -(spot[0] != homes[k][0][0]) - (spot[1] != homes[k][0][1]),
            )
            for k in homes
        }
        fan = 1 if all(len(spots) > 1 for spots in homes.values()) else 3
        firsts = [(0, dev(r, k, g)) for k in homes for r, g in homes[k]]
        far = None
        while any(todo.values()):
            held = s if far is None else chosen(firsts, s, far)
            rounds = [[] for _ in range(fan)]
            for k in homes:
                spots = list(have[k])
                for pairs in rounds:
                    for a in spots:
                        if todo[k]:
                            b = todo[k].pop()
                            have[k].append(b)
                            pairs.append((dev(a[0], k, a[1]), dev(b[0], k, b[1])))
            for pairs in rounds:
                if pairs:
                    got = send(held, pairs)
                    far = got if far is None else chosen(pairs, got, far)
        twins = {
            k: [(dev(r, k, g), dev(r ^ 1, k, g)) for r, g in have[k]] for k in homes
        }
        near_twins = [pair for k in homes for pair in twins[k][: len(homes[k])]]
        far_twins = [pair for k in homes for pair in twins[k][len(homes[k]):]]
        return s, far, send(s, near_twins), send(far, far_twins)

    spots = [(g // groups, g % groups) for g in range(4)]
    homes = (tuple(spots[:2]), (spots[1],), (spots[2],), (spots[3],))
    moved = send(s_1, [(line(1, 0), line(1, 1))])
    s_low = jnp.where(member == 0, s_0, moved)
    ways = spread(s_low, {0: homes[0], 1: homes[1]}) + spread(s_high, {2: homes[2], 3: homes[3]})

    far_share, part, longer = [
        jax.ShapeDtypeStruct((n, nrhs), F32)
        for n in (share, blocks * quarter + share, blocks * quarter + share + 8)
    ]

    def update(name, shapes, slots):
        return pl.pallas_call(
            functools.partial(update_kernel, (groups, row_count, share, homes, slots, blocks)),
            in_specs=[vmem] * 8 + [hbm],
            out_specs=[vmem] * len(shapes),
            out_shape=shapes,
            scratch_shapes=[
                VMEM((nrhs, width), F32),
                VMEM((quarter, nrhs), F32),
                VMEM((blocks, width, 2 * quarter), F32),
                pltpu.SemaphoreType.DMA((2 * blocks,)),
            ],
            compiler_params=PARAMS,
            cost_estimate=CHEAP,
            name=name,
        )(*ways, held_factor)

    part_a, part_b, far = update(
        "update_first", [part, longer, far_share], first_slots + ((3, 0, 0, 0),)
    )
    own, part_c = update("update_second", [part, longer], second_slots)
    across = [(r, g) for r in range(row_count) for g in range(groups)]

    def route(*hops):
        return [(dev(r, a, g), dev(r, b, g)) for a, b in hops for r, g in across]

    got_1 = send(part_a, route((3, 2), (0, 1), (1, 0), (2, 3)))
    got_4 = send(part_b, route((2, 1), (1, 2)))
    got_2 = send(part_b, route((3, 1), (1, 0), (0, 2), (2, 3)))
    got_3 = send_some(part_c, route((3, 2), (0, 1)))
    joined = pl.pallas_call(
        functools.partial(join_kernel, (groups, share)),
        in_specs=[vmem] * 2,
        out_specs=vmem,
        out_shape=part,
        compiler_params=PARAMS,
        cost_estimate=CHEAP,
        name="join",
    )(part_c, got_1)
    joined = send_some(joined, route((2, 0), (1, 3)))
    far = send(far, route((3, 0), (0, 3), (1, 2), (2, 1)))

    solved, remaining = pl.pallas_call(
        functools.partial(last_kernel, groups),
        in_specs=[vmem] * 8,
        out_specs=[vmem] * 2,
        out_shape=[
            jax.ShapeDtypeStruct((steps, share, nrhs), F32),
            jax.ShapeDtypeStruct((blocks, quarter, nrhs), F32),
        ],
        compiler_params=PARAMS,
        cost_estimate=CHEAP,
        name="add_up",
    )(rhs[:, 0, 0], own, got_1, got_2, got_3, got_4, joined, far)
    return solved, remaining[:, None, None]


def solution(mesh):
    in_specs = (P(None, "row", "col", None, None), P(None, "row", "col", None, None), P())
    out_specs = (P(None, "col", None), P(None, "row", "col", None, None))
    return jax.shard_map(
        on_device, mesh=mesh, in_specs=in_specs, out_specs=out_specs, check_vma=False
    )
```

```python
import functools

import jax
import jax.numpy as jnp
from jax import lax
from jax.experimental import pallas as pl
from jax.experimental.pallas import tpu as pltpu
from jax.sharding import PartitionSpec as P

AXES = ("row", "col")
F32 = jnp.float32
VMEM = pltpu.VMEM
PARAMS = pltpu.CompilerParams(vmem_limit_bytes=12 * 2**20)
CHEAP = pl.CostEstimate(flops=1000, bytes_accessed=1000, transcendentals=0)


def split(x):
    high = x.astype(jnp.bfloat16)
    return high, (x - high.astype(F32)).astype(jnp.bfloat16)


def product(a, b, transposed=False):
    b_high, b_low = b if isinstance(b, tuple) else split(b)
    dims = (((1,), (1 if transposed else 0,)), ((), ()))
    a_high, a_low = a if isinstance(a, tuple) else split(a)
    n = a_high.shape[0]
    both = lax.dot_general(
        jnp.concatenate([a_high, a_low], 0), b_high, dims, preferred_element_type=F32
    )
    cross = lax.dot_general(a_high, b_low, dims, preferred_element_type=F32)
    return both[:n] + (both[n:] + cross)


def position(col_count):
    return lax.axis_index("row") * col_count + lax.axis_index("col")


def fetch_kernel(factor, rhs, near, mine, sem):
    copies = [
        pltpu.make_async_copy(rhs.at[0, 0, 0], mine, sem.at[0]),
        pltpu.make_async_copy(factor.at[0, 0, 0], near, sem.at[1]),
    ]
    for copy in copies:
        copy.start()
    for copy in copies:
        copy.wait()


def ready_kernel(solvers, col_count, inverses, high, low, inv, sem):
    me = position(col_count)

    @pl.when((me == solvers[0]) | (me == solvers[1]))
    def _():
        copies = [pltpu.make_async_copy(inverses.at[i], inv.at[i], sem.at[i]) for i in range(2)]
        for copy in copies:
            copy.start()
        for i, copy in enumerate(copies):
            copy.wait()
            high[i], low[i] = split(inv[i])


def piece_columns(groups, table, quarter):
    member = lax.axis_index("col") // groups
    to = functools.reduce(jnp.add, [jnp.where(member == m, p, 0) for m, p in enumerate(table)])
    return pl.ds(pl.multiple_of(to * quarter, quarter), quarter)


def column_copies(groups, table_pair, panel, tiles, sems):
    quarter = tiles.shape[2] // 2
    return [
        [
            pltpu.make_async_copy(
                panel.at[r, 0, 0, :, piece_columns(groups, table, quarter)],
                tiles.at[r, :, pl.ds(i * quarter, quarter)],
                sems.at[2 * r + i],
            )
            for i, table in enumerate(table_pair)
        ]
        for r in range(tiles.shape[0])
    ]


def turn_kernel(order, solver, col_count, own, g1, g2, g3, high, low, out):
    me = position(col_count)

    def joined(pieces):
        return jnp.concatenate([piece[...].T for piece in pieces], axis=1)

    @pl.when(me == solver)
    def _():
        out[...] = product(joined((own, g1, g2, g3)), (high[0], low[0]), True)

    for device, places in order:
        @pl.when(me == device)
        def _(places=places):
            refs = (own, g1, g2, g3)
            out[...] = joined([refs[i] for i in places])


def low_kernel(homes, col_count, out, swapped, near, la, high, low, ly, s_a, s_b):
    del ly
    me = position(col_count)

    def work(first, right, block):
        s_a[...] = first[...]
        left = right[...] - product(first[...], block[...])
        s_b[...] = product(left, (high[1], low[1]), True)

    @pl.when(me == homes[0])
    def _():
        work(out, swapped, la)

    @pl.when(me == homes[1])
    def _():
        work(swapped, out, near)


def reduce_kernel(homes, col_count, s_a, s_b, lx, ly, w, block, sem):
    me = position(col_count)

    @pl.when((me == homes[0]) | (me == homes[1]))
    def _():
        copies = [pltpu.make_async_copy(ref, block.at[i], sem.at[i]) for i, ref in enumerate((ly, lx))]
        for copy in copies:
            copy.start()
        copies[0].wait()
        later = product(s_b[...], block[0])
        copies[1].wait()
        w[...] = product(s_a[...], block[1]) + later


def high_kernel(homes, col_count, own, swapped, w_1, w_2, inverses, last_block, s, inv, block, sem):
    me = position(col_count)
    copies = [pltpu.make_async_copy(inverses.at[2 + i], inv.at[i], sem.at[i]) for i in range(2)]
    copies.append(pltpu.make_async_copy(last_block, block, sem.at[2]))

    @pl.when(me == homes[0])
    def _():
        copies[0].start()
        right = own[...] - w_2[...]
        copies[0].wait()
        s[...] = product(right, inv[0], True)

    @pl.when(me == homes[1])
    def _():
        for copy in copies:
            copy.start()
        right = swapped[...] - w_1[...]
        copies[0].wait()
        first = product(right, inv[0], True)
        copies[2].wait()
        right = own[...] - w_2[...] - product(first, block[...])
        copies[1].wait()
        s[...] = product(right, inv[1], True)


def update_kernel(cfg, *refs):
    groups, row_count, share, homes, slots, blocks = cfg
    steps = len(homes)
    ways, panel, refs = refs[:8], refs[8], refs[9:]
    outs, shares, (s, turned, tiles, sems) = refs[:2], refs[2:-4], refs[-4:]
    copies = column_copies(groups, slots[:2], panel, tiles, sems)
    for pair in copies:
        for copy in pair:
            copy.start()
    quarter = turned.shape[0]
    row = lax.axis_index("row")
    col = lax.axis_index("col")
    member = col // groups
    group = col % groups
    columns = [piece_columns(groups, table, quarter) for table in slots]

    for half in range(2):
        planes = [m for m in range(steps) if m // (steps // 2) == half]

        def among(flip):
            return functools.reduce(jnp.logical_or, [
                (member == m) & (row == (r ^ flip)) & (group == g)
                for m in planes for r, g in homes[m]
            ])

        first, first_twin = among(0), among(1)
        here = functools.reduce(jnp.logical_or, [member == m for m in planes])
        same = here & (lax.rem(row, 2) == homes[planes[0]][0][0] % 2)
        other = here & (lax.rem(row, 2) != homes[planes[0]][0][0] % 2)
        roles = (
            first, same & jnp.logical_not(first), first_twin, other & jnp.logical_not(first_twin)
        )
        for way, role in zip(ways[4 * half:], roles):
            @pl.when(role)
            def _(src=way):
                s[...] = src[...]

    parts = split(s[...])
    for r in range(blocks):
        for copy in copies[r]:
            copy.wait()
        block_id = (r * row_count + row) * groups + group
        keep = (block_id > member).astype(F32)
        full = product(parts, tiles[r]) * keep
        for i, out in enumerate(outs):
            out[pl.ds(r * quarter, quarter), :] = full[:, i * quarter: (i + 1) * quarter]
    for place, out in zip(columns, outs + shares):
        turned[...] = s[:, place].T
        rows = pl.ds(pl.multiple_of(group * share, share), share)
        first = blocks * quarter if out.shape[0] > share else 0
        out[pl.ds(first, share), :] = turned[rows, :]


def join_kernel(cfg, mine, theirs, out):
    groups, share = cfg
    last = out.shape[0] - share
    member = lax.axis_index("col") // groups

    @pl.when((member == 1) | (member == 2))
    def _():
        out[:last, :] = mine[:last, :] + theirs[:last, :]
        out[last:, :] = mine[pl.ds(last, share), :]


def last_kernel(groups, rhs, own, got_1, got_2, got_3, got_4, joined, far, solved, out):
    blocks, quarter = rhs.shape[0], rhs.shape[1]
    last, share = blocks * quarter, solved.shape[1]
    member = lax.axis_index("col") // groups

    def finish(at, *parts):
        @pl.when(member == at)
        def _():
            for r in range(blocks):
                rows = pl.ds(r * quarter, quarter)
                total = functools.reduce(jnp.add, [part[rows, :] for part, _ in parts])
                out[r] = rhs[r] - total.T
            for part, k in parts:
                solved[k] = part[pl.ds(last, share), :]
            if at in (0, 3):
                solved[3 - at] = far[...]

    finish(0, (own, 0), (got_1, 1), (joined, 2))
    finish(1, (own, 1), (got_2, 3), (got_3, 0), (got_4, 2))
    finish(2, (own, 2), (got_2, 0), (got_3, 3), (got_4, 1))
    finish(3, (own, 3), (got_1, 2), (joined, 1))


def on_device(factor, rhs, inverses):
    steps = inverses.shape[0]
    blocks = factor.shape[0]
    width = factor.shape[3]
    quarter = rhs.shape[3]
    nrhs = rhs.shape[4]
    row_count = lax.axis_size("row")
    col_count = lax.axis_size("col")
    groups = col_count // steps
    row_pos = lax.axis_index("row")
    col_pos = lax.axis_index("col")
    member = col_pos // groups
    group = col_pos % groups
    share = width // col_count
    top = steps - 1
    me = row_pos * col_count + col_pos

    def dev(row, mem, grp):
        return row * col_count + mem * groups + grp

    def line(g, mem):
        return dev(g // groups, mem, g % groups)

    low_homes = (line(0, 0), line(1, 0))
    high_homes = (line(2, top - 1), line(3, top))

    def send(x, pairs):
        def twin(i):
            return i + col_count if (i // col_count) % 2 == 0 else i - col_count

        onward = dict(pairs)
        taken = set(onward) | set(onward.values())
        for start in sorted(set(onward) - set(onward.values())):
            stop = onward[start]
            while stop in onward:
                stop = onward[stop]
            back = [twin(stop), twin(start)]
            if twin(start) == stop or taken & set(back):
                onward[stop] = start
            else:
                onward[stop], onward[back[0]], onward[back[1]] = back[0], back[1], start
                taken |= set(back)
        left = []
        for i in range(row_count * col_count):
            if i not in onward:
                if twin(i) in taken:
                    left.append(i)
                else:
                    onward[i] = twin(i)
        paired = [i for i in sorted(onward) if onward[i] == twin(i) and i not in taken]
        for i in left:
            j = min(paired, key=lambda j: (j % col_count != i % col_count, abs(j - i)))
            onward[i], onward[j] = onward[j], i
            paired.remove(j)
        return lax.ppermute(x, AXES, sorted(onward.items()))

    def send_some(x, pairs):
        return lax.ppermute(x, AXES, pairs)

    def chosen(pairs, new, old):
        here = functools.reduce(jnp.logical_or, [me == d for _, d in pairs])
        return jnp.where(here, new, old)

    vmem = pl.BlockSpec(memory_space=VMEM)
    hbm = pl.BlockSpec(memory_space=pltpu.HBM)

    held_factor = pltpu.with_memory_space_constraint(factor, pltpu.HBM)
    held_inverses = pltpu.with_memory_space_constraint(inverses, pltpu.HBM)

    half = jax.ShapeDtypeStruct((2, width, width), jnp.bfloat16)
    near, mine = pl.pallas_call(
        fetch_kernel,
        in_specs=[hbm] * 2,
        out_specs=[vmem] * 2,
        out_shape=[
            jax.ShapeDtypeStruct((width, width), F32), jax.ShapeDtypeStruct((quarter, nrhs), F32)
        ],
        scratch_shapes=[pltpu.SemaphoreType.DMA((2,))],
        compiler_params=PARAMS,
        cost_estimate=CHEAP,
        name="fetch",
    )(held_factor, pltpu.with_memory_space_constraint(rhs, pltpu.HBM))
    ready = pl.pallas_call(
        functools.partial(ready_kernel, low_homes, col_count),
        in_specs=[hbm],
        out_specs=[vmem] * 2,
        out_shape=[half] * 2,
        scratch_shapes=[VMEM((2, width, width), F32), pltpu.SemaphoreType.DMA((2,))],
        compiler_params=PARAMS,
        cost_estimate=CHEAP,
        name="ready",
    )(held_inverses)
    gathered = [
        send(
            mine,
            [(line(g, j), line(g, 0)) for g in (0, 1)]
            + [(line(2, (top - 1 - j) % steps), high_homes[0]), (line(3, top - j), high_homes[1])],
        )
        for j in range(1, steps)
    ]
    la = send(near, [(line(1, 0), low_homes[0])])
    ly = send_some(near, [(line(2, 1), low_homes[0]), (line(3, 1), low_homes[1])])

    vector = VMEM((nrhs, width), F32)
    order = ((low_homes[1], (0, 1, 2, 3)), (high_homes[0], (2, 1, 0, 3)), (high_homes[1], (3, 2, 1, 0)))
    turned = pl.pallas_call(
        functools.partial(turn_kernel, order, low_homes[0], col_count),
        in_specs=[vmem] * 6,
        out_specs=vmem,
        out_shape=vector,
        compiler_params=PARAMS,
        cost_estimate=CHEAP,
        name="turn",
    )(mine, *gathered, *ready)
    swapped = send(turned, [low_homes, low_homes[::-1], high_homes])
    later = lax.optimization_barrier((near, turned))[0]
    last_block = send_some(later, [(line(3, 2), high_homes[1])])
    last_block = pltpu.with_memory_space_constraint(last_block, pltpu.HBM)
    lx = send(later, [(line(2, 0), low_homes[0]), (line(3, 0), low_homes[1])])
    lx = pltpu.with_memory_space_constraint(lx, pltpu.HBM)
    s_0, s_1 = pl.pallas_call(
        functools.partial(low_kernel, low_homes, col_count),
        in_specs=[vmem] * 6 + [pl.BlockSpec(memory_space=pl.ANY)],
        out_specs=[vmem] * 2,
        out_shape=[vector] * 2,
        compiler_params=PARAMS,
        cost_estimate=CHEAP,
        name="solve_low",
    )(turned, swapped, near, la, *ready, ly)
    w = pl.pallas_call(
        functools.partial(reduce_kernel, low_homes, col_count),
        in_specs=[vmem] * 2 + [pl.BlockSpec(memory_space=pl.ANY)] * 2,
        out_specs=vmem,
        out_shape=vector,
        scratch_shapes=[VMEM((2, width, width), F32), pltpu.SemaphoreType.DMA((2,))],
        compiler_params=PARAMS,
        cost_estimate=CHEAP,
        name="reduce_low",
    )(s_0, s_1, lx, ly)
    w_1 = send(w, [(low_homes[0], high_homes[1])])
    w_2 = send(w, [(low_homes[1], high_homes[1]), (low_homes[0], high_homes[0])])
    first_slots, second_slots = ((3, 0, 3, 0), (2, 2, 1, 1)), ((0, 1, 2, 3), (1, 3, 0, 2))
    s_high = pl.pallas_call(
        functools.partial(high_kernel, high_homes, col_count),
        in_specs=[vmem] * 4 + [hbm, pl.BlockSpec(memory_space=pl.ANY)],
        out_specs=vmem,
        out_shape=vector,
        scratch_shapes=[
            VMEM((2, width, width), F32), VMEM((width, width), F32), pltpu.SemaphoreType.DMA((3,))
        ],
        compiler_params=PARAMS,
        cost_estimate=CHEAP,
        name="solve_high",
    )(turned, swapped, w_1, w_2, held_inverses, last_block)

    def spread(s, homes):
        have = {k: list(homes[k]) for k in homes}
        todo = {
            k: sorted(
                [
                    (r, g) for r in range(row_count) for g in range(groups)
                    if r % 2 == homes[k][0][0] % 2 and (r, g) not in homes[k]
                ],
                key=lambda spot: -(spot[0] != homes[k][0][0]) - (spot[1] != homes[k][0][1]),
            )
            for k in homes
        }
        fan = 1 if all(len(spots) > 1 for spots in homes.values()) else 3
        firsts = [(0, dev(r, k, g)) for k in homes for r, g in homes[k]]
        far = None
        while any(todo.values()):
            held = s if far is None else chosen(firsts, s, far)
            rounds = [[] for _ in range(fan)]
            for k in homes:
                spots = list(have[k])
                for pairs in rounds:
                    for a in spots:
                        if todo[k]:
                            b = todo[k].pop()
                            have[k].append(b)
                            pairs.append((dev(a[0], k, a[1]), dev(b[0], k, b[1])))
            for pairs in rounds:
                if pairs:
                    got = send(held, pairs)
                    far = got if far is None else chosen(pairs, got, far)
        twins = {
            k: [(dev(r, k, g), dev(r ^ 1, k, g)) for r, g in have[k]] for k in homes
        }
        near_twins = [pair for k in homes for pair in twins[k][: len(homes[k])]]
        far_twins = [pair for k in homes for pair in twins[k][len(homes[k]):]]
        return s, far, send(s, near_twins), send(far, far_twins)

    spots = [(g // groups, g % groups) for g in range(4)]
    homes = (tuple(spots[:2]), (spots[1],), (spots[2],), (spots[3],))
    moved = send(s_1, [(line(1, 0), line(1, 1))])
    s_low = jnp.where(member == 0, s_0, moved)
    ways = spread(s_low, {0: homes[0], 1: homes[1]}) + spread(s_high, {2: homes[2], 3: homes[3]})

    far_share, part, longer = [
        jax.ShapeDtypeStruct((n, nrhs), F32)
        for n in (share, blocks * quarter + share, blocks * quarter + share + 8)
    ]

    def update(name, shapes, slots):
        return pl.pallas_call(
            functools.partial(update_kernel, (groups, row_count, share, homes, slots, blocks)),
            in_specs=[vmem] * 8 + [hbm],
            out_specs=[vmem] * len(shapes),
            out_shape=shapes,
            scratch_shapes=[
                VMEM((nrhs, width), F32),
                VMEM((quarter, nrhs), F32),
                VMEM((blocks, width, 2 * quarter), F32),
                pltpu.SemaphoreType.DMA((2 * blocks,)),
            ],
            compiler_params=PARAMS,
            cost_estimate=CHEAP,
            name=name,
        )(*ways, held_factor)

    part_a, part_b, far = update(
        "update_first", [part, longer, far_share], first_slots + ((3, 0, 0, 0),)
    )
    own, part_c = update("update_second", [part, longer], second_slots)
    across = [(r, g) for r in range(row_count) for g in range(groups)]

    def route(*hops):
        return [(dev(r, a, g), dev(r, b, g)) for a, b in hops for r, g in across]

    got_1 = send(part_a, route((3, 2), (0, 1), (1, 0), (2, 3)))
    got_4 = send(part_b, route((2, 1), (1, 2)))
    got_2 = send(part_b, route((3, 1), (1, 0), (0, 2), (2, 3)))
    got_3 = send_some(part_c, route((3, 2), (0, 1)))
    joined = pl.pallas_call(
        functools.partial(join_kernel, (groups, share)),
        in_specs=[vmem] * 2,
        out_specs=vmem,
        out_shape=part,
        compiler_params=PARAMS,
        cost_estimate=CHEAP,
        name="join",
    )(part_c, got_1)
    joined = send_some(joined, route((2, 0), (1, 3)))
    far = send(far, route((3, 0), (0, 3), (1, 2), (2, 1)))

    solved, remaining = pl.pallas_call(
        functools.partial(last_kernel, groups),
        in_specs=[vmem] * 8,
        out_specs=[vmem] * 2,
        out_shape=[
            jax.ShapeDtypeStruct((steps, share, nrhs), F32),
            jax.ShapeDtypeStruct((blocks, quarter, nrhs), F32),
        ],
        compiler_params=PARAMS,
        cost_estimate=CHEAP,
        name="add_up",
    )(rhs[:, 0, 0], own, got_1, got_2, got_3, got_4, joined, far)
    return solved, remaining[:, None, None]


def solution(mesh):
    in_specs = (P(None, "row", "col", None, None), P(None, "row", "col", None, None), P())
    out_specs = (P(None, "col", None), P(None, "row", "col", None, None))
    return jax.shard_map(
        on_device, mesh=mesh, in_specs=in_specs, out_specs=out_specs, check_vma=False
    )
```

```python
import functools

import jax
import jax.numpy as jnp
from jax import lax
from jax.experimental import pallas as pl
from jax.experimental.pallas import tpu as pltpu
from jax.sharding import PartitionSpec as P

AXES = ("row", "col")
F32 = jnp.float32
VMEM = pltpu.VMEM
PARAMS = pltpu.CompilerParams(vmem_limit_bytes=12 * 2**20)
CHEAP = pl.CostEstimate(flops=1000, bytes_accessed=1000, transcendentals=0)


def split(x):
    high = x.astype(jnp.bfloat16)
    return high, (x - high.astype(F32)).astype(jnp.bfloat16)


def product(a, b, transposed=False):
    b_high, b_low = b if isinstance(b, tuple) else split(b)
    dims = (((1,), (1 if transposed else 0,)), ((), ()))
    a_high, a_low = a if isinstance(a, tuple) else split(a)
    n = a_high.shape[0]
    both = lax.dot_general(
        jnp.concatenate([a_high, a_low], 0), b_high, dims, preferred_element_type=F32
    )
    cross = lax.dot_general(a_high, b_low, dims, preferred_element_type=F32)
    return both[:n] + (both[n:] + cross)


def position(col_count):
    return lax.axis_index("row") * col_count + lax.axis_index("col")


def fetch_kernel(factor, rhs, near, mine, sem):
    copies = [
        pltpu.make_async_copy(rhs.at[0, 0, 0], mine, sem.at[0]),
        pltpu.make_async_copy(factor.at[0, 0, 0], near, sem.at[1]),
    ]
    for copy in copies:
        copy.start()
    for copy in copies:
        copy.wait()


def ready_kernel(solvers, col_count, inverses, high, low, inv, sem):
    me = position(col_count)

    @pl.when((me == solvers[0]) | (me == solvers[1]))
    def _():
        copies = [pltpu.make_async_copy(inverses.at[i], inv.at[i], sem.at[i]) for i in range(2)]
        for copy in copies:
            copy.start()
        for i, copy in enumerate(copies):
            copy.wait()
            high[i], low[i] = split(inv[i])


def piece_columns(groups, table, quarter):
    member = lax.axis_index("col") // groups
    to = functools.reduce(jnp.add, [jnp.where(member == m, p, 0) for m, p in enumerate(table)])
    return pl.ds(pl.multiple_of(to * quarter, quarter), quarter)


def column_copies(groups, table_pair, panel, tiles, sems):
    quarter = tiles.shape[2] // 2
    return [
        [
            pltpu.make_async_copy(
                panel.at[r, 0, 0, :, piece_columns(groups, table, quarter)],
                tiles.at[r, :, pl.ds(i * quarter, quarter)],
                sems.at[2 * r + i],
            )
            for i, table in enumerate(table_pair)
        ]
        for r in range(tiles.shape[0])
    ]


def turn_kernel(order, solver, col_count, own, g1, g2, g3, high, low, out):
    me = position(col_count)

    def joined(pieces):
        return jnp.concatenate([piece[...].T for piece in pieces], axis=1)

    @pl.when(me == solver)
    def _():
        out[...] = product(joined((own, g1, g2, g3)), (high[0], low[0]), True)

    for device, places in order:
        @pl.when(me == device)
        def _(places=places):
            refs = (own, g1, g2, g3)
            out[...] = joined([refs[i] for i in places])


def low_kernel(homes, col_count, out, swapped, near, la, high, low, ly, s_a, s_b):
    del ly
    me = position(col_count)

    def work(first, right, block):
        s_a[...] = first[...]
        left = right[...] - product(first[...], block[...])
        s_b[...] = product(left, (high[1], low[1]), True)

    @pl.when(me == homes[0])
    def _():
        work(out, swapped, la)

    @pl.when(me == homes[1])
    def _():
        work(swapped, out, near)


def reduce_kernel(homes, col_count, s_a, s_b, lx, ly, w, block, sem):
    me = position(col_count)

    @pl.when((me == homes[0]) | (me == homes[1]))
    def _():
        copies = [pltpu.make_async_copy(ref, block.at[i], sem.at[i]) for i, ref in enumerate((ly, lx))]
        for copy in copies:
            copy.start()
        copies[1].wait()
        sooner = product(s_a[...], block[1])
        copies[0].wait()
        w[...] = sooner + product(s_b[...], block[0])


def high_kernel(homes, col_count, own, swapped, w_1, w_2, inverses, last_block, s, inv, block, sem):
    me = position(col_count)
    copies = [pltpu.make_async_copy(inverses.at[2 + i], inv.at[i], sem.at[i]) for i in range(2)]
    copies.append(pltpu.make_async_copy(last_block, block, sem.at[2]))

    @pl.when(me == homes[0])
    def _():
        copies[0].start()
        right = own[...] - w_2[...]
        copies[0].wait()
        s[...] = product(right, inv[0], True)

    @pl.when(me == homes[1])
    def _():
        for copy in copies:
            copy.start()
        right = swapped[...] - w_1[...]
        copies[0].wait()
        first = product(right, inv[0], True)
        copies[2].wait()
        right = own[...] - w_2[...] - product(first, block[...])
        copies[1].wait()
        s[...] = product(right, inv[1], True)


def update_kernel(cfg, *refs):
    groups, row_count, share, homes, slots, blocks = cfg
    steps = len(homes)
    ways, panel, refs = refs[:8], refs[8], refs[9:]
    outs, shares, (s, turned, tiles, sems) = refs[:2], refs[2:-4], refs[-4:]
    copies = column_copies(groups, slots[:2], panel, tiles, sems)
    for pair in copies:
        for copy in pair:
            copy.start()
    quarter = turned.shape[0]
    row = lax.axis_index("row")
    col = lax.axis_index("col")
    member = col // groups
    group = col % groups
    columns = [piece_columns(groups, table, quarter) for table in slots]

    for half in range(2):
        planes = [m for m in range(steps) if m // (steps // 2) == half]

        def among(flip):
            return functools.reduce(jnp.logical_or, [
                (member == m) & (row == (r ^ flip)) & (group == g)
                for m in planes for r, g in homes[m]
            ])

        first, first_twin = among(0), among(1)
        here = functools.reduce(jnp.logical_or, [member == m for m in planes])
        same = here & (lax.rem(row, 2) == homes[planes[0]][0][0] % 2)
        other = here & (lax.rem(row, 2) != homes[planes[0]][0][0] % 2)
        roles = (
            first, same & jnp.logical_not(first), first_twin, other & jnp.logical_not(first_twin)
        )
        for way, role in zip(ways[4 * half:], roles):
            @pl.when(role)
            def _(src=way):
                s[...] = src[...]

    parts = split(s[...])
    for r in range(blocks):
        for copy in copies[r]:
            copy.wait()
        block_id = (r * row_count + row) * groups + group
        keep = (block_id > member).astype(F32)
        full = product(parts, tiles[r]) * keep
        for i, out in enumerate(outs):
            out[pl.ds(r * quarter, quarter), :] = full[:, i * quarter: (i + 1) * quarter]
    for place, out in zip(columns, outs + shares):
        turned[...] = s[:, place].T
        rows = pl.ds(pl.multiple_of(group * share, share), share)
        first = blocks * quarter if out.shape[0] > share else 0
        out[pl.ds(first, share), :] = turned[rows, :]


def join_kernel(cfg, mine, theirs, out):
    groups, share = cfg
    last = out.shape[0] - share
    member = lax.axis_index("col") // groups

    @pl.when((member == 1) | (member == 2))
    def _():
        out[:last, :] = mine[:last, :] + theirs[:last, :]
        out[last:, :] = mine[pl.ds(last, share), :]


def last_kernel(groups, rhs, own, got_1, got_2, got_3, got_4, joined, far, solved, out):
    blocks, quarter = rhs.shape[0], rhs.shape[1]
    last, share = blocks * quarter, solved.shape[1]
    member = lax.axis_index("col") // groups

    def finish(at, *parts):
        @pl.when(member == at)
        def _():
            for r in range(blocks):
                rows = pl.ds(r * quarter, quarter)
                total = functools.reduce(jnp.add, [part[rows, :] for part, _ in parts])
                out[r] = rhs[r] - total.T
            for part, k in parts:
                solved[k] = part[pl.ds(last, share), :]
            if at in (0, 3):
                solved[3 - at] = far[...]

    finish(0, (own, 0), (got_1, 1), (joined, 2))
    finish(1, (own, 1), (got_2, 3), (got_3, 0), (got_4, 2))
    finish(2, (own, 2), (got_2, 0), (got_3, 3), (got_4, 1))
    finish(3, (own, 3), (got_1, 2), (joined, 1))


def on_device(factor, rhs, inverses):
    steps = inverses.shape[0]
    blocks = factor.shape[0]
    width = factor.shape[3]
    quarter = rhs.shape[3]
    nrhs = rhs.shape[4]
    row_count = lax.axis_size("row")
    col_count = lax.axis_size("col")
    groups = col_count // steps
    row_pos = lax.axis_index("row")
    col_pos = lax.axis_index("col")
    member = col_pos // groups
    group = col_pos % groups
    share = width // col_count
    top = steps - 1
    me = row_pos * col_count + col_pos

    def dev(row, mem, grp):
        return row * col_count + mem * groups + grp

    def line(g, mem):
        return dev(g // groups, mem, g % groups)

    low_homes = (line(0, 0), line(1, 0))
    high_homes = (line(2, top - 1), line(3, top))

    def send(x, pairs):
        def twin(i):
            return i + col_count if (i // col_count) % 2 == 0 else i - col_count

        onward = dict(pairs)
        taken = set(onward) | set(onward.values())
        for start in sorted(set(onward) - set(onward.values())):
            stop = onward[start]
            while stop in onward:
                stop = onward[stop]
            back = [twin(stop), twin(start)]
            if twin(start) == stop or taken & set(back):
                onward[stop] = start
            else:
                onward[stop], onward[back[0]], onward[back[1]] = back[0], back[1], start
                taken |= set(back)
        left = []
        for i in range(row_count * col_count):
            if i not in onward:
                if twin(i) in taken:
                    left.append(i)
                else:
                    onward[i] = twin(i)
        paired = [i for i in sorted(onward) if onward[i] == twin(i) and i not in taken]
        for i in left:
            j = min(paired, key=lambda j: (j % col_count != i % col_count, abs(j - i)))
            onward[i], onward[j] = onward[j], i
            paired.remove(j)
        return lax.ppermute(x, AXES, sorted(onward.items()))

    def send_some(x, pairs):
        return lax.ppermute(x, AXES, pairs)

    def chosen(pairs, new, old):
        here = functools.reduce(jnp.logical_or, [me == d for _, d in pairs])
        return jnp.where(here, new, old)

    vmem = pl.BlockSpec(memory_space=VMEM)
    hbm = pl.BlockSpec(memory_space=pltpu.HBM)

    held_factor = pltpu.with_memory_space_constraint(factor, pltpu.HBM)
    held_inverses = pltpu.with_memory_space_constraint(inverses, pltpu.HBM)

    half = jax.ShapeDtypeStruct((2, width, width), jnp.bfloat16)
    near, mine = pl.pallas_call(
        fetch_kernel,
        in_specs=[hbm] * 2,
        out_specs=[vmem] * 2,
        out_shape=[
            jax.ShapeDtypeStruct((width, width), F32), jax.ShapeDtypeStruct((quarter, nrhs), F32)
        ],
        scratch_shapes=[pltpu.SemaphoreType.DMA((2,))],
        compiler_params=PARAMS,
        cost_estimate=CHEAP,
        name="fetch",
    )(held_factor, pltpu.with_memory_space_constraint(rhs, pltpu.HBM))
    ready = pl.pallas_call(
        functools.partial(ready_kernel, low_homes, col_count),
        in_specs=[hbm],
        out_specs=[vmem] * 2,
        out_shape=[half] * 2,
        scratch_shapes=[VMEM((2, width, width), F32), pltpu.SemaphoreType.DMA((2,))],
        compiler_params=PARAMS,
        cost_estimate=CHEAP,
        name="ready",
    )(held_inverses)
    gathered = [
        send(
            mine,
            [(line(g, j), line(g, 0)) for g in (0, 1)]
            + [(line(2, (top - 1 - j) % steps), high_homes[0]), (line(3, top - j), high_homes[1])],
        )
        for j in range(1, steps)
    ]
    la = send(near, [(line(1, 0), low_homes[0])])
    ly = send_some(near, [(line(2, 1), low_homes[0]), (line(3, 1), low_homes[1])])

    vector = VMEM((nrhs, width), F32)
    order = ((low_homes[1], (0, 1, 2, 3)), (high_homes[0], (2, 1, 0, 3)), (high_homes[1], (3, 2, 1, 0)))
    turned = pl.pallas_call(
        functools.partial(turn_kernel, order, low_homes[0], col_count),
        in_specs=[vmem] * 6,
        out_specs=vmem,
        out_shape=vector,
        compiler_params=PARAMS,
        cost_estimate=CHEAP,
        name="turn",
    )(mine, *gathered, *ready)
    swapped = send(turned, [low_homes, low_homes[::-1], high_homes])
    later = lax.optimization_barrier((near, turned))[0]
    last_block = send_some(later, [(line(3, 2), high_homes[1])])
    last_block = pltpu.with_memory_space_constraint(last_block, pltpu.HBM)
    lx = send(later, [(line(2, 0), low_homes[0]), (line(3, 0), low_homes[1])])
    ly = pltpu.with_memory_space_constraint(ly, pltpu.HBM)
    s_0, s_1 = pl.pallas_call(
        functools.partial(low_kernel, low_homes, col_count),
        in_specs=[vmem] * 6 + [pl.BlockSpec(memory_space=pl.ANY)],
        out_specs=[vmem] * 2,
        out_shape=[vector] * 2,
        compiler_params=PARAMS,
        cost_estimate=CHEAP,
        name="solve_low",
    )(turned, swapped, near, la, *ready, ly)
    w = pl.pallas_call(
        functools.partial(reduce_kernel, low_homes, col_count),
        in_specs=[vmem] * 2 + [pl.BlockSpec(memory_space=pl.ANY)] * 2,
        out_specs=vmem,
        out_shape=vector,
        scratch_shapes=[VMEM((2, width, width), F32), pltpu.SemaphoreType.DMA((2,))],
        compiler_params=PARAMS,
        cost_estimate=CHEAP,
        name="reduce_low",
    )(s_0, s_1, lx, ly)
    w_1 = send(w, [(low_homes[0], high_homes[1])])
    w_2 = send(w, [(low_homes[1], high_homes[1]), (low_homes[0], high_homes[0])])
    first_slots, second_slots = ((3, 0, 3, 0), (2, 2, 1, 1)), ((0, 1, 2, 3), (1, 3, 0, 2))
    s_high = pl.pallas_call(
        functools.partial(high_kernel, high_homes, col_count),
        in_specs=[vmem] * 4 + [hbm, pl.BlockSpec(memory_space=pl.ANY)],
        out_specs=vmem,
        out_shape=vector,
        scratch_shapes=[
            VMEM((2, width, width), F32), VMEM((width, width), F32), pltpu.SemaphoreType.DMA((3,))
        ],
        compiler_params=PARAMS,
        cost_estimate=CHEAP,
        name="solve_high",
    )(turned, swapped, w_1, w_2, held_inverses, last_block)

    def spread(s, homes):
        have = {k: list(homes[k]) for k in homes}
        todo = {
            k: sorted(
                [
                    (r, g) for r in range(row_count) for g in range(groups)
                    if r % 2 == homes[k][0][0] % 2 and (r, g) not in homes[k]
                ],
                key=lambda spot: -(spot[0] != homes[k][0][0]) - (spot[1] != homes[k][0][1]),
            )
            for k in homes
        }
        fan = 1 if all(len(spots) > 1 for spots in homes.values()) else 3
        firsts = [(0, dev(r, k, g)) for k in homes for r, g in homes[k]]
        far = None
        while any(todo.values()):
            held = s if far is None else chosen(firsts, s, far)
            rounds = [[] for _ in range(fan)]
            for k in homes:
                spots = list(have[k])
                for pairs in rounds:
                    for a in spots:
                        if todo[k]:
                            b = todo[k].pop()
                            have[k].append(b)
                            pairs.append((dev(a[0], k, a[1]), dev(b[0], k, b[1])))
            for pairs in rounds:
                if pairs:
                    got = send(held, pairs)
                    far = got if far is None else chosen(pairs, got, far)
        twins = {
            k: [(dev(r, k, g), dev(r ^ 1, k, g)) for r, g in have[k]] for k in homes
        }
        near_twins = [pair for k in homes for pair in twins[k][: len(homes[k])]]
        far_twins = [pair for k in homes for pair in twins[k][len(homes[k]):]]
        return s, far, send(s, near_twins), send(far, far_twins)

    spots = [(g // groups, g % groups) for g in range(4)]
    homes = (tuple(spots[:2]), (spots[1],), (spots[2],), (spots[3],))
    moved = send(s_1, [(line(1, 0), line(1, 1))])
    s_low = jnp.where(member == 0, s_0, moved)
    ways = spread(s_low, {0: homes[0], 1: homes[1]}) + spread(s_high, {2: homes[2], 3: homes[3]})

    far_share, part, longer = [
        jax.ShapeDtypeStruct((n, nrhs), F32)
        for n in (share, blocks * quarter + share, blocks * quarter + share + 8)
    ]

    def update(name, shapes, slots):
        return pl.pallas_call(
            functools.partial(update_kernel, (groups, row_count, share, homes, slots, blocks)),
            in_specs=[vmem] * 8 + [hbm],
            out_specs=[vmem] * len(shapes),
            out_shape=shapes,
            scratch_shapes=[
                VMEM((nrhs, width), F32),
                VMEM((quarter, nrhs), F32),
                VMEM((blocks, width, 2 * quarter), F32),
                pltpu.SemaphoreType.DMA((2 * blocks,)),
            ],
            compiler_params=PARAMS,
            cost_estimate=CHEAP,
            name=name,
        )(*ways, held_factor)

    part_a, part_b, far = update(
        "update_first", [part, longer, far_share], first_slots + ((3, 0, 0, 0),)
    )
    own, part_c = update("update_second", [part, longer], second_slots)
    across = [(r, g) for r in range(row_count) for g in range(groups)]

    def route(*hops):
        return [(dev(r, a, g), dev(r, b, g)) for a, b in hops for r, g in across]

    got_1 = send(part_a, route((3, 2), (0, 1), (1, 0), (2, 3)))
    got_4 = send(part_b, route((2, 1), (1, 2)))
    got_2 = send(part_b, route((3, 1), (1, 0), (0, 2), (2, 3)))
    got_3 = send_some(part_c, route((3, 2), (0, 1)))
    joined = pl.pallas_call(
        functools.partial(join_kernel, (groups, share)),
        in_specs=[vmem] * 2,
        out_specs=vmem,
        out_shape=part,
        compiler_params=PARAMS,
        cost_estimate=CHEAP,
        name="join",
    )(part_c, got_1)
    joined = send_some(joined, route((2, 0), (1, 3)))
    far = send(far, route((3, 0), (0, 3), (1, 2), (2, 1)))

    solved, remaining = pl.pallas_call(
        functools.partial(last_kernel, groups),
        in_specs=[vmem] * 8,
        out_specs=[vmem] * 2,
        out_shape=[
            jax.ShapeDtypeStruct((steps, share, nrhs), F32),
            jax.ShapeDtypeStruct((blocks, quarter, nrhs), F32),
        ],
        compiler_params=PARAMS,
        cost_estimate=CHEAP,
        name="add_up",
    )(rhs[:, 0, 0], own, got_1, got_2, got_3, got_4, joined, far)
    return solved, remaining[:, None, None]


def solution(mesh):
    in_specs = (P(None, "row", "col", None, None), P(None, "row", "col", None, None), P())
    out_specs = (P(None, "col", None), P(None, "row", "col", None, None))
    return jax.shard_map(
        on_device, mesh=mesh, in_specs=in_specs, out_specs=out_specs, check_vma=False
    )
```
